32 devices in a mesh: dp: 8 (over z, x), tensor: 4 (over y, core).
Axes of the slice: x: 2, y: 2, z: 4, core: 2. Of those that a mesh axis runs over, the one named last changes fastest.
Arguments:
- hidden_in: bfloat16 [16, 512, 768], P('dp', 'tensor'), may hold values from -6 to 6
- lengths: int32 [16], P('dp'), may hold values from 32 to 512, as said below
- w_query: bfloat16 [768, 768], P(None, 'tensor'), may hold values from -0.21875 to 0.21875
- b_query: float32 [768], P('tensor'), may hold values from -3 to 3
- w_key: bfloat16 [768, 768], P(None, 'tensor'), may hold values from -0.21875 to 0.21875
- w_value: bfloat16 [768, 768], P(None, 'tensor'), may hold values from -0.21875 to 0.21875
- b_value: float32 [768], P('tensor'), may hold values from -3 to 3
- w_out: bfloat16 [768, 768], P('tensor'), may hold values from -0.875 to 0.875
- b_out: float32 [768], replicated, may hold values from -3 to 3
- norm1_gain: float32 [768], replicated, may hold values from 0.5 to 1.5
- norm1_shift: float32 [768], replicated, may hold values from -3 to 3
- w_up: bfloat16 [768, 3072], P(None, 'tensor'), may hold values from -0.21875 to 0.21875
- b_up: float32 [3072], P('tensor'), may hold values from -3 to 3
- w_down: bfloat16 [3072, 768], P('tensor'), may hold values from -0.21875 to 0.21875
- b_down: float32 [768], replicated, may hold values from -3 to 3
- norm2_gain: float32 [768], replicated, may hold values from 0.5 to 1.5
- norm2_shift: float32 [768], replicated, may hold values from -3 to 3
- out_grad: float32 [16, 512, 768], P('dp', 'tensor'), may hold values from -6 to 6
Outputs:
- out: float32 [16, 512, 768], P('dp', 'tensor')
- grad_input: float32 [16, 512, 768], P('dp', 'tensor')
- grad_w_query: float32 [768, 768], P(None, 'tensor')
- grad_b_query: float32 [768], P('tensor')
- grad_w_key: float32 [768, 768], P(None, 'tensor')
- grad_w_value: float32 [768, 768], P(None, 'tensor')
- grad_b_value: float32 [768], P('tensor')
- grad_w_out: float32 [768, 768], P('tensor')
- grad_b_out: float32 [768], replicated
- grad_norm1_gain: float32 [768], replicated
- grad_norm1_shift: float32 [768], replicated
- grad_w_up: float32 [768, 3072], P(None, 'tensor')
- grad_b_up: float32 [3072], P('tensor')
- grad_w_down: float32 [3072, 768], P('tensor')
- grad_b_down: float32 [768], replicated
- grad_norm2_gain: float32 [768], replicated
- grad_norm2_shift: float32 [768], replicated
The draws below stay inside these ranges and needn't reach their ends.
Inputs may be any that keep to these rules, and one draw needn't show every extreme that they name: `lengths`: in each aligned block of 2 rows, one row, which one drawn from the seed, has length 512; the others are skewed short.
All inputs are finite; a program needn't handle non-finite values.
Results may differ from the reference program's by a relative error of at most 0.035.
Values may be sent and summed in bfloat16 or wider, within the bound.
A program may use at most 128 MiB of HBM per device.

```python
import jax
import jax.numpy as jnp
from jax import lax

D = 768
HEADS = 12
HEAD = 64
FF = 3072
LEN = 512
SEQ_DEV = 2
SEQS = 16


def draw_lengths(key, part):
    key = jax.random.fold_in(key, 7)
    first_key, second_key, pick_key = jax.random.split(key, 3)
    shortest = max(LEN // 16, 1)
    first = jax.random.randint(first_key, (SEQS,), shortest, LEN + 1)
    second = jax.random.randint(second_key, (SEQS,), shortest, LEN + 1)
    skewed = jnp.minimum(first, second).reshape(SEQS // SEQ_DEV, SEQ_DEV)
    chosen = jax.random.randint(pick_key, (SEQS // SEQ_DEV, 1), 0, SEQ_DEV)
    places = jnp.arange(SEQ_DEV)[None, :]
    whole = jnp.where(places == chosen, LEN, skewed)
    return whole.reshape(SEQS).astype(jnp.int32)


def block_scale(stream_key, shape, pieces, low, top_value):
    def one(axis_at, blocks):
        heights = jax.random.uniform(jax.random.fold_in(jax.random.fold_in(stream_key, 6), axis_at), (blocks,), jnp.float32, low / len(pieces), top_value / len(pieces))
        return jnp.repeat(jnp.exp(heights), shape[axis_at] // blocks).reshape((-1,) + (1,) * (len(shape) - axis_at - 1))

    factor_of = one(*pieces[0])
    for cut in pieces[1:]:
        factor_of = factor_of * one(*cut)
    return factor_of


def bell_draw(rng, dims, deviation, bound, cuts=(), dtype=jnp.bfloat16):
    drawn = deviation * jax.random.normal(rng, dims, jnp.float32)
    if cuts:
        drawn = drawn * block_scale(rng, dims, cuts, -0.22, 0.18)
    return jnp.clip(drawn, -bound, bound).astype(dtype)


def setup_inputs(seed: int = 0) -> dict:
    seeds = jax.random.split(jax.random.key(seed), 19)
    return {
        "hidden_in": bell_draw(seeds[0], (SEQS, LEN, D), 1.0, 6.0, ((0, 8), (1, 4))),
        "lengths": draw_lengths(jax.random.fold_in(seeds[18], 71), 0),
        "w_query": bell_draw(seeds[2], (D, D), D ** -0.5, 0.21875, ((1, 4),)),
        "b_query": bell_draw(seeds[3], (D,), 0.5, 3.0, ((0, 4),), jnp.float32),
        "w_key": bell_draw(seeds[4], (D, D), D ** -0.5, 0.21875, ((1, 4),)),
        "w_value": bell_draw(seeds[5], (D, D), D ** -0.5, 0.21875, ((1, 4),)),
        "b_value": bell_draw(seeds[6], (D,), 0.5, 3.0, ((0, 4),), jnp.float32),
        "w_out": bell_draw(seeds[7], (D, D), (D // 16) ** -0.5, 0.875, ((0, 4),)),
        "b_out": bell_draw(seeds[8], (D,), 0.5, 3.0, (), jnp.float32),
        "norm1_gain": jnp.clip(1.0 + 0.1 * jax.random.normal(seeds[9], (D,), jnp.float32), 0.5, 1.5),
        "norm1_shift": bell_draw(seeds[10], (D,), 0.5, 3.0, (), jnp.float32),
        "w_up": bell_draw(seeds[11], (D, FF), D ** -0.5, 0.21875, ((1, 4),)),
        "b_up": bell_draw(seeds[12], (FF,), 0.5, 3.0, ((0, 4),), jnp.float32),
        "w_down": bell_draw(seeds[13], (FF, D), (FF // 4) ** -0.5, 0.21875, ((0, 4),)),
        "b_down": bell_draw(seeds[14], (D,), 0.5, 3.0, (), jnp.float32),
        "norm2_gain": jnp.clip(1.0 + 0.1 * jax.random.normal(seeds[15], (D,), jnp.float32), 0.5, 1.5),
        "norm2_shift": bell_draw(seeds[16], (D,), 0.5, 3.0, (), jnp.float32),
        "out_grad": bell_draw(seeds[17], (SEQS, LEN, D), 1.0, 6.0, ((0, 8), (1, 4)), jnp.float32),
    }


@jax.custom_vjp
def low(v):
    return lax.optimization_barrier(v.astype(jnp.bfloat16)).astype(jnp.float32)

@jax.custom_vjp
def low_back(v):
    return v

def low_keep(v):
    return (low(v), None)

def low_pass(kept, grad):
    return (grad,)

def back_keep(v):
    return (v, None)

def back_low(kept, grad):
    return (low(grad),)
low.defvjp(low_keep, low_pass)
low_back.defvjp(back_keep, back_low)
norm_eps = 1e-12

def matmul(left, right):
    return jnp.einsum('...d,de->...e', left, right, precision=lax.Precision.HIGHEST)

def normalize(resid, gain, shift):
    centre = resid - lax.optimization_barrier(jnp.mean(resid, axis=-1, keepdims=True))
    spread = lax.optimization_barrier(jnp.mean(centre * centre, axis=-1, keepdims=True))
    return centre * lax.rsqrt(spread + norm_eps) * gain + shift

def attend_one(packed):
    query, key_rows, value_rows, length = packed
    query = query.reshape(LEN, HEADS, HEAD)
    key_rows = key_rows.reshape(LEN, HEADS, HEAD)
    value_rows = value_rows.reshape(LEN, HEADS, HEAD)
    scores = jnp.einsum('qhd,khd->hqk', query, key_rows, precision=lax.Precision.HIGHEST) * HEAD ** (-0.5)
    scores = low_back(scores)
    counted = jnp.arange(LEN) < length
    scores = jnp.where(counted[None, None, :], scores, -1000000000.0)
    probs = low(jax.nn.softmax(scores, axis=-1))
    attention_context = jnp.einsum('hqk,khd->qhd', probs, value_rows, precision=lax.Precision.HIGHEST)
    return attention_context.reshape(LEN, D)

def layer(hidden, lengths, params):
    w_query, b_query, w_key, w_value, b_value, w_out, b_out, gain_one, shift_one, w_up, b_up, w_down, b_down, gain_two, shift_two = params
    rounded = low(hidden)
    query = low(low_back(matmul(rounded, w_query) + b_query))
    key_rows = low(low_back(matmul(rounded, w_key)))
    value_rows = low(low_back(matmul(rounded, w_value) + b_value))
    attention_context = lax.map(jax.checkpoint(attend_one), (query, key_rows, value_rows, lengths))
    attention_context = low(low_back(attention_context))
    attn = low_back(matmul(attention_context, w_out))
    first = normalize(attn + b_out + hidden, gain_one, shift_one)
    first_low = low(first)
    pre = low_back(matmul(first_low, w_up) + b_up)
    gelu_activation = low(jax.nn.gelu(pre, approximate=True))
    ffn = low_back(matmul(gelu_activation, w_down))
    return normalize(ffn + b_down + first, gain_two, shift_two)

def reference(hidden_in, lengths, w_query, b_query, w_key, w_value, b_value, w_out, b_out, norm1_gain, norm1_shift, w_up, b_up, w_down, b_down, norm2_gain, norm2_shift, out_grad):

    def widen(value):
        return value.astype(jnp.float32)

    def forward(start, *params):
        middle = layer(start, lengths, params)
        return layer(middle, lengths, params)
    out, pull = jax.vjp(forward, widen(hidden_in), widen(w_query), widen(b_query), widen(w_key), widen(w_value), widen(b_value), widen(w_out), widen(b_out), widen(norm1_gain), widen(norm1_shift), widen(w_up), widen(b_up), widen(w_down), widen(b_down), widen(norm2_gain), widen(norm2_shift))
    grads = pull(widen(out_grad))
    return (out, grads[0], grads[1], grads[2], grads[3], grads[4], grads[5], grads[6], grads[7], grads[8], grads[9], grads[10], grads[11], grads[12], grads[13], grads[14], grads[15])
```

```python
import functools

import jax
import jax.numpy as jnp
from jax import lax
from jax.experimental import pallas as pl
from jax.experimental.pallas import tpu as pltpu
from jax.sharding import PartitionSpec as P

HEAD = 64
NORM_EPS = 1e-12
NEG = -1000000000.0
GELU_C = 0.7978845608
GELU_A = 0.044715

NN = (((1,), (0,)), ((), ()))
NT = (((1,), (1,)), ((), ()))
TN = (((0,), (0,)), ((), ()))

b16 = jnp.bfloat16
f32 = jnp.float32


def dot(left, right, dims):
    return lax.dot_general(left, right, dims, preferred_element_type=f32)


def rms_back(dout, scaled, rstd, gain):
    dscaled = dout * gain
    return rstd * (
        dscaled
        - jnp.mean(dscaled, axis=-1, keepdims=True)
        - scaled * jnp.mean(dscaled * scaled, axis=-1, keepdims=True)
    )


def col_sum(value):
    return jnp.sum(value, axis=0, keepdims=True)


def whole_step(
    cfg,
    len_ref,
    hid,
    og,
    wq,
    wk,
    wv,
    wo,
    wu,
    wd,
    vec,
    out,
    gib_out,
    g_out,
    sm_out,
    w,
    hb,
    qkv,
    ex,
    inv,
    ctx,
    zs,
    rs,
    yb,
    act,
    gp,
    X,
    Y,
    dffn,
    dpre,
    dattn,
    dqkv,
    dct,
    xs,
    xr,
    vecr,
    bcol,
    acc,
    sm,
    smr,
    G,
    gs,
    yr,
    xh,
    zr,
    hr,
    F,
    lsem,
    fs,
    fr,
    wys,
    wyr,
    wxs,
    wxr,
    es,
    er,
    ys,
    yrs,
    gxs,
    gxr,
    zss,
    zrs,
    hss,
    hrs,
    azs,
    azr,
    axs,
    axr,
    os,
    sms,
    smrs,
):
    T, D, A, B, C, R, NP, NH = (
        cfg["T"],
        cfg["D"],
        cfg["A"],
        cfg["B"],
        cfg["C"],
        cfg["R"],
        cfg["NP"],
        cfg["NH"],
    )
    NCH = T // C
    TOT = 4 * A + 2 * D
    NS = TOT // R
    HR = R // 2
    Q = HR // NP
    NHH = A // HEAD
    HEADS = 2 * NHH
    WCH = A // 2
    MESH = pl.DeviceIdType.MESH
    UP, DN = 4 * A, 4 * A + D

    d = lax.axis_index("dp")
    t = lax.axis_index("tensor")
    y = t // 2
    c = t % 2
    x = d % 2
    z = d // 2
    zlo = z % NP
    zhi = z // NP
    t2 = (t + 2) % 4
    sib = (d, t + 1 - 2 * c)
    par = (d, t2)
    xp = (d + 1 - 2 * x, t)

    def zdev(k):
        return ((zhi * NP + (zlo + k) % NP) * 2 + x, t)

    def hdev(k):
        return ((((zhi + k) % NH) * NP + zlo) * 2 + x, t)

    def remote(src, dst, send, recv, dev):
        return pltpu.make_async_remote_copy(
            src_ref=src,
            dst_ref=dst,
            send_sem=send,
            recv_sem=recv,
            device_id=dev,
            device_id_type=MESH,
        )

    local = [
        pltpu.make_async_copy(hid.at[y], hb.at[0, pl.ds(t * B, B)], lsem.at[0]),
        pltpu.make_async_copy(wo, w.at[0, pl.ds(3 * A, A)], lsem.at[1]),
        pltpu.make_async_copy(wu, w.at[0, pl.ds(UP, D)], lsem.at[2]),
        pltpu.make_async_copy(wd, w.at[0, pl.ds(DN, D)], lsem.at[3]),
        pltpu.make_async_copy(og.at[0], Y.at[pl.ds(0, B)], lsem.at[4]),
        pltpu.make_async_copy(og.at[1], Y.at[pl.ds(B, B)], lsem.at[5]),
    ]
    for copy in local:
        copy.start()

    barrier = pltpu.get_barrier_semaphore()
    friends = [sib, par, xp] + [zdev(k) for k in range(1, NP)] + [hdev(k) for k in range(1, NH)]
    for dev in friends:
        pl.semaphore_signal(barrier, inc=1, device_id=dev, device_id_type=MESH)
    pl.semaphore_wait(barrier, len(friends))

    hid_sib = remote(hid.at[y], hb.at[0, pl.ds(t * B, B)], fs.at[0], fr.at[0], sib)
    hid_par = remote(hid.at[1 - y], hb.at[0, pl.ds(t * B, B)], fs.at[1], fr.at[1], par)
    vec_par = remote(vec, vecr, fs.at[2], fr.at[2], par)
    hid_par.start()
    vec_par.start()
    hid_sib.start()

    w[0, 0:A] = wq[...].T
    w[0, A : 2 * A] = wk[...].T
    w[0, 2 * A : 3 * A] = wv[...].T
    acc[...] = jnp.zeros_like(acc)

    WST = TOT // (2 * WCH)

    def wrows(i, which):
        return pl.ds(pl.multiple_of(i * (2 * WCH) + which * WCH, WCH), WCH)

    def wy(i):
        rows = wrows(i, x)
        return remote(w.at[0, rows], w.at[1, rows], wys.at[i], wyr.at[i], par)

    def wx(i, which):
        rows = wrows(i, which)
        return remote(w.at[1, rows], w.at[1, rows], wxs.at[i], wxr.at[i], xp)

    LOOK = 2

    def pump(i):
        wy(i).wait_recv()
        wx(i, x).start()
        if i + LOOK < WST:
            wy(i + LOOK).start()

    def have(lo, hi):
        for i in range(lo, hi):
            wx(i, 1 - x).wait_recv()

    wy(0).start()
    wy(1).start()
    for copy in local:
        copy.wait()
    G[0 : 2 * B] = Y[0 : 2 * B].astype(b16)

    hid_par.wait_recv()
    rows_t2 = pl.ds(t2 * B, B)
    hid_fwd = remote(hb.at[0, rows_t2], hb.at[0, rows_t2], fs.at[3], fr.at[3], sib)
    hid_fwd.start()
    vec_par.wait_recv()
    for half, source in enumerate((vec, vecr)):
        row = source[1:2, 0 : 2 * A]
        bcol[half] = jnp.transpose(jnp.broadcast_to(row, (128, 2 * A)))
    hid_sib.wait_recv()
    hid_fwd.wait_recv()

    b_out, gain1, shift1 = vec[2:3], vec[3:4], vec[4:5]
    b_down, gain2, shift2 = vec[5:6], vec[6:7], vec[7:8]
    length = len_ref[y]

    def chunk(m):
        return pl.ds(m * C, C)

    def xcopy(k, m):
        return remote(xs.at[k % 2, chunk(m)], xr.at[k % 2, chunk(m)], es.at[k % 2, m], er.at[k % 2, m], sib)

    def xsend(k, m, value):
        xs[k % 2, chunk(m)] = value.astype(b16)
        xcopy(k, m).start()

    def xget(k, m):
        xcopy(k, m).wait()
        return xs[k % 2, chunk(m)].astype(f32) + xr[k % 2, chunk(m)].astype(f32)

    def project(l, m):
        tok = pl.ds(m * C, C)
        for half in range(2):
            got = dot(w[half, 0 : 3 * A], hb[l, tok], NT)
            base = half * 3 * A
            bq = jnp.concatenate([bcol[half, 0:A]] * (C // 128), axis=1)
            bv = jnp.concatenate([bcol[half, A : 2 * A]] * (C // 128), axis=1)
            qkv[l, base : base + A, tok] = ((got[0:A] + bq).astype(b16) * b16(HEAD**-0.5)).astype(b16)
            qkv[l, base + A : base + 2 * A, tok] = got[A : 2 * A].astype(b16)
            qkv[l, base + 2 * A : base + 3 * A, tok] = (got[2 * A : 3 * A] + bv).astype(b16)

    def head_rows(h, part):
        base = (h // NHH) * (3 * A) + part * A + (h % NHH) * HEAD
        return pl.ds(pl.multiple_of(base, HEAD), HEAD)

    def attend(l, h):
        counted = lax.broadcasted_iota(jnp.int32, (T, T), 0) < length
        scores = dot(qkv[l, head_rows(h, 1)], qkv[l, head_rows(h, 0)], TN)
        scores = jnp.where(counted, scores, NEG)
        top = jnp.max(scores, axis=0, keepdims=True)
        e = jnp.exp(scores - top)
        one = 1.0 / jnp.sum(e, axis=0, keepdims=True)
        eb = e.astype(b16)
        ex[l, h] = eb
        inv[l, h] = one
        got = dot(qkv[l, head_rows(h, 2)], eb, NN) * one
        ctx[l, pl.ds(pl.multiple_of(h * HEAD, HEAD), HEAD)] = got.astype(b16)

    def attend_range(l, lo, hi):
        def step(h, carry):
            attend(l, h)
            return carry

        lax.fori_loop(lo, hi, step, 0)

    def attn_out(l, k):
        for m in range(NCH):
            tok = pl.ds(m * C, C)
            part = dot(ctx[l, 0:A, tok], w[0, 3 * A : 4 * A], TN)
            part += dot(ctx[l, A : 2 * A, tok], w[1, 3 * A : 4 * A], TN)
            xsend(k, m, part)

    def zrows(z_at, m):
        return pl.ds(z_at * T + m * C, C)

    def norm(resid, gain, shift, z_at, m):
        rows = chunk(m)
        centre = resid - jnp.mean(resid, axis=-1, keepdims=True)
        rstd = lax.rsqrt(jnp.mean(centre * centre, axis=-1, keepdims=True) + NORM_EPS)
        scaled = centre * rstd
        zs[zrows(z_at, m)] = scaled.astype(b16)
        rs[rows, z_at : z_at + 1] = rstd
        return scaled * gain + shift

    def norm_one(l, k, m):
        rows = chunk(m)
        before = hb[0, rows].astype(f32) if l == 0 else X[rows]
        first = norm(xget(k, m) + b_out + before, gain1, shift1, 2 * l, m)
        Y[rows] = first
        yb[l, rows] = first.astype(b16)

    def up_chunk(l, m):
        rows = chunk(m)
        for half, source in enumerate((vec, vecr)):
            cols = pl.ds(half * D, D)
            pre = dot(yb[l, rows], w[half, UP : UP + D], NN) + source[0:1]
            square = pre * pre
            th = jnp.tanh(GELU_C * pre * (1.0 + GELU_A * square))
            more = 0.5 * (1.0 + th)
            act[l, rows, cols] = (pre * more).astype(b16)
            slope = more + (0.5 * GELU_C) * pre * (1.0 - th * th) * (1.0 + (3 * GELU_A) * square)
            gp[l, rows, cols] = slope.astype(b16)

    def down_chunk(l, k, m):
        rows = chunk(m)
        part = dot(act[l, rows, 0:D], w[0, DN : DN + D], NN)
        part += dot(act[l, rows, D : 2 * D], w[1, DN : DN + D], NN)
        xsend(k, m, part)

    def norm_two(l, k, m):
        rows = chunk(m)
        result = norm(xget(k, m) + b_down + Y[rows], gain2, shift2, 2 * l + 1, m)
        X[rows] = result
        if l == 0:
            hb[1, rows] = result.astype(b16)

    for i in range(3):
        pump(i)
    have(0, 3)
    for m in range(NCH):
        project(0, m)
    cuts = [HEADS * i // 3 for i in range(4)]
    for i in range(3):
        attend_range(0, cuts[i], cuts[i + 1])
        pump(3 + i)
    have(3, 4)
    attn_out(0, 0)
    pump(6)
    for m in range(NCH):
        norm_one(0, 0, m)
    pump(7)
    have(4, 8)
    for m in range(NCH):
        up_chunk(0, m)
        pump(8 + m)
    for i in range(8 + NCH, WST):
        pump(i)
    og_rows = pl.ds(t * B, B)
    og_mine, og_other = G.at[pl.ds(y * B, B)], G.at[pl.ds((1 - y) * B, B)]
    og_keep = pltpu.make_async_copy(og_mine, dattn.at[0, og_rows], lsem.at[0])
    og_sib = remote(og_mine, dattn.at[0, og_rows], fs.at[4], fr.at[4], sib)
    og_par = remote(og_other, dattn.at[0, og_rows], fs.at[5], fr.at[5], par)
    og_keep.start()
    og_par.start()
    og_sib.start()
    have(8, WST)
    for m in range(NCH):
        down_chunk(0, 1, m)
    for m in range(NCH):
        norm_two(0, 1, m)
        project(1, m)

    attend_range(1, 0, HEADS)
    og_par.wait_recv()
    og_fwd = remote(dattn.at[0, rows_t2], dattn.at[0, rows_t2], fs.at[6], fr.at[6], sib)
    og_fwd.start()
    attn_out(1, 2)
    for m in range(NCH):
        norm_one(1, 2, m)
        up_chunk(1, m)
        down_chunk(1, 3, m)
    for m in range(NCH):
        norm_two(1, 3, m)
    out_keep = pltpu.make_async_copy(X.at[pl.ds(t * B, B)], out.at[y], lsem.at[1])
    out_par = remote(X.at[pl.ds(t2 * B, B)], out.at[y], fs.at[7], fr.at[7], par)
    out_keep.start()
    out_par.start()
    og_keep.wait()
    og_sib.wait_recv()
    og_fwd.wait_recv()

    def ffn_back(l, k, m):
        rows = chunk(m)
        dout = dattn[0, rows].astype(f32) if l == 1 else X[rows]
        scaled = zs[zrows(2 * l + 1, m)].astype(f32)
        dr = rms_back(dout, scaled, rs[rows, 2 * l + 1 : 2 * l + 2], gain2)
        acc[3:4] += col_sum(dr)
        acc[4:5] += col_sum(dout * scaled)
        acc[5:6] += col_sum(dout)
        Y[rows] = dr
        drb = dr.astype(b16)
        dffn[l, rows] = drb
        part = None
        for half in range(2):
            cols = pl.ds(half * D, D)
            dact = dot(drb, w[half, DN : DN + D], NT)
            dp = (dact * gp[l, rows, cols].astype(f32)).astype(b16)
            dpre[l, rows, cols] = dp
            row = 6 + 8 * half
            acc[row : row + 1] += col_sum(dp.astype(f32))
            got = dot(dp, w[half, UP : UP + D], NT)
            part = got if part is None else part + got
        xsend(k, m, part)

    def attn_out_back(l, k, m):
        rows = chunk(m)
        dfirst = Y[rows] + xget(k, m)
        scaled = zs[zrows(2 * l, m)].astype(f32)
        dr = rms_back(dfirst, scaled, rs[rows, 2 * l : 2 * l + 1], gain1)
        acc[0:1] += col_sum(dr)
        acc[1:2] += col_sum(dfirst * scaled)
        acc[2:3] += col_sum(dfirst)
        Y[rows] = dr
        drb = dr.astype(b16)
        dattn[l, rows] = drb
        for half in range(2):
            got = dot(w[half, 3 * A : 4 * A], drb, NT)
            for j in range(NHH):
                h = half * NHH + j
                scaled_rows = got[j * HEAD : (j + 1) * HEAD] * inv[l, h, :, m * C : (m + 1) * C]
                dct[h * HEAD : (h + 1) * HEAD, m * C : (m + 1) * C] = scaled_rows.astype(b16)

    def attend_back(l, h):
        mine = pl.ds(pl.multiple_of(h * HEAD, HEAD), HEAD)
        dc = dct[mine]
        dprobs = dot(qkv[l, head_rows(h, 2)], dc, TN)
        eb = ex[l, h]
        ef = eb.astype(f32)
        inner = col_sum(ef * dprobs) * inv[l, h]
        ds = (ef * (dprobs - inner)).astype(b16)
        dqkv[l, head_rows(h, 2)] = dot(dc, eb, NT).astype(b16)
        dqkv[l, head_rows(h, 0)] = (dot(qkv[l, head_rows(h, 1)], ds, NN) * (HEAD**-0.5)).astype(b16)
        dqkv[l, head_rows(h, 1)] = dot(qkv[l, head_rows(h, 0)], ds, NT).astype(b16)

    def attend_back_all(l):
        def step(h, carry):
            attend_back(l, h)
            return carry

        lax.fori_loop(0, HEADS, step, 0)

    def project_back(l, k):
        for m in range(NCH):
            tok = pl.ds(m * C, C)
            part = dot(dqkv[l, 0 : 3 * A, tok], w[0, 0 : 3 * A], TN)
            part += dot(dqkv[l, 3 * A : 6 * A, tok], w[1, 0 : 3 * A], TN)
            xsend(k, m, part)
        ones = jnp.ones((8, T), b16)
        for half in range(2):
            sums = dot(ones, dqkv[l, half * 3 * A : (half + 1) * 3 * A], NT)
            row = 7 + 8 * half
            acc[row : row + 1, 0 : 3 * A] += sums[0:1]

    for m in range(NCH):
        ffn_back(1, 4, m)
    for m in range(NCH):
        attn_out_back(1, 4, m)
    attend_back_all(1)
    for copy in (og_sib, og_par, og_fwd):
        copy.wait_send()
    out_keep.wait()
    out_par.wait_send()
    project_back(1, 5)
    for m in range(NCH):
        rows = chunk(m)
        X[rows] = Y[rows] + xget(5, m)
        ffn_back(0, 6, m)

    def both(ref, cols=slice(None)):
        value = ref[:, :, cols]
        return value.reshape(2 * value.shape[1], value.shape[2])

    FREE = T - 4 * A

    def grad_down(half, dst, off=0):
        dy = both(dffn)
        for i in reversed(range(D // 256)):
            left = both(act, slice(half * D + i * 256, half * D + (i + 1) * 256))
            dst[off + DN + i * 256 : off + DN + (i + 1) * 256] = dot(left, dy, TN).astype(b16)

    def grad_up(half, dst, off=0):
        dy = both(dpre, slice(half * D, (half + 1) * D))
        for i in reversed(range(D // 256)):
            left = both(yb, slice(i * 256, (i + 1) * 256))
            dst[off + UP + i * 256 : off + UP + (i + 1) * 256] = dot(left, dy, TN).astype(b16)

    def grad_attn(half, dst):
        rows = slice(half * A, (half + 1) * A)
        got = dot(ctx[0, rows], dattn[0], NN) + dot(ctx[1, rows], dattn[1], NN)
        dst[3 * A : 4 * A] = got.astype(b16)
        rows = slice(half * 3 * A, (half + 1) * 3 * A)
        got = dot(dqkv[0, rows], hb[0], NN) + dot(dqkv[1, rows], hb[1], NN)
        dst[0 : 3 * A] = got.astype(b16)

    def top_of(s):
        return pl.multiple_of(TOT - (s + 1) * R, R)

    def piece(s):
        return pl.ds(top_of(s), R)

    def half_of(s, which):
        return pl.ds(pl.multiple_of(top_of(s) + which * HR, HR), HR)

    def part_of(s, which, p):
        return pl.ds(pl.multiple_of(top_of(s) + which * HR + p * Q, Q), Q)

    def loop(lo, hi, f):
        def step(i, carry):
            f(i)
            return carry

        lax.fori_loop(lo, hi, step, 0)

    def ycopy_ffn(s):
        src = zs.at[pl.ds(pl.multiple_of(top_of(s) + FREE, R), R)]
        return remote(src, yr.at[piece(s)], ys.at[s], yrs.at[s], par)

    def ycopy_attn(s):
        return remote(gs.at[piece(s)], yr.at[piece(s)], ys.at[s], yrs.at[s], par)

    def ycopy(s):
        return remote(yr.at[piece(s)], yr.at[piece(s)], ys.at[s], yrs.at[s], par)

    def gxcopy(s):
        return remote(G.at[half_of(s, 1 - x)], xh.at[s], gxs.at[s], gxr.at[s], xp)

    def zcopy(s, k):
        src = G.at[part_of(s, x, (zlo + k) % NP)]
        return remote(src, zr.at[s, k - 1], zss.at[s, k - 1], zrs.at[s, k - 1], zdev(k))

    def hcopy(s, k):
        src = G.at[part_of(s, x, zlo)]
        return remote(src, hr.at[s % 2, k - 1], hss.at[s, k - 1], hrs.at[s, k - 1], hdev(k))

    def azcopy(s, k):
        rows = part_of(s, x, zlo)
        return remote(F.at[rows], F.at[rows], azs.at[s, k - 1], azr.at[s, k - 1], zdev(k))

    def axcopy(s, k):
        rows = part_of(s, x, (zlo + NP - k) % NP)
        return remote(F.at[rows], F.at[rows], axs.at[s, k], axr.at[s, k], xp)

    def ocopy(s):
        return pltpu.make_async_copy(F.at[piece(s)], g_out.at[piece(s)], os.at[s])

    def stage_x(s):
        ycopy(s).wait_recv()
        for which in (1 - x, x):
            rows = half_of(s, which)
            G[rows] = (G[rows].astype(f32) + yr[rows].astype(f32)).astype(b16)
            if which is not x:
                gxcopy(s).start()

    def stage_z(s):
        gxcopy(s).wait_recv()
        rows = half_of(s, x)
        G[rows] = (G[rows].astype(f32) + xh[s].astype(f32)).astype(b16)
        for k in range(1, NP):
            zcopy(s, k).start()

    def stage_sum(s):
        rows = part_of(s, x, zlo)
        total = G[rows].astype(f32)
        for k in range(1, NP):
            zcopy(s, k).wait_recv()
            total += zr[s, k - 1].astype(f32)
        if NH > 1:
            G[rows] = total.astype(b16)
            for k in range(1, NH):
                hcopy(s, k).start()
            for k in range(1, NH):
                hcopy(s, k).wait()
                total += hr[s % 2, k - 1].astype(f32)
        F[rows] = total.astype(b16)
        for k in range(1, NP):
            azcopy(s, k).start()
        axcopy(s, 0).start()

    def stage_swap(s):
        for k in range(1, NP):
            azcopy(s, k).wait_recv()
            axcopy(s, k).start()

    def stage_out(s):
        for k in range(NP):
            axcopy(s, k).wait_recv()
        ocopy(s).start()

    grad_down(1, zs, FREE)
    loop(0, D // R, lambda s: ycopy_ffn(s).start())
    grad_up(1, zs, FREE)
    loop(D // R, 2 * D // R, lambda s: ycopy_ffn(s).start())
    grad_down(0, G)
    grad_up(0, G)
    for m in range(NCH):
        attn_out_back(0, 6, m)
    attend_back_all(0)
    project_back(0, 7)
    grad_attn(1, gs)
    loop(2 * D // R, NS, lambda s: ycopy_attn(s).start())
    acc[8:14] = acc[0:6]
    sm_y = remote(acc.at[pl.ds(8, 8)], smr.at[0], sms.at[0], smrs.at[0], par)
    sm_y.start()
    for m in range(NCH):
        rows = chunk(m)
        X[rows] = Y[rows] + xget(7, m)
    xs[0, 0:B] = X[pl.ds(t * B, B)].astype(b16)
    xs[0, B : 2 * B] = X[pl.ds(t2 * B, B)].astype(b16)
    gi_keep = pltpu.make_async_copy(xs.at[0, pl.ds(0, B)], gib_out.at[y], lsem.at[2])
    gi_par = remote(xs.at[0, pl.ds(B, B)], gib_out.at[y], fs.at[8], fr.at[8], par)
    gi_keep.start()
    gi_par.start()
    grad_attn(0, G)

    stages = (stage_x, stage_z, stage_sum, stage_swap, stage_out)

    def run(i):
        for lag, stage in enumerate(stages):
            s = i - lag
            if isinstance(s, int) and not 0 <= s < NS:
                continue
            stage(s)

    for i in range(4):
        run(i)
    loop(4, NS, run)
    for i in range(NS, NS + 2):
        run(i)
    sm_y.wait_recv()
    sm[0] = acc[0:8] + smr[0]
    sm_x = remote(sm.at[0], smr.at[1], sms.at[1], smrs.at[1], xp)
    sm_x.start()
    run(NS + 2)
    sm_x.wait_recv()
    sm[1] = sm[0] + smr[1]
    sm_z = [
        remote(sm.at[1], smr.at[1 + k], sms.at[1 + k], smrs.at[1 + k], zdev(k)) for k in range(1, NP)
    ]
    for copy in sm_z:
        copy.start()
    run(NS + 3)
    total = sm[1]
    for k, copy in enumerate(sm_z):
        copy.wait_recv()
        total += smr[2 + k]
    sm[2] = total
    if NH > 1:
        sm_h = [
            remote(sm.at[2], smr.at[NP + k], sms.at[NP + k], smrs.at[NP + k], hdev(k))
            for k in range(1, NH)
        ]
        for copy in sm_h:
            copy.start()
        for k, copy in enumerate(sm_h):
            copy.wait()
            total += smr[NP + 1 + k]
    sm_out[...] = total

    for copy in (hid_sib, hid_par, vec_par, hid_fwd, gi_par, sm_y, sm_x):
        copy.wait_send()
    for copy in sm_z:
        copy.wait_send()
    out_par.wait_recv()
    gi_par.wait_recv()
    gi_keep.wait()
    for i in range(WST):
        wy(i).wait_send()
        wx(i, x).wait_send()

    def drain(s):
        ycopy(s).wait_send()
        gxcopy(s).wait_send()
        for k in range(1, NP):
            zcopy(s, k).wait_send()
            azcopy(s, k).wait_send()
        for k in range(NP):
            axcopy(s, k).wait_send()
        ocopy(s).wait()

    loop(0, NS, drain)


def shards(
    dp,
    hidden_in,
    lengths,
    w_query,
    b_query,
    w_key,
    w_value,
    b_value,
    w_out,
    b_out,
    norm1_gain,
    norm1_shift,
    w_up,
    b_up,
    w_down,
    b_down,
    norm2_gain,
    norm2_shift,
    out_grad,
):
    _, B, D = hidden_in.shape
    A = w_query.shape[1]
    T = 4 * B
    TOT = 4 * A + 2 * D
    R = 128
    HR = R // 2
    nz = dp // 2
    NP = 1
    while nz % (2 * NP) == 0 and HR % (32 * NP) == 0:
        NP *= 2
    NH = nz // NP
    C = T // 2
    NCH = T // C
    NS = TOT // R
    Q = HR // NP
    heads = 2 * A // HEAD
    cfg = dict(T=T, D=D, A=A, B=B, C=C, R=R, NP=NP, NH=NH)
    qv = jnp.concatenate([b_query, b_value, jnp.zeros((D - 2 * A,), f32)])
    vec = jnp.stack([b_up, qv, b_out, norm1_gain, norm1_shift, b_down, norm2_gain, norm2_shift])
    V = functools.partial(pltpu.VMEM)
    DMA = pltpu.SemaphoreType.DMA
    NPx = max(NP - 1, 1)
    NHx = max(NH - 1, 1)
    scratch = [
        V((2, TOT, D), b16),
        V((2, T, D), b16),
        V((2, 6 * A, T), b16),
        V((2, heads, T, T), b16),
        V((2, heads, 1, T), f32),
        V((2, 2 * A, T), b16),
        V((max(4 * T, T + 2 * D), D), b16),
        V((T, 128), f32),
        V((2, T, D), b16),
        V((2, T, 2 * D), b16),
        V((2, T, 2 * D), b16),
        V((T, D), f32),
        V((T, D), f32),
        V((2, T, D), b16),
        V((2, T, 2 * D), b16),
        V((2, T, D), b16),
        V((2, 6 * A, T), b16),
        V((2 * A, T), b16),
        V((2, T, D), b16),
        V((2, T, D), b16),
        V((8, D), f32),
        V((2, 2 * A, 128), f32),
        V((16, D), f32),
        V((3, 8, D), f32),
        V((NP + NH, 8, D), f32),
        V((TOT, D), b16),
        V((4 * A, D), b16),
        V((TOT, D), b16),
        V((NS, HR, D), b16),
        V((NS, NPx, Q, D), b16),
        V((2, NHx, Q, D), b16),
        V((TOT, D), b16),
        DMA((6,)),
        DMA((9,)),
        DMA((9,)),
        DMA((12,)),
        DMA((12,)),
        DMA((12,)),
        DMA((12,)),
        DMA((2, NCH)),
        DMA((2, NCH)),
        DMA((NS,)),
        DMA((NS,)),
        DMA((NS,)),
        DMA((NS,)),
        DMA((NS, NPx)),
        DMA((NS, NPx)),
        DMA((NS, NHx)),
        DMA((NS, NHx)),
        DMA((NS, NPx)),
        DMA((NS, NPx)),
        DMA((NS, NP)),
        DMA((NS, NP)),
        DMA((NS,)),
        DMA((NP + NH,)),
        DMA((NP + NH,)),
    ]
    anywhere = pl.BlockSpec(memory_space=pl.ANY)
    vmem = pl.BlockSpec(memory_space=pltpu.VMEM)
    smem = pl.BlockSpec(memory_space=pltpu.SMEM)
    result, gib, grads, small = pl.pallas_call(
        functools.partial(whole_step, cfg),
        out_shape=(
            jax.ShapeDtypeStruct((2, B, D), f32),
            jax.ShapeDtypeStruct((2, B, D), b16),
            jax.ShapeDtypeStruct((TOT, D), b16),
            jax.ShapeDtypeStruct((8, D), f32),
        ),
        in_specs=[smem, anywhere, anywhere, vmem, vmem, vmem, anywhere, anywhere, anywhere, vmem],
        out_specs=(anywhere, anywhere, anywhere, vmem),
        scratch_shapes=scratch,
        compiler_params=pltpu.CompilerParams(
            collective_id=0, has_side_effects=True, vmem_limit_bytes=cfg_vmem()
        ),
    )(lengths, hidden_in, out_grad, w_query, w_key, w_value, w_out, w_up, w_down, vec)
    wide = grads.astype(f32)
    return (
        result,
        gib.astype(f32),
        wide[0:A].T,
        small[7, 0:A],
        wide[A : 2 * A].T,
        wide[2 * A : 3 * A].T,
        small[7, 2 * A : 3 * A],
        wide[3 * A : 4 * A],
        small[0],
        small[1],
        small[2],
        wide[4 * A : 4 * A + D],
        small[6],
        wide[4 * A + D :],
        small[3],
        small[4],
        small[5],
    )


def cfg_vmem():
    return 64 * 2**20


def solution(mesh):
    placed = (
        P("dp", "tensor", None),
        P("dp"),
        P(None, "tensor"),
        P("tensor"),
        P(None, "tensor"),
        P(None, "tensor"),
        P("tensor"),
        P("tensor", None),
        P(),
        P(),
        P(),
        P(None, "tensor"),
        P("tensor"),
        P("tensor", None),
        P(),
        P(),
        P(),
        P("dp", "tensor", None),
    )
    return jax.shard_map(
        functools.partial(shards, mesh.shape["dp"]),
        mesh=mesh,
        in_specs=placed,
        out_specs=(
            P("dp", "tensor", None),
            P("dp", "tensor", None),
            P(None, "tensor"),
            P("tensor"),
            P(None, "tensor"),
            P(None, "tensor"),
            P("tensor"),
            P("tensor", None),
            P(),
            P(),
            P(),
            P(None, "tensor"),
            P("tensor"),
            P("tensor", None),
            P(),
            P(),
            P(),
        ),
        check_vma=False,
    )
```

```python
import functools

import jax
import jax.numpy as jnp
from jax import lax
from jax.experimental import pallas as pl
from jax.experimental.pallas import tpu as pltpu
from jax.sharding import PartitionSpec as P

HEAD = 64
NORM_EPS = 1e-12
NEG = -1000000000.0
GELU_C = 0.7978845608
GELU_A = 0.044715

NN = (((1,), (0,)), ((), ()))
NT = (((1,), (1,)), ((), ()))
TN = (((0,), (0,)), ((), ()))

b16 = jnp.bfloat16
f32 = jnp.float32


def dot(left, right, dims):
    return lax.dot_general(left, right, dims, preferred_element_type=f32)


def rms_back(dout, scaled, rstd, gain):
    dscaled = dout * gain
    return rstd * (
        dscaled
        - jnp.mean(dscaled, axis=-1, keepdims=True)
        - scaled * jnp.mean(dscaled * scaled, axis=-1, keepdims=True)
    )


def col_sum(value):
    return jnp.sum(value, axis=0, keepdims=True)


def whole_step(
    cfg,
    len_ref,
    hid,
    og,
    wq,
    wk,
    wv,
    wo,
    wu,
    wd,
    bu,
    bq,
    bv,
    b_out,
    gain1,
    shift1,
    b_down,
    gain2,
    shift2,
    out,
    gib_out,
    gq_out,
    gk_out,
    gv_out,
    go_out,
    gu_out,
    gd_out,
    sm_out,
    w,
    hb,
    qkv,
    ex,
    inv,
    ctx,
    zs,
    rs,
    yb,
    act,
    gp,
    X,
    Y,
    dffn,
    dpre,
    dattn,
    dqkv,
    dct,
    xs,
    xr,
    bur,
    bqr,
    bvr,
    bcol,
    acc,
    sm,
    smr,
    G,
    gs,
    yr,
    xh,
    zr,
    hr,
    F,
    lsem,
    fs,
    fr,
    wys,
    wyr,
    wxs,
    wxr,
    wzs,
    wzr,
    wfs,
    wfr,
    es,
    er,
    ys,
    yrs,
    gxs,
    gxr,
    zss,
    zrs,
    hss,
    hrs,
    azs,
    azr,
    axs,
    axr,
    os,
    sms,
    smrs,
):
    T, D, A, B, C, R, NP, NH = (
        cfg["T"],
        cfg["D"],
        cfg["A"],
        cfg["B"],
        cfg["C"],
        cfg["R"],
        cfg["NP"],
        cfg["NH"],
    )
    NCH = T // C
    W = C
    TOT = 4 * A + 2 * D
    NS = TOT // R
    HR = R // 2
    Q = HR // NP
    NHH = A // HEAD
    HEADS = 2 * NHH
    MESH = pl.DeviceIdType.MESH
    UP, DN = 4 * A, 4 * A + D

    d = lax.axis_index("dp")
    t = lax.axis_index("tensor")
    y = t // 2
    c = t % 2
    x = d % 2
    z = d // 2
    zlo = z % NP
    zhi = z // NP
    t2 = (t + 2) % 4
    sib = (d, t + 1 - 2 * c)
    par = (d, t2)
    xp = (d + 1 - 2 * x, t)

    def zdev(k):
        return ((zhi * NP + (zlo + k) % NP) * 2 + x, t)

    def hdev(k):
        return ((((zhi + k) % NH) * NP + zlo) * 2 + x, t)

    def remote(src, dst, send, recv, dev):
        return pltpu.make_async_remote_copy(
            src_ref=src,
            dst_ref=dst,
            send_sem=send,
            recv_sem=recv,
            device_id=dev,
            device_id_type=MESH,
        )

    local = [
        pltpu.make_async_copy(hid.at[y], hb.at[0, pl.ds(t * B, B)], lsem.at[0]),
        pltpu.make_async_copy(wo, w.at[0, pl.ds(3 * A, A)], lsem.at[1]),
        pltpu.make_async_copy(wu, w.at[0, pl.ds(UP, D)], lsem.at[2]),
        pltpu.make_async_copy(wd, w.at[0, pl.ds(DN, D)], lsem.at[3]),
        pltpu.make_async_copy(og.at[0], Y.at[pl.ds(0, B)], lsem.at[4]),
        pltpu.make_async_copy(og.at[1], Y.at[pl.ds(B, B)], lsem.at[5]),
        pltpu.make_async_copy(wq, w.at[0, pl.ds(0, A)], lsem.at[6]),
        pltpu.make_async_copy(wk, w.at[0, pl.ds(A, A)], lsem.at[7]),
        pltpu.make_async_copy(wv, w.at[0, pl.ds(2 * A, A)], lsem.at[8]),
    ]
    for copy in local:
        copy.start()

    barrier = pltpu.get_barrier_semaphore()
    friends = [sib, par, xp] + [zdev(k) for k in range(1, NP)] + [hdev(k) for k in range(1, NH)]
    for dev in friends:
        pl.semaphore_signal(barrier, inc=1, device_id=dev, device_id_type=MESH)
    pl.semaphore_wait(barrier, len(friends))

    hid_sib = remote(hid.at[y], hb.at[0, pl.ds(t * B, B)], fs.at[0], fr.at[0], sib)
    hid_par = remote(hid.at[1 - y], hb.at[0, pl.ds(t * B, B)], fs.at[1], fr.at[1], par)
    bias_par = [
        remote(mine, theirs, fs.at[9 + i], fr.at[9 + i], par)
        for i, (mine, theirs) in enumerate(((bu, bur), (bq, bqr), (bv, bvr)))
    ]
    hid_sib.start()

    acc[...] = jnp.zeros_like(acc)

    WST = TOT // A
    WCH = A // 4
    zb = z % 2
    zp = ((z + 1 - 2 * zb) * 2 + x, t)

    def wrows(i, qx, qz):
        return pl.ds(pl.multiple_of(i * A + (2 * qx + qz) * WCH, WCH), WCH)

    def wy(i):
        rows = wrows(i, x, zb)
        return remote(w.at[0, rows], w.at[1, rows], wys.at[i], wyr.at[i], par)

    def wx(i):
        rows = wrows(i, x, zb)
        return remote(w.at[1, rows], w.at[1, rows], wxs.at[i], wxr.at[i], xp)

    def wz(i):
        rows = wrows(i, x, zb)
        return remote(w.at[1, rows], w.at[1, rows], wzs.at[i], wzr.at[i], zp)

    def wf(i):
        rows = wrows(i, 1 - x, zb) if i % 2 == 0 else wrows(i, x, 1 - zb)
        return remote(w.at[1, rows], w.at[1, rows], wfs.at[i], wfr.at[i], zp if i % 2 == 0 else xp)

    LOOK = 3

    def pump(i):
        wy(i).wait_recv()
        wx(i).start()
        wz(i).start()
        if i + LOOK < WST:
            wy(i + LOOK).start()

    def pass_on(i):
        (wx if i % 2 == 0 else wz)(i).wait_recv()
        wf(i).start()

    def have(lo, hi):
        for i in range(lo, hi):
            (wz if i % 2 == 0 else wx)(i).wait_recv()
            wf(i).wait_recv()

    for copy in local[6:]:
        copy.wait()
    wy(0).start()
    hid_par.start()
    for copy in bias_par:
        copy.start()
    wy(1).start()
    wy(2).start()
    for copy in local[:6]:
        copy.wait()
    G[0 : 2 * B] = Y[0 : 2 * B].astype(b16)

    pump(0)
    hid_par.wait_recv()
    rows_t2 = pl.ds(t2 * B, B)
    hid_fwd = remote(hb.at[0, rows_t2], hb.at[0, rows_t2], fs.at[3], fr.at[3], sib)
    hid_fwd.start()
    for copy in bias_par:
        copy.wait_recv()
    for half, sources in enumerate(((bq, bv), (bqr, bvr))):
        for i, source in enumerate(sources):
            bcol[half, i * A : (i + 1) * A] = jnp.transpose(jnp.broadcast_to(source[...], (128, A)))
    hid_sib.wait_recv()
    hid_fwd.wait_recv()

    b_out, gain1, shift1, b_down, gain2, shift2 = (
        ref[...].reshape(1, D) for ref in (b_out, gain1, shift1, b_down, gain2, shift2)
    )
    length = len_ref[y]

    def loop(lo, hi, f):
        def step(i, carry):
            f(i)
            return carry

        lax.fori_loop(lo, hi, step, 0)

    def chunk(m):
        return pl.ds(pl.multiple_of(m * C, C), C)

    def wide_chunk(m):
        return pl.ds(pl.multiple_of(m * W, W), W)

    def xcopy(k, m):
        return remote(xs.at[k % 2, chunk(m)], xr.at[k % 2, chunk(m)], es.at[k % 2, m], er.at[k % 2, m], sib)

    def xsend(k, m, value):
        xs[k % 2, chunk(m)] = value.astype(b16)
        xcopy(k, m).start()

    def xget(k, m):
        xcopy(k, m).wait()
        return xs[k % 2, chunk(m)].astype(f32) + xr[k % 2, chunk(m)].astype(f32)

    def project(l, m):
        tok = wide_chunk(m)
        for half in range(2):
            got = dot(w[half, 0 : 3 * A], hb[l, tok], NT)
            base = half * 3 * A
            bq = jnp.concatenate([bcol[half, 0:A]] * (W // 128), axis=1)
            bv = jnp.concatenate([bcol[half, A : 2 * A]] * (W // 128), axis=1)
            qkv[l, base : base + A, tok] = ((got[0:A] + bq).astype(b16) * b16(HEAD**-0.5)).astype(b16)
            qkv[l, base + A : base + 2 * A, tok] = got[A : 2 * A].astype(b16)
            qkv[l, base + 2 * A : base + 3 * A, tok] = (got[2 * A : 3 * A] + bv).astype(b16)

    def head_rows(h, part):
        base = (h // NHH) * (3 * A) + part * A + (h % NHH) * HEAD
        return pl.ds(pl.multiple_of(base, HEAD), HEAD)

    def attend(l, h):
        counted = lax.broadcasted_iota(jnp.int32, (T, T), 0) < length
        scores = dot(qkv[l, head_rows(h, 1)], qkv[l, head_rows(h, 0)], TN)
        scores = jnp.where(counted, scores, NEG)
        top = jnp.max(scores, axis=0, keepdims=True)
        e = jnp.exp(scores - top)
        one = 1.0 / jnp.sum(e, axis=0, keepdims=True)
        eb = e.astype(b16)
        ex[l, h] = eb
        inv[l, h] = one
        got = dot(qkv[l, head_rows(h, 2)], eb, NN) * one
        ctx[l, pl.ds(pl.multiple_of(h * HEAD, HEAD), HEAD)] = got.astype(b16)

    def attend_range(l, lo, hi):
        loop(lo, hi, lambda h: attend(l, h))

    def attn_out(l, k):
        def step(m):
            tok = chunk(m)
            part = dot(ctx[l, 0:A, tok], w[0, 3 * A : 4 * A], TN)
            part += dot(ctx[l, A : 2 * A, tok], w[1, 3 * A : 4 * A], TN)
            xsend(k, m, part)

        loop(0, NCH, step)

    def zrows(z_at, m):
        return pl.ds(pl.multiple_of(z_at * T + m * C, C), C)

    def norm(resid, gain, shift, z_at, m):
        rows = chunk(m)
        centre = resid - jnp.mean(resid, axis=-1, keepdims=True)
        rstd = lax.rsqrt(jnp.mean(centre * centre, axis=-1, keepdims=True) + NORM_EPS)
        scaled = centre * rstd
        zs[zrows(z_at, m)] = scaled.astype(b16)
        rs[rows, z_at : z_at + 1] = rstd
        return scaled * gain + shift

    def norm_one(l, k, m):
        rows = chunk(m)
        before = hb[0, rows].astype(f32) if l == 0 else X[rows]
        first = norm(xget(k, m) + b_out + before, gain1, shift1, 2 * l, m)
        Y[rows] = first
        yb[l, rows] = first.astype(b16)

    def up_chunk(l, m):
        rows = chunk(m)
        for half, source in enumerate((bu, bur)):
            cols = pl.ds(half * D, D)
            pre = dot(yb[l, rows], w[half, UP : UP + D], NN) + source[...].reshape(1, D)
            square = pre * pre
            th = jnp.tanh(GELU_C * pre * (1.0 + GELU_A * square))
            more = 0.5 * (1.0 + th)
            act[l, rows, cols] = (pre * more).astype(b16)
            slope = more + (0.5 * GELU_C) * pre * (1.0 - th * th) * (1.0 + (3 * GELU_A) * square)
            gp[l, rows, cols] = slope.astype(b16)

    def down_chunk(l, k, m):
        rows = chunk(m)
        part = dot(act[l, rows, 0:D], w[0, DN : DN + D], NN)
        part += dot(act[l, rows, D : 2 * D], w[1, DN : DN + D], NN)
        xsend(k, m, part)

    def norm_two(l, k, m):
        rows = chunk(m)
        result = norm(xget(k, m) + b_down + Y[rows], gain2, shift2, 2 * l + 1, m)
        X[rows] = result
        if l == 0:
            hb[1, rows] = result.astype(b16)

    pump(1)
    pass_on(0)
    pump(2)
    pass_on(1)
    pump(3)
    pass_on(2)
    have(0, 3)
    loop(0, T // W, lambda m: project(0, m))
    done = 4
    for h in range(HEADS):
        attend(0, h)
        if done < WST:
            pump(done)
            pass_on(done - 1)
            done += 1
    have(3, 4)
    attn_out(0, 0)
    while done < WST:
        pump(done)
        pass_on(done - 1)
        done += 1
    pass_on(WST - 1)
    loop(0, NCH, lambda m: norm_one(0, 0, m))
    have(4, 8)
    loop(0, NCH, lambda m: up_chunk(0, m))
    og_rows = pl.ds(t * B, B)
    og_mine, og_other = G.at[pl.ds(y * B, B)], G.at[pl.ds((1 - y) * B, B)]
    og_keep = pltpu.make_async_copy(og_mine, dattn.at[0, og_rows], lsem.at[0])
    og_sib = remote(og_mine, dattn.at[0, og_rows], fs.at[4], fr.at[4], sib)
    og_par = remote(og_other, dattn.at[0, og_rows], fs.at[5], fr.at[5], par)
    og_keep.start()
    og_par.start()
    og_sib.start()
    have(8, WST)
    loop(0, NCH, lambda m: down_chunk(0, 1, m))

    def next_layer(m):
        norm_two(0, 1, m)
        project(1, m)

    loop(0, T // W, next_layer)

    attend_range(1, 0, HEADS)
    og_par.wait_recv()
    og_fwd = remote(dattn.at[0, rows_t2], dattn.at[0, rows_t2], fs.at[6], fr.at[6], sib)
    og_fwd.start()
    attn_out(1, 2)

    def feed_forward(m):
        norm_one(1, 2, m)
        up_chunk(1, m)
        down_chunk(1, 3, m)

    loop(0, NCH, feed_forward)
    loop(0, NCH, lambda m: norm_two(1, 3, m))
    out_keep = pltpu.make_async_copy(X.at[pl.ds(t * B, B)], out.at[y], lsem.at[1])
    out_par = remote(X.at[pl.ds(t2 * B, B)], out.at[y], fs.at[7], fr.at[7], par)
    out_keep.start()
    out_par.start()
    og_keep.wait()
    og_sib.wait_recv()
    og_fwd.wait_recv()

    def ffn_back(l, k, m):
        rows = chunk(m)
        dout = dattn[0, rows].astype(f32) if l == 1 else X[rows]
        scaled = zs[zrows(2 * l + 1, m)].astype(f32)
        dr = rms_back(dout, scaled, rs[rows, 2 * l + 1 : 2 * l + 2], gain2)
        acc[3:4] += col_sum(dr)
        acc[4:5] += col_sum(dout * scaled)
        acc[5:6] += col_sum(dout)
        Y[rows] = dr
        drb = dr.astype(b16)
        dffn[l, rows] = drb
        part = None
        for half in range(2):
            cols = pl.ds(half * D, D)
            dact = dot(drb, w[half, DN : DN + D], NT)
            dp = (dact * gp[l, rows, cols].astype(f32)).astype(b16)
            dpre[l, rows, cols] = dp
            row = 6 + 8 * half
            acc[row : row + 1] += col_sum(dp.astype(f32))
            got = dot(dp, w[half, UP : UP + D], NT)
            part = got if part is None else part + got
        xsend(k, m, part)

    def attn_out_back(l, k, m):
        rows = chunk(m)
        dfirst = Y[rows] + xget(k, m)
        scaled = zs[zrows(2 * l, m)].astype(f32)
        dr = rms_back(dfirst, scaled, rs[rows, 2 * l : 2 * l + 1], gain1)
        acc[0:1] += col_sum(dr)
        acc[1:2] += col_sum(dfirst * scaled)
        acc[2:3] += col_sum(dfirst)
        Y[rows] = dr
        drb = dr.astype(b16)
        dattn[l, rows] = drb

    def context_back(l):
        for half in range(2):
            got = dot(w[half, 3 * A : 4 * A], dattn[l], NT)
            for j in range(NHH):
                h = half * NHH + j
                scaled_rows = got[j * HEAD : (j + 1) * HEAD] * inv[l, h]
                dct[h * HEAD : (h + 1) * HEAD] = scaled_rows.astype(b16)

    def attend_back(l, h):
        mine = pl.ds(pl.multiple_of(h * HEAD, HEAD), HEAD)
        dc = dct[mine]
        dprobs = dot(qkv[l, head_rows(h, 2)], dc, TN)
        eb = ex[l, h]
        ef = eb.astype(f32)
        inner = col_sum(ef * dprobs) * inv[l, h]
        ds = (ef * (dprobs - inner)).astype(b16)
        dqkv[l, head_rows(h, 2)] = dot(dc, eb, NT).astype(b16)
        dqkv[l, head_rows(h, 0)] = (dot(qkv[l, head_rows(h, 1)], ds, NN) * (HEAD**-0.5)).astype(b16)
        dqkv[l, head_rows(h, 1)] = dot(qkv[l, head_rows(h, 0)], ds, NT).astype(b16)

    def attend_back_range(l, lo, hi):
        loop(lo, hi, lambda h: attend_back(l, h))

    def project_back(l, k):
        def step(m):
            tok = chunk(m)
            part = dot(dqkv[l, 0 : 3 * A, tok], w[0, 0 : 3 * A], TN)
            part += dot(dqkv[l, 3 * A : 6 * A, tok], w[1, 0 : 3 * A], TN)
            xsend(k, m, part)

        loop(0, NCH, step)
        ones = jnp.ones((8, T), b16)
        for half in range(2):
            sums = dot(ones, dqkv[l, half * 3 * A : (half + 1) * 3 * A], NT)
            row = 7 + 8 * half
            acc[row : row + 1, 0 : 3 * A] += sums[0:1]

    loop(0, NCH, lambda m: ffn_back(1, 4, m))
    loop(0, NCH, lambda m: attn_out_back(1, 4, m))
    context_back(1)
    attend_back_range(1, 0, HEADS)
    for copy in (og_sib, og_par, og_fwd):
        copy.wait_send()
    out_keep.wait()
    out_par.wait_send()
    project_back(1, 5)

    def first_layer(m):
        rows = chunk(m)
        X[rows] = Y[rows] + xget(5, m)
        ffn_back(0, 6, m)

    loop(0, NCH, first_layer)

    def both(ref, cols=slice(None)):
        value = ref[:, :, cols]
        return value.reshape(2 * value.shape[1], value.shape[2])

    FREE = T - 4 * A

    def grad_down(half, dst, off=0):
        dy = both(dffn)
        for i in reversed(range(D // 256)):
            left = both(act, slice(half * D + i * 256, half * D + (i + 1) * 256))
            dst[off + DN + i * 256 : off + DN + (i + 1) * 256] = dot(left, dy, TN).astype(b16)

    def grad_up(half, dst, off=0):
        dy = both(dpre, slice(half * D, (half + 1) * D))
        for i in reversed(range(D // 256)):
            left = both(yb, slice(i * 256, (i + 1) * 256))
            dst[off + UP + i * 256 : off + UP + (i + 1) * 256] = dot(left, dy, TN).astype(b16)

    def grad_attn(half, dst):
        rows = slice(half * A, (half + 1) * A)
        got = dot(ctx[0, rows], dattn[0], NN) + dot(ctx[1, rows], dattn[1], NN)
        dst[3 * A : 4 * A] = got.astype(b16)
        rows = slice(half * 3 * A, (half + 1) * 3 * A)
        got = dot(dqkv[0, rows], hb[0], NN) + dot(dqkv[1, rows], hb[1], NN)
        dst[0 : 3 * A] = got.astype(b16)

    def top_of(s):
        return pl.multiple_of(TOT - (s + 1) * R, R)

    def piece(s):
        return pl.ds(top_of(s), R)

    def half_of(s, which):
        return pl.ds(pl.multiple_of(top_of(s) + which * HR, HR), HR)

    def part_of(s, which, p):
        return pl.ds(pl.multiple_of(top_of(s) + which * HR + p * Q, Q), Q)

    def ycopy_ffn(s):
        src = zs.at[pl.ds(pl.multiple_of(top_of(s) + FREE, R), R)]
        return remote(src, yr.at[piece(s)], ys.at[s], yrs.at[s], par)

    def ycopy_attn(s):
        return remote(gs.at[piece(s)], yr.at[piece(s)], ys.at[s], yrs.at[s], par)

    def ycopy(s):
        return remote(yr.at[piece(s)], yr.at[piece(s)], ys.at[s], yrs.at[s], par)

    def gxcopy(s):
        return remote(G.at[half_of(s, 1 - x)], xh.at[s], gxs.at[s], gxr.at[s], xp)

    def zcopy(s, k):
        src = G.at[part_of(s, x, (zlo + k) % NP)]
        return remote(src, zr.at[s, k - 1], zss.at[s, k - 1], zrs.at[s, k - 1], zdev(k))

    def hcopy(s, k):
        src = G.at[part_of(s, x, zlo)]
        return remote(src, hr.at[s % 2, k - 1], hss.at[s, k - 1], hrs.at[s, k - 1], hdev(k))

    def azcopy(s, k):
        rows = part_of(s, x, zlo)
        return remote(F.at[rows], F.at[rows], azs.at[s, k - 1], azr.at[s, k - 1], zdev(k))

    def axcopy(s, k):
        rows = part_of(s, x, (zlo + NP - k) % NP)
        return remote(F.at[rows], F.at[rows], axs.at[s, k], axr.at[s, k], xp)

    ocopies = [
        pltpu.make_async_copy(F.at[pl.ds(lo, rows)], ref, os.at[i])
        for i, (ref, lo, rows) in enumerate(
            (
                (gd_out, DN, D),
                (gu_out, UP, D),
                (go_out, 3 * A, A),
                (gv_out, 2 * A, A),
                (gk_out, A, A),
                (gq_out, 0, A),
            )
        )
    ]

    YLOOK = 3

    def ystart(s):
        if isinstance(s, int):
            if s < NS:
                (ycopy_ffn if s < 2 * D // R else ycopy_attn)(s).start()
            return

        @pl.when(s < 2 * D // R)
        def _():
            ycopy_ffn(s).start()

        @pl.when((s >= 2 * D // R) & (s < NS))
        def _():
            ycopy_attn(s).start()

    def stage_x(s):
        ycopy(s).wait_recv()
        ystart(s + YLOOK)
        for which in (1 - x, x):
            rows = half_of(s, which)
            G[rows] = (G[rows].astype(f32) + yr[rows].astype(f32)).astype(b16)
            if which is not x:
                gxcopy(s).start()

    def stage_z(s):
        gxcopy(s).wait_recv()
        rows = half_of(s, x)
        G[rows] = (G[rows].astype(f32) + xh[s].astype(f32)).astype(b16)
        for k in range(1, NP):
            zcopy(s, k).start()

    def stage_sum(s):
        rows = part_of(s, x, zlo)
        total = G[rows].astype(f32)
        for k in range(1, NP):
            zcopy(s, k).wait_recv()
            total += zr[s, k - 1].astype(f32)
        if NH > 1:
            G[rows] = total.astype(b16)
            for k in range(1, NH):
                hcopy(s, k).start()
            for k in range(1, NH):
                hcopy(s, k).wait()
                total += hr[s % 2, k - 1].astype(f32)
        F[rows] = total.astype(b16)
        for k in range(1, NP):
            azcopy(s, k).start()
        axcopy(s, 0).start()

    def stage_swap(s):
        for k in range(1, NP):
            azcopy(s, k).wait_recv()
            axcopy(s, k).start()

    def stage_out(s):
        for k in range(NP):
            axcopy(s, k).wait_recv()

    stages = (stage_x, stage_z, stage_sum, stage_swap, stage_out)

    def run(i):
        for lag, stage in enumerate(stages):
            s = i - lag
            if isinstance(s, int) and not 0 <= s < NS:
                continue
            stage(s)

    grad_down(1, zs, FREE)
    for s in range(YLOOK):
        ystart(s)
    grad_up(1, zs, FREE)
    grad_down(0, G)
    loop(0, NCH, lambda m: attn_out_back(0, 6, m))
    context_back(0)
    run(0)
    grad_up(0, G)
    attend_back_range(0, 0, HEADS // 2)
    run(1)
    attend_back_range(0, HEADS // 2, HEADS)
    run(2)
    project_back(0, 7)
    grad_attn(1, gs)
    run(3)
    acc[8:14] = acc[0:6]
    sm_y = remote(acc.at[pl.ds(8, 8)], smr.at[0], sms.at[0], smrs.at[0], par)
    sm_y.start()

    def last(m):
        rows = chunk(m)
        X[rows] = Y[rows] + xget(7, m)

    loop(0, NCH, last)
    xs[0, 0:B] = X[pl.ds(t * B, B)].astype(b16)
    xs[0, B : 2 * B] = X[pl.ds(t2 * B, B)].astype(b16)
    gi_keep = pltpu.make_async_copy(xs.at[0, pl.ds(0, B)], gib_out.at[y], lsem.at[2])
    gi_par = remote(xs.at[0, pl.ds(B, B)], gib_out.at[y], fs.at[8], fr.at[8], par)
    gi_keep.start()
    gi_par.start()
    grad_attn(0, G)

    loop(4, D // R + 4, run)
    ocopies[0].start()
    loop(D // R + 4, NS, run)
    for i in range(NS, NS + 2):
        run(i)
    sm_y.wait_recv()
    sm[0] = acc[0:8] + smr[0]
    sm_x = remote(sm.at[0], smr.at[1], sms.at[1], smrs.at[1], xp)
    sm_x.start()
    run(NS + 2)
    sm_x.wait_recv()
    sm[1] = sm[0] + smr[1]
    sm_z = [
        remote(sm.at[1], smr.at[1 + k], sms.at[1 + k], smrs.at[1 + k], zdev(k)) for k in range(1, NP)
    ]
    for copy in sm_z:
        copy.start()
    run(NS + 3)
    for copy in ocopies[1:]:
        copy.start()
    total = sm[1]
    for k, copy in enumerate(sm_z):
        copy.wait_recv()
        total += smr[2 + k]
    sm[2] = total
    if NH > 1:
        sm_h = [
            remote(sm.at[2], smr.at[NP + k], sms.at[NP + k], smrs.at[NP + k], hdev(k))
            for k in range(1, NH)
        ]
        for copy in sm_h:
            copy.start()
        for k, copy in enumerate(sm_h):
            copy.wait()
            total += smr[NP + 1 + k]
    sm_out[...] = total

    for copy in (hid_sib, hid_par, *bias_par, hid_fwd, gi_par, sm_y, sm_x):
        copy.wait_send()
    for copy in sm_z:
        copy.wait_send()
    out_par.wait_recv()
    gi_par.wait_recv()
    gi_keep.wait()
    for i in range(WST):
        wy(i).wait_send()
        wx(i).wait_send()
        wz(i).wait_send()
        wf(i).wait_send()

    def drain(s):
        ycopy(s).wait_send()
        gxcopy(s).wait_send()
        for k in range(1, NP):
            zcopy(s, k).wait_send()
            azcopy(s, k).wait_send()
        for k in range(NP):
            axcopy(s, k).wait_send()

    loop(0, NS, drain)
    for copy in ocopies:
        copy.wait()


def widen(*refs):
    names = 7
    big, result, small = refs[:names], refs[names], refs[names + 1]
    refs = refs[names + 2 :]
    wide, result_out, vectors = refs[:names], refs[names], refs[names + 1 : names + 10]
    refs = refs[names + 10 :]
    narrow, broad = refs[:names], refs[names : 2 * names]
    through, isem, osem = refs[2 * names :]
    loads = [pltpu.make_async_copy(big[i], narrow[i], isem.at[i]) for i in range(names)]
    stores = [pltpu.make_async_copy(broad[i], wide[i], osem.at[i]) for i in range(names)]
    keep_in = pltpu.make_async_copy(result, through, isem.at[names])
    keep = pltpu.make_async_copy(through, result_out, osem.at[names])
    for copy in loads:
        copy.start()
    keep_in.start()
    for i, ref in enumerate(vectors):
        if i < 7:
            ref[...] = small[i, :]
        else:
            rows = ref.shape[0]
            at = (i - 7) * 2 * rows
            ref[...] = small[7, at : at + rows]
    for load, store, i in zip(loads, stores, range(names)):
        load.wait()
        broad[i][...] = narrow[i][...].astype(f32)
        store.start()
    keep_in.wait()
    keep.start()
    for copy in stores:
        copy.wait()
    keep.wait()


def shards(
    dp,
    hidden_in,
    lengths,
    w_query,
    b_query,
    w_key,
    w_value,
    b_value,
    w_out,
    b_out,
    norm1_gain,
    norm1_shift,
    w_up,
    b_up,
    w_down,
    b_down,
    norm2_gain,
    norm2_shift,
    out_grad,
):
    _, B, D = hidden_in.shape
    A = w_query.shape[1]
    T = 4 * B
    TOT = 4 * A + 2 * D
    R = 128
    HR = R // 2
    nz = dp // 2
    NP = 1
    while nz % (2 * NP) == 0 and HR % (32 * NP) == 0:
        NP *= 2
    NH = nz // NP
    C = T // 2
    NCH = T // C
    NS = TOT // R
    Q = HR // NP
    heads = 2 * A // HEAD
    cfg = dict(T=T, D=D, A=A, B=B, C=C, R=R, NP=NP, NH=NH)
    rows = [
        value if value.shape[0] == D else value.reshape(1, -1)
        for value in (
            b_up,
            b_query,
            b_value,
            b_out,
            norm1_gain,
            norm1_shift,
            b_down,
            norm2_gain,
            norm2_shift,
        )
    ]
    V = functools.partial(pltpu.VMEM)
    DMA = pltpu.SemaphoreType.DMA
    NPx = max(NP - 1, 1)
    NHx = max(NH - 1, 1)
    scratch = [
        V((2, TOT, D), b16),
        V((2, T, D), b16),
        V((2, 6 * A, T), b16),
        V((2, heads, T, T), b16),
        V((2, heads, 1, T), f32),
        V((2, 2 * A, T), b16),
        V((max(4 * T, T + 2 * D), D), b16),
        V((T, 128), f32),
        V((2, T, D), b16),
        V((2, T, 2 * D), b16),
        V((2, T, 2 * D), b16),
        V((T, D), f32),
        V((T, D), f32),
        V((2, T, D), b16),
        V((2, T, 2 * D), b16),
        V((2, T, D), b16),
        V((2, 6 * A, T), b16),
        V((2 * A, T), b16),
        V((2, T, D), b16),
        V((2, T, D), b16),
        V((D,), f32),
        V((1, A), f32),
        V((1, A), f32),
        V((2, 2 * A, 128), f32),
        V((16, D), f32),
        V((3, 8, D), f32),
        V((NP + NH, 8, D), f32),
        V((TOT, D), b16),
        V((4 * A, D), b16),
        V((TOT, D), b16),
        V((NS, HR, D), b16),
        V((NS, NPx, Q, D), b16),
        V((2, NHx, Q, D), b16),
        V((TOT, D), b16),
        DMA((9,)),
        DMA((12,)),
        DMA((12,)),
        DMA((TOT // A,)),
        DMA((TOT // A,)),
        DMA((TOT // A,)),
        DMA((TOT // A,)),
        DMA((TOT // A,)),
        DMA((TOT // A,)),
        DMA((TOT // A,)),
        DMA((TOT // A,)),
        DMA((2, NCH)),
        DMA((2, NCH)),
        DMA((NS,)),
        DMA((NS,)),
        DMA((NS,)),
        DMA((NS,)),
        DMA((NS, NPx)),
        DMA((NS, NPx)),
        DMA((NS, NHx)),
        DMA((NS, NHx)),
        DMA((NS, NPx)),
        DMA((NS, NPx)),
        DMA((NS, NP)),
        DMA((NS, NP)),
        DMA((6,)),
        DMA((NP + NH,)),
        DMA((NP + NH,)),
    ]
    anywhere = pl.BlockSpec(memory_space=pl.ANY)
    vmem = pl.BlockSpec(memory_space=pltpu.VMEM)
    smem = pl.BlockSpec(memory_space=pltpu.SMEM)
    result, gib, gq, gk, gv, go, gu, gd, small = pl.pallas_call(
        functools.partial(whole_step, cfg),
        out_shape=(
            jax.ShapeDtypeStruct((2, B, D), f32),
            jax.ShapeDtypeStruct((2, B, D), b16),
            jax.ShapeDtypeStruct((A, D), b16),
            jax.ShapeDtypeStruct((A, D), b16),
            jax.ShapeDtypeStruct((A, D), b16),
            jax.ShapeDtypeStruct((A, D), b16),
            jax.ShapeDtypeStruct((D, D), b16),
            jax.ShapeDtypeStruct((D, D), b16),
            jax.ShapeDtypeStruct((8, D), f32),
        ),
        in_specs=[smem] + [anywhere] * 8 + [vmem] * 9,
        out_specs=(anywhere,) * 8 + (vmem,),
        scratch_shapes=scratch,
        compiler_params=pltpu.CompilerParams(
            collective_id=0, has_side_effects=True, vmem_limit_bytes=64 * 2**20
        ),
    )(
        lengths,
        hidden_in,
        out_grad,
        w_query.T,
        w_key.T,
        w_value.T,
        w_out,
        w_up,
        w_down,
        *rows,
    )
    bigs = (gd, gu, go, gq, gk, gv, gib)
    gd, gu, go, gq, gk, gv, gi, result, *vectors = pl.pallas_call(
        widen,
        out_shape=tuple(jax.ShapeDtypeStruct(v.shape, f32) for v in bigs + (result,))
        + (jax.ShapeDtypeStruct((D,), f32),) * 7
        + (jax.ShapeDtypeStruct((A,), f32),) * 2,
        in_specs=[anywhere] * 8 + [vmem],
        out_specs=(anywhere,) * 8 + (vmem,) * 9,
        scratch_shapes=[V(v.shape, b16) for v in bigs]
        + [V(v.shape, f32) for v in bigs]
        + [V(result.shape, f32), DMA((8,)), DMA((8,))],
        compiler_params=pltpu.CompilerParams(vmem_limit_bytes=64 * 2**20),
    )(*bigs, result, small)
    db_out, dgain1, dshift1, db_down, dgain2, dshift2, db_up, db_query, db_value = vectors
    return (
        result,
        gi,
        gq.T,
        db_query,
        gk.T,
        gv.T,
        db_value,
        go,
        db_out,
        dgain1,
        dshift1,
        gu,
        db_up,
        gd,
        db_down,
        dgain2,
        dshift2,
    )


def solution(mesh):
    placed = (
        P("dp", "tensor", None),
        P("dp"),
        P(None, "tensor"),
        P("tensor"),
        P(None, "tensor"),
        P(None, "tensor"),
        P("tensor"),
        P("tensor", None),
        P(),
        P(),
        P(),
        P(None, "tensor"),
        P("tensor"),
        P("tensor", None),
        P(),
        P(),
        P(),
        P("dp", "tensor", None),
    )
    return jax.shard_map(
        functools.partial(shards, mesh.shape["dp"]),
        mesh=mesh,
        in_specs=placed,
        out_specs=(
            P("dp", "tensor", None),
            P("dp", "tensor", None),
            P(None, "tensor"),
            P("tensor"),
            P(None, "tensor"),
            P(None, "tensor"),
            P("tensor"),
            P("tensor", None),
            P(),
            P(),
            P(),
            P(None, "tensor"),
            P("tensor"),
            P("tensor", None),
            P(),
            P(),
            P(),
        ),
        check_vma=False,
    )
```

```python
import functools

import jax
import jax.numpy as jnp
from jax import lax
from jax.experimental import pallas as pl
from jax.experimental.pallas import tpu as pltpu
from jax.sharding import PartitionSpec as P

HEAD = 64
NORM_EPS = 1e-12
NEG = -1000000000.0
GELU_C = 0.7978845608
GELU_A = 0.044715

NN = (((1,), (0,)), ((), ()))
NT = (((1,), (1,)), ((), ()))
TN = (((0,), (0,)), ((), ()))

b16 = jnp.bfloat16
f32 = jnp.float32


def dot(left, right, dims):
    return lax.dot_general(left, right, dims, preferred_element_type=f32)


def rms_back(dout, scaled, rstd, gain):
    dscaled = dout * gain
    return rstd * (
        dscaled
        - jnp.mean(dscaled, axis=-1, keepdims=True)
        - scaled * jnp.mean(dscaled * scaled, axis=-1, keepdims=True)
    )


def col_sum(value):
    return jnp.sum(value, axis=0, keepdims=True)


def whole_step(
    cfg,
    len_ref,
    hid,
    og,
    wq,
    wk,
    wv,
    wo,
    wu,
    wd,
    bu,
    bq,
    bv,
    b_out,
    gain1,
    shift1,
    b_down,
    gain2,
    shift2,
    out,
    gib_out,
    gq_out,
    gk_out,
    gv_out,
    go_out,
    gu_out,
    gd_out,
    sm_out,
    w,
    hb,
    qkv,
    ex,
    inv,
    ctx,
    zs,
    rs,
    yb,
    act,
    gp,
    X,
    Y,
    dffn,
    dpre,
    dattn,
    dqkv,
    dct,
    xs,
    xr,
    bur,
    bqr,
    bvr,
    bcol,
    acc,
    sm,
    smr,
    G,
    gs,
    yr,
    xh,
    zr,
    hr,
    F,
    lsem,
    fs,
    fr,
    wys,
    wyr,
    wxs,
    wxr,
    wzs,
    wzr,
    wfs,
    wfr,
    wds,
    wdr,
    es,
    er,
    ys,
    yrs,
    gxs,
    gxr,
    zss,
    zrs,
    hss,
    hrs,
    azs,
    azr,
    axs,
    axr,
    os,
    sms,
    smrs,
):
    T, D, A, B, C, R, NP, NH = (
        cfg["T"],
        cfg["D"],
        cfg["A"],
        cfg["B"],
        cfg["C"],
        cfg["R"],
        cfg["NP"],
        cfg["NH"],
    )
    NCH = T // C
    W = 2 * C
    NW = T // W
    TOT = 4 * A + 2 * D
    NS = TOT // R
    HR = R // 2
    Q = HR // NP
    NHH = A // HEAD
    HEADS = 2 * NHH
    MESH = pl.DeviceIdType.MESH
    UP, DN = 4 * A, 4 * A + D

    d = lax.axis_index("dp")
    t = lax.axis_index("tensor")
    y = t // 2
    c = t % 2
    x = d % 2
    z = d // 2
    zlo = z % NP
    zhi = z // NP
    t2 = (t + 2) % 4
    sib = (d, t + 1 - 2 * c)
    par = (d, t2)
    xp = (d + 1 - 2 * x, t)

    def zdev(k):
        return ((zhi * NP + (zlo + k) % NP) * 2 + x, t)

    def hdev(k):
        return ((((zhi + k) % NH) * NP + zlo) * 2 + x, t)

    def remote(src, dst, send, recv, dev):
        return pltpu.make_async_remote_copy(
            src_ref=src,
            dst_ref=dst,
            send_sem=send,
            recv_sem=recv,
            device_id=dev,
            device_id_type=MESH,
        )

    local = [
        pltpu.make_async_copy(hid.at[y], hb.at[0, pl.ds(t * B, B)], lsem.at[0]),
        pltpu.make_async_copy(wo, w.at[0, pl.ds(3 * A, A)], lsem.at[1]),
        pltpu.make_async_copy(wu, w.at[0, pl.ds(UP, D)], lsem.at[2]),
        pltpu.make_async_copy(wd, w.at[0, pl.ds(DN, D)], lsem.at[3]),
        pltpu.make_async_copy(og.at[0], Y.at[pl.ds(0, B)], lsem.at[4]),
        pltpu.make_async_copy(og.at[1], Y.at[pl.ds(B, B)], lsem.at[5]),
        pltpu.make_async_copy(wq, w.at[0, pl.ds(0, A)], lsem.at[6]),
        pltpu.make_async_copy(wk, w.at[0, pl.ds(A, A)], lsem.at[7]),
        pltpu.make_async_copy(wv, w.at[0, pl.ds(2 * A, A)], lsem.at[8]),
    ]
    for copy in local:
        copy.start()

    barrier = pltpu.get_barrier_semaphore()
    friends = [sib, par, xp] + [zdev(k) for k in range(1, NP)] + [hdev(k) for k in range(1, NH)]
    for dev in friends:
        pl.semaphore_signal(barrier, inc=1, device_id=dev, device_id_type=MESH)
    pl.semaphore_wait(barrier, len(friends))

    hid_sib = remote(hid.at[y], hb.at[0, pl.ds(t * B, B)], fs.at[0], fr.at[0], sib)
    hid_par = remote(hid.at[1 - y], hb.at[0, pl.ds(t * B, B)], fs.at[1], fr.at[1], par)
    bias_par = [
        remote(mine, theirs, fs.at[9 + i], fr.at[9 + i], par)
        for i, (mine, theirs) in enumerate(((bu, bur), (bq, bqr), (bv, bvr)))
    ]
    hid_sib.start()

    acc[...] = jnp.zeros_like(acc)

    WST = TOT // A
    WCH = A // 4
    zb = z % 2
    zp = ((z + 1 - 2 * zb) * 2 + x, t)

    def wrows(i, qx, qz):
        return pl.ds(pl.multiple_of(i * A + (2 * qx + qz) * WCH, WCH), WCH)

    def wy(i):
        rows = wrows(i, x, zb)
        return remote(w.at[0, rows], w.at[1, rows], wys.at[i], wyr.at[i], par)

    def wx(i):
        rows = wrows(i, x, zb)
        return remote(w.at[1, rows], w.at[1, rows], wxs.at[i], wxr.at[i], xp)

    def wz(i):
        rows = wrows(i, x, zb)
        return remote(w.at[1, rows], w.at[1, rows], wzs.at[i], wzr.at[i], zp)

    def wf(i):
        rows = wrows(i, 1 - x, zb) if i % 2 == 0 else wrows(i, x, 1 - zb)
        return remote(w.at[1, rows], w.at[1, rows], wfs.at[i], wfr.at[i], zp if i % 2 == 0 else xp)

    LATE = WST - D // A

    def wd(i):
        rows = wrows(i, 1 - x, 1 - zb)
        return remote(w.at[0, rows], w.at[1, rows], wds.at[i], wdr.at[i], par)

    LOOK = 4

    def send_quarters(i):
        if i < WST:
            wy(i).start()
            if i >= LATE:
                wd(i).start()

    def pump(i):
        wy(i).wait_recv()
        wx(i).start()
        wz(i).start()
        send_quarters(i + LOOK)

    def pass_on(i):
        (wx if i % 2 == 0 else wz)(i).wait_recv()
        wf(i).start()

    def have(lo, hi):
        for i in range(lo, hi):
            if i >= LATE:
                wx(i).wait_recv()
                wz(i).wait_recv()
                wd(i).wait_recv()
                continue
            (wz if i % 2 == 0 else wx)(i).wait_recv()
            wf(i).wait_recv()

    for copy in local[6:]:
        copy.wait()
    for i in range(3):
        wy(i).start()
    hid_par.start()
    for copy in bias_par:
        copy.start()
    for copy in local[:6]:
        copy.wait()
    wy(3).start()
    G[0 : 2 * B] = Y[0 : 2 * B].astype(b16)

    pump(0)
    pump(1)
    pass_on(0)
    pump(2)
    pass_on(1)
    hid_par.wait_recv()
    rows_t2 = pl.ds(t2 * B, B)
    hid_fwd = remote(hb.at[0, rows_t2], hb.at[0, rows_t2], fs.at[3], fr.at[3], sib)
    hid_fwd.start()
    for copy in bias_par:
        copy.wait_recv()
    for half, sources in enumerate(((bq, bv), (bqr, bvr))):
        for i, source in enumerate(sources):
            bcol[half, i * A : (i + 1) * A] = jnp.transpose(jnp.broadcast_to(source[...], (128, A)))
    hid_sib.wait_recv()
    hid_fwd.wait_recv()

    b_out, gain1, shift1, b_down, gain2, shift2 = (
        ref[...].reshape(1, D) for ref in (b_out, gain1, shift1, b_down, gain2, shift2)
    )
    length = len_ref[y]

    def loop(lo, hi, f):
        def step(i, carry):
            f(i)
            return carry

        lax.fori_loop(lo, hi, step, 0)

    def chunk(m):
        return pl.ds(pl.multiple_of(m * C, C), C)

    def wide_chunk(m):
        return pl.ds(pl.multiple_of(m * W, W), W)

    def xcopy(k, m):
        return remote(xs.at[k % 2, chunk(m)], xr.at[k % 2, chunk(m)], es.at[k % 2, m], er.at[k % 2, m], sib)

    def xsend(k, m, value):
        xs[k % 2, chunk(m)] = value.astype(b16)
        xcopy(k, m).start()

    def xget(k, m):
        xcopy(k, m).wait()
        return xs[k % 2, chunk(m)].astype(f32) + xr[k % 2, chunk(m)].astype(f32)

    def xsend_wide(k, m, value):
        xsend(k, 2 * m, value[0:C])
        xsend(k, 2 * m + 1, value[C:W])

    def project(l, m):
        tok = wide_chunk(m)
        for half in range(2):
            got = dot(w[half, 0 : 3 * A], hb[l, tok], NT)
            base = half * 3 * A
            bq = jnp.concatenate([bcol[half, 0:A]] * (W // 128), axis=1)
            bv = jnp.concatenate([bcol[half, A : 2 * A]] * (W // 128), axis=1)
            qkv[l, base : base + A, tok] = ((got[0:A] + bq).astype(b16) * b16(HEAD**-0.5)).astype(b16)
            qkv[l, base + A : base + 2 * A, tok] = got[A : 2 * A].astype(b16)
            qkv[l, base + 2 * A : base + 3 * A, tok] = (got[2 * A : 3 * A] + bv).astype(b16)

    def head_rows(h, part):
        base = (h // NHH) * (3 * A) + part * A + (h % NHH) * HEAD
        return pl.ds(pl.multiple_of(base, HEAD), HEAD)

    def attend(l, h):
        counted = lax.broadcasted_iota(jnp.int32, (T, T), 0) < length
        scores = dot(qkv[l, head_rows(h, 1)], qkv[l, head_rows(h, 0)], TN)
        scores = jnp.where(counted, scores, NEG)
        top = jnp.max(scores, axis=0, keepdims=True)
        e = jnp.exp(scores - top)
        one = 1.0 / jnp.sum(e, axis=0, keepdims=True)
        eb = e.astype(b16)
        ex[l, h] = eb
        inv[l, h] = one
        got = dot(qkv[l, head_rows(h, 2)], eb, NN) * one
        ctx[l, pl.ds(pl.multiple_of(h * HEAD, HEAD), HEAD)] = got.astype(b16)

    def attend_range(l, lo, hi):
        loop(lo, hi, lambda h: attend(l, h))

    def attn_out(l, k):
        def step(m):
            tok = wide_chunk(m)
            part = dot(ctx[l, 0:A, tok], w[0, 3 * A : 4 * A], TN)
            part += dot(ctx[l, A : 2 * A, tok], w[1, 3 * A : 4 * A], TN)
            xsend_wide(k, m, part)

        loop(0, NW, step)

    def zrows(z_at, m):
        return pl.ds(pl.multiple_of(z_at * T + m * C, C), C)

    def norm(resid, gain, shift, z_at, m):
        rows = chunk(m)
        centre = resid - jnp.mean(resid, axis=-1, keepdims=True)
        rstd = lax.rsqrt(jnp.mean(centre * centre, axis=-1, keepdims=True) + NORM_EPS)
        scaled = centre * rstd
        zs[zrows(z_at, m)] = scaled.astype(b16)
        rs[rows, z_at : z_at + 1] = rstd
        return scaled * gain + shift

    def norm_one(l, k, m):
        rows = chunk(m)
        before = hb[0, rows].astype(f32) if l == 0 else X[rows]
        first = norm(xget(k, m) + b_out + before, gain1, shift1, 2 * l, m)
        Y[rows] = first
        yb[l, rows] = first.astype(b16)

    def up_chunk(l, m):
        rows = wide_chunk(m)
        for half, source in enumerate((bu, bur)):
            cols = pl.ds(half * D, D)
            pre = dot(yb[l, rows], w[half, UP : UP + D], NN) + source[...].reshape(1, D)
            square = pre * pre
            more = 0.5 + 0.5 * jnp.tanh(pre * (GELU_C + (GELU_C * GELU_A) * square))
            value = pre * more
            act[l, rows, cols] = value.astype(b16)
            slope = more + value * (1.0 - more) * (2.0 * GELU_C + (6.0 * GELU_C * GELU_A) * square)
            gp[l, rows, cols] = slope.astype(b16)

    def down_chunk(l, k, m):
        rows = wide_chunk(m)
        part = dot(act[l, rows, 0:D], w[0, DN : DN + D], NN)
        part += dot(act[l, rows, D : 2 * D], w[1, DN : DN + D], NN)
        xsend_wide(k, m, part)

    def norm_two(l, k, m):
        rows = chunk(m)
        result = norm(xget(k, m) + b_down + Y[rows], gain2, shift2, 2 * l + 1, m)
        X[rows] = result
        if l == 0:
            hb[1, rows] = result.astype(b16)

    pass_on(2)
    pump(3)
    have(0, 3)
    pump(4)
    pass_on(3)
    loop(0, NW, lambda m: project(0, m))
    done = 5
    for h in range(HEADS):
        if h % 2 == 0 and done < LATE:
            pump(done)
            pass_on(done - 1)
            done += 1
        attend(0, h)
    while done < LATE:
        pump(done)
        pass_on(done - 1)
        done += 1
    have(3, 4)
    attn_out(0, 0)
    pass_on(LATE - 1)
    pump(LATE)
    loop(0, NCH, lambda m: norm_one(0, 0, m))
    pump(LATE + 1)
    have(4, LATE)
    for m in range(NW):
        up_chunk(0, m)
        pump(LATE + 2 + m)
    og_rows = pl.ds(t * B, B)
    og_mine, og_other = G.at[pl.ds(y * B, B)], G.at[pl.ds((1 - y) * B, B)]
    og_keep = pltpu.make_async_copy(og_mine, dattn.at[0, og_rows], lsem.at[0])
    og_sib = remote(og_mine, dattn.at[0, og_rows], fs.at[4], fr.at[4], sib)
    og_par = remote(og_other, dattn.at[0, og_rows], fs.at[5], fr.at[5], par)
    og_keep.start()
    og_par.start()
    og_sib.start()
    have(LATE, WST)
    loop(0, NW, lambda m: down_chunk(0, 1, m))

    def next_layer(m):
        norm_two(0, 1, 2 * m)
        norm_two(0, 1, 2 * m + 1)
        project(1, m)

    loop(0, NW, next_layer)

    attend_range(1, 0, HEADS)
    og_par.wait_recv()
    og_fwd = remote(dattn.at[0, rows_t2], dattn.at[0, rows_t2], fs.at[6], fr.at[6], sib)
    og_fwd.start()
    attn_out(1, 2)

    def feed_forward(m):
        norm_one(1, 2, 2 * m)
        norm_one(1, 2, 2 * m + 1)
        up_chunk(1, m)
        down_chunk(1, 3, m)

    loop(0, NW, feed_forward)
    loop(0, NCH, lambda m: norm_two(1, 3, m))
    out_keep = pltpu.make_async_copy(X.at[pl.ds(t * B, B)], out.at[y], lsem.at[1])
    out_par = remote(X.at[pl.ds(t2 * B, B)], out.at[y], fs.at[7], fr.at[7], par)
    out_keep.start()
    out_par.start()
    og_keep.wait()
    for i in range(WST):
        wy(i).wait_send()
        wx(i).wait_send()
        wz(i).wait_send()
        if i >= LATE:
            wd(i).wait_send()
        else:
            wf(i).wait_send()
    og_sib.wait_recv()
    og_fwd.wait_recv()

    def norm_two_back(l, m):
        rows = chunk(m)
        dout = dattn[0, rows].astype(f32) if l == 1 else X[rows]
        scaled = zs[zrows(2 * l + 1, m)].astype(f32)
        dr = rms_back(dout, scaled, rs[rows, 2 * l + 1 : 2 * l + 2], gain2)
        acc[3:4] += col_sum(dr)
        acc[4:5] += col_sum(dout * scaled)
        acc[5:6] += col_sum(dout)
        Y[rows] = dr
        dffn[l, rows] = dr.astype(b16)

    def ffn_back(l, k, m):
        rows = wide_chunk(m)
        drb = dffn[l, rows]
        part = None
        for half in range(2):
            cols = pl.ds(half * D, D)
            dact = dot(drb, w[half, DN : DN + D], NT)
            dp = (dact * gp[l, rows, cols].astype(f32)).astype(b16)
            dpre[l, rows, cols] = dp
            row = 6 + 8 * half
            acc[row : row + 1] += col_sum(dp.astype(f32))
            got = dot(dp, w[half, UP : UP + D], NT)
            part = got if part is None else part + got
        xsend_wide(k, m, part)

    def attn_out_back(l, k, m):
        rows = chunk(m)
        dfirst = Y[rows] + xget(k, m)
        scaled = zs[zrows(2 * l, m)].astype(f32)
        dr = rms_back(dfirst, scaled, rs[rows, 2 * l : 2 * l + 1], gain1)
        acc[0:1] += col_sum(dr)
        acc[1:2] += col_sum(dfirst * scaled)
        acc[2:3] += col_sum(dfirst)
        Y[rows] = dr
        drb = dr.astype(b16)
        dattn[l, rows] = drb

    def context_back(l):
        for half in range(2):
            got = dot(w[half, 3 * A : 4 * A], dattn[l], NT)
            for j in range(NHH):
                h = half * NHH + j
                scaled_rows = got[j * HEAD : (j + 1) * HEAD] * inv[l, h]
                dct[h * HEAD : (h + 1) * HEAD] = scaled_rows.astype(b16)

    def attend_back(l, h):
        mine = pl.ds(pl.multiple_of(h * HEAD, HEAD), HEAD)
        dc = dct[mine]
        dprobs = dot(qkv[l, head_rows(h, 2)], dc, TN)
        eb = ex[l, h]
        ef = eb.astype(f32)
        inner = col_sum(ef * dprobs) * inv[l, h]
        ds = (ef * (dprobs - inner)).astype(b16)
        dqkv[l, head_rows(h, 2)] = dot(dc, eb, NT).astype(b16)
        dqkv[l, head_rows(h, 0)] = (dot(qkv[l, head_rows(h, 1)], ds, NN) * (HEAD**-0.5)).astype(b16)
        dqkv[l, head_rows(h, 1)] = dot(qkv[l, head_rows(h, 0)], ds, NT).astype(b16)

    def attend_back_range(l, lo, hi):
        loop(lo, hi, lambda h: attend_back(l, h))

    def project_back(l, k):
        def step(m):
            tok = wide_chunk(m)
            part = dot(dqkv[l, 0 : 3 * A, tok], w[0, 0 : 3 * A], TN)
            part += dot(dqkv[l, 3 * A : 6 * A, tok], w[1, 0 : 3 * A], TN)
            xsend_wide(k, m, part)

        loop(0, NW, step)
        ones = jnp.ones((8, T), b16)
        for half in range(2):
            sums = dot(ones, dqkv[l, half * 3 * A : (half + 1) * 3 * A], NT)
            row = 7 + 8 * half
            acc[row : row + 1, 0 : 3 * A] += sums[0:1]


    def second_layer_back(m):
        norm_two_back(1, 2 * m)
        norm_two_back(1, 2 * m + 1)
        ffn_back(1, 4, m)

    loop(0, NW, second_layer_back)
    loop(0, NCH, lambda m: attn_out_back(1, 4, m))
    context_back(1)
    attend_back_range(1, 0, HEADS)
    for copy in (og_sib, og_par, og_fwd):
        copy.wait_send()
    out_keep.wait()
    out_par.wait_send()
    project_back(1, 5)

    def first_layer_back(m):
        for i in (2 * m, 2 * m + 1):
            rows = chunk(i)
            X[rows] = Y[rows] + xget(5, i)
            norm_two_back(0, i)
        ffn_back(0, 6, m)

    loop(0, NW, first_layer_back)

    def both(ref, cols=slice(None)):
        value = ref[:, :, cols]
        return value.reshape(2 * value.shape[1], value.shape[2])

    FREE = T - 4 * A

    def grad_down(half, dst, off=0, ready=None):
        dy = both(dffn)
        for i in reversed(range(D // 256)):
            left = both(act, slice(half * D + i * 256, half * D + (i + 1) * 256))
            dst[off + DN + i * 256 : off + DN + (i + 1) * 256] = dot(left, dy, TN).astype(b16)
            if ready is not None:
                ready((D // 256 - i) * 256 // R)

    def grad_up(half, dst, off=0):
        dy = both(dpre, slice(half * D, (half + 1) * D))
        for i in reversed(range(D // 256)):
            left = both(yb, slice(i * 256, (i + 1) * 256))
            dst[off + UP + i * 256 : off + UP + (i + 1) * 256] = dot(left, dy, TN).astype(b16)

    def grad_attn(half, dst):
        rows = slice(half * A, (half + 1) * A)
        got = dot(ctx[0, rows], dattn[0], NN) + dot(ctx[1, rows], dattn[1], NN)
        dst[3 * A : 4 * A] = got.astype(b16)
        rows = slice(half * 3 * A, (half + 1) * 3 * A)
        got = dot(dqkv[0, rows], hb[0], NN) + dot(dqkv[1, rows], hb[1], NN)
        dst[0 : 3 * A] = got.astype(b16)

    def top_of(s):
        return pl.multiple_of(TOT - (s + 1) * R, R)

    def piece(s):
        return pl.ds(top_of(s), R)

    def half_of(s, which):
        return pl.ds(pl.multiple_of(top_of(s) + which * HR, HR), HR)

    def part_of(s, which, p):
        return pl.ds(pl.multiple_of(top_of(s) + which * HR + p * Q, Q), Q)

    def ycopy_ffn(s):
        src = zs.at[pl.ds(pl.multiple_of(top_of(s) + FREE, R), R)]
        return remote(src, yr.at[piece(s)], ys.at[s], yrs.at[s], par)

    def ycopy_attn(s):
        return remote(gs.at[piece(s)], yr.at[piece(s)], ys.at[s], yrs.at[s], par)

    def ycopy(s):
        return remote(yr.at[piece(s)], yr.at[piece(s)], ys.at[s], yrs.at[s], par)

    def gxcopy(s):
        return remote(G.at[half_of(s, 1 - x)], xh.at[s], gxs.at[s], gxr.at[s], xp)

    def zcopy(s, k):
        src = G.at[part_of(s, x, (zlo + k) % NP)]
        return remote(src, zr.at[s, k - 1], zss.at[s, k - 1], zrs.at[s, k - 1], zdev(k))

    def hcopy(s, k):
        src = G.at[part_of(s, x, zlo)]
        return remote(src, hr.at[s % 2, k - 1], hss.at[s, k - 1], hrs.at[s, k - 1], hdev(k))

    def azcopy(s, k):
        rows = part_of(s, x, zlo)
        return remote(F.at[rows], F.at[rows], azs.at[s, k - 1], azr.at[s, k - 1], zdev(k))

    def axcopy(s, k):
        rows = part_of(s, x, (zlo + NP - k) % NP)
        return remote(F.at[rows], F.at[rows], axs.at[s, k], axr.at[s, k], xp)

    ocopies = [
        pltpu.make_async_copy(F.at[pl.ds(lo, rows)], ref, os.at[i])
        for i, (ref, lo, rows) in enumerate(
            (
                (gd_out, DN, D),
                (gu_out, UP, D),
                (go_out, 3 * A, A),
                (gv_out, 2 * A, A),
                (gk_out, A, A),
                (gq_out, 0, A),
            )
        )
    ]

    YLOOK = 3

    def ystart(s):
        if isinstance(s, int):
            if s < NS:
                (ycopy_ffn if s < 2 * D // R else ycopy_attn)(s).start()
            return

        @pl.when(s < 2 * D // R)
        def _():
            ycopy_ffn(s).start()

        @pl.when((s >= 2 * D // R) & (s < NS))
        def _():
            ycopy_attn(s).start()

    def stage_x(s):
        ycopy(s).wait_recv()
        ystart(s + YLOOK)
        for which in (1 - x, x):
            rows = half_of(s, which)
            G[rows] = (G[rows].astype(f32) + yr[rows].astype(f32)).astype(b16)
            if which is not x:
                gxcopy(s).start()

    def stage_z(s):
        gxcopy(s).wait_recv()
        rows = half_of(s, x)
        G[rows] = (G[rows].astype(f32) + xh[s].astype(f32)).astype(b16)
        for k in range(1, NP):
            zcopy(s, k).start()

    def stage_sum(s):
        rows = part_of(s, x, zlo)
        total = G[rows].astype(f32)
        for k in range(1, NP):
            zcopy(s, k).wait_recv()
            total += zr[s, k - 1].astype(f32)
        if NH > 1:
            G[rows] = total.astype(b16)
            for k in range(1, NH):
                hcopy(s, k).start()
            for k in range(1, NH):
                hcopy(s, k).wait()
                total += hr[s % 2, k - 1].astype(f32)
        F[rows] = total.astype(b16)
        for k in range(1, NP):
            azcopy(s, k).start()
        axcopy(s, 0).start()

    def stage_swap(s):
        for k in range(1, NP):
            azcopy(s, k).wait_recv()
            axcopy(s, k).start()

    def stage_out(s):
        for k in range(NP):
            axcopy(s, k).wait_recv()

    def drain(s):
        ycopy(s).wait_send()
        gxcopy(s).wait_send()
        for k in range(1, NP):
            zcopy(s, k).wait_send()
            azcopy(s, k).wait_send()
        for k in range(NP):
            axcopy(s, k).wait_send()

    stages = (stage_x, stage_z, stage_sum, stage_swap, stage_out, drain)

    def run(i):
        for lag, stage in enumerate(stages):
            s = i - lag
            if isinstance(s, int) and not 0 <= s < NS:
                continue
            stage(s)

    begun = []

    def begin(ready):
        while len(begun) < min(ready, YLOOK):
            ystart(len(begun))
            begun.append(0)

    grad_down(1, zs, FREE, begin)
    grad_up(1, zs, FREE)
    grad_down(0, G)
    loop(0, NCH, lambda m: attn_out_back(0, 6, m))
    context_back(0)
    run(0)
    grad_up(0, G)
    attend_back_range(0, 0, HEADS // 2)
    run(1)
    attend_back_range(0, HEADS // 2, HEADS)
    run(2)
    project_back(0, 7)
    grad_attn(1, gs)
    run(3)
    acc[8:14] = acc[0:6]
    sm_y = remote(acc.at[pl.ds(8, 8)], smr.at[0], sms.at[0], smrs.at[0], par)
    sm_y.start()

    def last(m):
        rows = chunk(m)
        X[rows] = Y[rows] + xget(7, m)

    loop(0, NCH, last)
    xs[0, 0:B] = X[pl.ds(t * B, B)].astype(b16)
    xs[0, B : 2 * B] = X[pl.ds(t2 * B, B)].astype(b16)
    gi_keep = pltpu.make_async_copy(xs.at[0, pl.ds(0, B)], gib_out.at[y], lsem.at[2])
    gi_par = remote(xs.at[0, pl.ds(B, B)], gib_out.at[y], fs.at[8], fr.at[8], par)
    gi_keep.start()
    grad_attn(0, G)

    run(4)
    loop(5, D // R + 4, run)
    ocopies[0].start()
    loop(D // R + 4, NS, run)
    gi_par.start()
    for i in range(NS, NS + 2):
        run(i)
    sm_y.wait_recv()
    sm[0] = acc[0:8] + smr[0]
    sm_x = remote(sm.at[0], smr.at[1], sms.at[1], smrs.at[1], xp)
    sm_x.start()
    run(NS + 2)
    sm_x.wait_recv()
    sm[1] = sm[0] + smr[1]
    sm_z = [
        remote(sm.at[1], smr.at[1 + k], sms.at[1 + k], smrs.at[1 + k], zdev(k)) for k in range(1, NP)
    ]
    for copy in sm_z:
        copy.start()
    run(NS + 3)
    for copy in ocopies[1:]:
        copy.start()
    total = sm[1]
    for k, copy in enumerate(sm_z):
        copy.wait_recv()
        total += smr[2 + k]
    sm[2] = total
    if NH > 1:
        sm_h = [
            remote(sm.at[2], smr.at[NP + k], sms.at[NP + k], smrs.at[NP + k], hdev(k))
            for k in range(1, NH)
        ]
        for copy in sm_h:
            copy.start()
        for k, copy in enumerate(sm_h):
            copy.wait()
            total += smr[NP + 1 + k]
    sm_out[...] = total

    for copy in (hid_sib, hid_par, *bias_par, hid_fwd, gi_par, sm_y, sm_x):
        copy.wait_send()
    for copy in sm_z:
        copy.wait_send()
    out_par.wait_recv()
    gi_par.wait_recv()
    gi_keep.wait()
    drain(NS - 1)
    for copy in ocopies:
        copy.wait()


def widen(*refs):
    names = 7
    big, result, small = refs[:names], refs[names], refs[names + 1]
    refs = refs[names + 2 :]
    wide, result_out, vectors = refs[:names], refs[names], refs[names + 1 : names + 10]
    refs = refs[names + 10 :]
    narrow, broad = refs[:names], refs[names : 2 * names]
    through, isem, osem = refs[2 * names :]
    loads = [pltpu.make_async_copy(big[i], narrow[i], isem.at[i]) for i in range(names)]
    stores = [pltpu.make_async_copy(broad[i], wide[i], osem.at[i]) for i in range(names)]
    keep_in = pltpu.make_async_copy(result, through, isem.at[names])
    keep = pltpu.make_async_copy(through, result_out, osem.at[names])
    for copy in loads:
        copy.start()
    keep_in.start()
    for i, ref in enumerate(vectors):
        if i < 7:
            ref[...] = small[i, :]
        else:
            rows = ref.shape[0]
            at = (i - 7) * 2 * rows
            ref[...] = small[7, at : at + rows]
    for load, store, i in zip(loads, stores, range(names)):
        load.wait()
        broad[i][...] = narrow[i][...].astype(f32)
        store.start()
    keep_in.wait()
    keep.start()
    for copy in stores:
        copy.wait()
    keep.wait()


def shards(
    dp,
    hidden_in,
    lengths,
    w_query,
    b_query,
    w_key,
    w_value,
    b_value,
    w_out,
    b_out,
    norm1_gain,
    norm1_shift,
    w_up,
    b_up,
    w_down,
    b_down,
    norm2_gain,
    norm2_shift,
    out_grad,
):
    _, B, D = hidden_in.shape
    A = w_query.shape[1]
    T = 4 * B
    TOT = 4 * A + 2 * D
    R = 128
    HR = R // 2
    nz = dp // 2
    NP = 1
    while nz % (2 * NP) == 0 and HR % (32 * NP) == 0:
        NP *= 2
    NH = nz // NP
    C = T // 4
    NCH = T // C
    NS = TOT // R
    Q = HR // NP
    heads = 2 * A // HEAD
    cfg = dict(T=T, D=D, A=A, B=B, C=C, R=R, NP=NP, NH=NH)
    rows = [
        value if value.shape[0] == D else value.reshape(1, -1)
        for value in (
            b_up,
            b_query,
            b_value,
            b_out,
            norm1_gain,
            norm1_shift,
            b_down,
            norm2_gain,
            norm2_shift,
        )
    ]
    V = functools.partial(pltpu.VMEM)
    DMA = pltpu.SemaphoreType.DMA
    NPx = max(NP - 1, 1)
    NHx = max(NH - 1, 1)
    scratch = [
        V((2, TOT, D), b16),
        V((2, T, D), b16),
        V((2, 6 * A, T), b16),
        V((2, heads, T, T), b16),
        V((2, heads, 1, T), f32),
        V((2, 2 * A, T), b16),
        V((max(4 * T, T + 2 * D), D), b16),
        V((T, 128), f32),
        V((2, T, D), b16),
        V((2, T, 2 * D), b16),
        V((2, T, 2 * D), b16),
        V((T, D), f32),
        V((T, D), f32),
        V((2, T, D), b16),
        V((2, T, 2 * D), b16),
        V((2, T, D), b16),
        V((2, 6 * A, T), b16),
        V((2 * A, T), b16),
        V((2, T, D), b16),
        V((2, T, D), b16),
        V((D,), f32),
        V((1, A), f32),
        V((1, A), f32),
        V((2, 2 * A, 128), f32),
        V((16, D), f32),
        V((3, 8, D), f32),
        V((NP + NH, 8, D), f32),
        V((TOT, D), b16),
        V((4 * A, D), b16),
        V((TOT, D), b16),
        V((NS, HR, D), b16),
        V((NS, NPx, Q, D), b16),
        V((2, NHx, Q, D), b16),
        V((TOT, D), b16),
        DMA((9,)),
        DMA((12,)),
        DMA((12,)),
        DMA((TOT // A,)),
        DMA((TOT // A,)),
        DMA((TOT // A,)),
        DMA((TOT // A,)),
        DMA((TOT // A,)),
        DMA((TOT // A,)),
        DMA((TOT // A,)),
        DMA((TOT // A,)),
        DMA((TOT // A,)),
        DMA((TOT // A,)),
        DMA((2, NCH)),
        DMA((2, NCH)),
        DMA((NS,)),
        DMA((NS,)),
        DMA((NS,)),
        DMA((NS,)),
        DMA((NS, NPx)),
        DMA((NS, NPx)),
        DMA((NS, NHx)),
        DMA((NS, NHx)),
        DMA((NS, NPx)),
        DMA((NS, NPx)),
        DMA((NS, NP)),
        DMA((NS, NP)),
        DMA((6,)),
        DMA((NP + NH,)),
        DMA((NP + NH,)),
    ]
    anywhere = pl.BlockSpec(memory_space=pl.ANY)
    vmem = pl.BlockSpec(memory_space=pltpu.VMEM)
    smem = pl.BlockSpec(memory_space=pltpu.SMEM)
    result, gib, gq, gk, gv, go, gu, gd, small = pl.pallas_call(
        functools.partial(whole_step, cfg),
        out_shape=(
            jax.ShapeDtypeStruct((2, B, D), f32),
            jax.ShapeDtypeStruct((2, B, D), b16),
            jax.ShapeDtypeStruct((A, D), b16),
            jax.ShapeDtypeStruct((A, D), b16),
            jax.ShapeDtypeStruct((A, D), b16),
            jax.ShapeDtypeStruct((A, D), b16),
            jax.ShapeDtypeStruct((D, D), b16),
            jax.ShapeDtypeStruct((D, D), b16),
            jax.ShapeDtypeStruct((8, D), f32),
        ),
        in_specs=[smem] + [anywhere] * 8 + [vmem] * 9,
        out_specs=(anywhere,) * 8 + (vmem,),
        scratch_shapes=scratch,
        compiler_params=pltpu.CompilerParams(
            collective_id=0, has_side_effects=True, vmem_limit_bytes=64 * 2**20
        ),
    )(
        lengths,
        hidden_in,
        out_grad,
        w_query.T,
        w_key.T,
        w_value.T,
        w_out,
        w_up,
        w_down,
        *rows,
    )
    bigs = (gd, gu, go, gq, gk, gv, gib)
    gd, gu, go, gq, gk, gv, gi, result, *vectors = pl.pallas_call(
        widen,
        out_shape=tuple(jax.ShapeDtypeStruct(v.shape, f32) for v in bigs + (result,))
        + (jax.ShapeDtypeStruct((D,), f32),) * 7
        + (jax.ShapeDtypeStruct((A,), f32),) * 2,
        in_specs=[anywhere] * 8 + [vmem],
        out_specs=(anywhere,) * 8 + (vmem,) * 9,
        scratch_shapes=[V(v.shape, b16) for v in bigs]
        + [V(v.shape, f32) for v in bigs]
        + [V(result.shape, f32), DMA((8,)), DMA((8,))],
        compiler_params=pltpu.CompilerParams(vmem_limit_bytes=64 * 2**20),
    )(*bigs, result, small)
    db_out, dgain1, dshift1, db_down, dgain2, dshift2, db_up, db_query, db_value = vectors
    return (
        result,
        gi,
        gq.T,
        db_query,
        gk.T,
        gv.T,
        db_value,
        go,
        db_out,
        dgain1,
        dshift1,
        gu,
        db_up,
        gd,
        db_down,
        dgain2,
        dshift2,
    )


def solution(mesh):
    placed = (
        P("dp", "tensor", None),
        P("dp"),
        P(None, "tensor"),
        P("tensor"),
        P(None, "tensor"),
        P(None, "tensor"),
        P("tensor"),
        P("tensor", None),
        P(),
        P(),
        P(),
        P(None, "tensor"),
        P("tensor"),
        P("tensor", None),
        P(),
        P(),
        P(),
        P("dp", "tensor", None),
    )
    return jax.shard_map(
        functools.partial(shards, mesh.shape["dp"]),
        mesh=mesh,
        in_specs=placed,
        out_specs=(
            P("dp", "tensor", None),
            P("dp", "tensor", None),
            P(None, "tensor"),
            P("tensor"),
            P(None, "tensor"),
            P(None, "tensor"),
            P("tensor"),
            P("tensor", None),
            P(),
            P(),
            P(),
            P(None, "tensor"),
            P("tensor"),
            P("tensor", None),
            P(),
            P(),
            P(),
        ),
        check_vma=False,
    )
```

```python
import functools

import jax
import jax.numpy as jnp
from jax import lax
from jax.experimental import pallas as pl
from jax.experimental.pallas import tpu as pltpu
from jax.sharding import PartitionSpec as P

HEAD = 64
NORM_EPS = 1e-12
NEG = -1000000000.0
GELU_C = 0.7978845608
GELU_A = 0.044715

NN = (((1,), (0,)), ((), ()))
NT = (((1,), (1,)), ((), ()))
TN = (((0,), (0,)), ((), ()))

b16 = jnp.bfloat16
f32 = jnp.float32


def dot(left, right, dims):
    return lax.dot_general(left, right, dims, preferred_element_type=f32)


def rms_back(dout, scaled, rstd, gain):
    dscaled = dout * gain
    return rstd * (
        dscaled
        - jnp.mean(dscaled, axis=-1, keepdims=True)
        - scaled * jnp.mean(dscaled * scaled, axis=-1, keepdims=True)
    )


def col_sum(value):
    return jnp.sum(value, axis=0, keepdims=True)


def whole_step(
    cfg,
    len_ref,
    hid,
    og,
    wq,
    wk,
    wv,
    wo,
    wu,
    wd,
    bu,
    bq,
    bv,
    b_out,
    gain1,
    shift1,
    b_down,
    gain2,
    shift2,
    out,
    gib_out,
    gq_out,
    gk_out,
    gv_out,
    go_out,
    gu_out,
    gd_out,
    sm_out,
    w,
    hb,
    qkv,
    ex,
    inv,
    ctx,
    zs,
    rs,
    yb,
    act,
    gp,
    X,
    Y,
    dffn,
    dpre,
    dattn,
    dqkv,
    dct,
    xs,
    xr,
    bur,
    bqr,
    bvr,
    bcol,
    acc,
    sm,
    smr,
    G,
    gs,
    yr,
    xh,
    zr,
    hr,
    F,
    lsem,
    fs,
    fr,
    wys,
    wyr,
    wxs,
    wxr,
    wzs,
    wzr,
    wfs,
    wfr,
    wds,
    wdr,
    es,
    er,
    ys,
    yrs,
    gxs,
    gxr,
    zss,
    zrs,
    hss,
    hrs,
    azs,
    azr,
    axs,
    axr,
    os,
    sms,
    smrs,
):
    T, D, A, B, C, R, NP, NH = (
        cfg["T"],
        cfg["D"],
        cfg["A"],
        cfg["B"],
        cfg["C"],
        cfg["R"],
        cfg["NP"],
        cfg["NH"],
    )
    NCH = T // C
    W = 2 * C
    NW = T // W
    TOT = 4 * A + 2 * D
    CS = cfg["CS"]
    CW = D // CS
    NS = CS * TOT // R
    HR = R // 2
    Q = HR // NP
    NHH = A // HEAD
    HEADS = 2 * NHH
    MESH = pl.DeviceIdType.MESH
    UP, DN = 4 * A, 4 * A + D

    d = lax.axis_index("dp")
    t = lax.axis_index("tensor")
    y = t // 2
    c = t % 2
    x = d % 2
    z = d // 2
    zlo = z % NP
    zhi = z // NP
    t2 = (t + 2) % 4
    sib = (d, t + 1 - 2 * c)
    par = (d, t2)
    xp = (d + 1 - 2 * x, t)

    def zdev(k):
        return ((zhi * NP + (zlo + k) % NP) * 2 + x, t)

    def hdev(k):
        return ((((zhi + k) % NH) * NP + zlo) * 2 + x, t)

    def remote(src, dst, send, recv, dev):
        return pltpu.make_async_remote_copy(
            src_ref=src,
            dst_ref=dst,
            send_sem=send,
            recv_sem=recv,
            device_id=dev,
            device_id_type=MESH,
        )

    local = [
        pltpu.make_async_copy(hid.at[y], hb.at[0, pl.ds(t * B, B)], lsem.at[0]),
        pltpu.make_async_copy(wo, w.at[0, pl.ds(3 * A, A)], lsem.at[1]),
        pltpu.make_async_copy(wu, w.at[0, pl.ds(UP, D)], lsem.at[2]),
        pltpu.make_async_copy(wd, w.at[0, pl.ds(DN, D)], lsem.at[3]),
        pltpu.make_async_copy(og.at[0], Y.at[pl.ds(0, B)], lsem.at[4]),
        pltpu.make_async_copy(og.at[1], Y.at[pl.ds(B, B)], lsem.at[5]),
        pltpu.make_async_copy(wq, w.at[0, pl.ds(0, A)], lsem.at[6]),
        pltpu.make_async_copy(wk, w.at[0, pl.ds(A, A)], lsem.at[7]),
        pltpu.make_async_copy(wv, w.at[0, pl.ds(2 * A, A)], lsem.at[8]),
    ]
    for copy in local:
        copy.start()

    barrier = pltpu.get_barrier_semaphore()
    friends = [sib, par, xp] + [zdev(k) for k in range(1, NP)] + [hdev(k) for k in range(1, NH)]
    for dev in friends:
        pl.semaphore_signal(barrier, inc=1, device_id=dev, device_id_type=MESH)
    pl.semaphore_wait(barrier, len(friends))

    hid_sib = remote(hid.at[y], hb.at[0, pl.ds(t * B, B)], fs.at[0], fr.at[0], sib)
    hid_par = remote(hid.at[1 - y], hb.at[0, pl.ds(t * B, B)], fs.at[1], fr.at[1], par)
    bias_par = [
        remote(mine, theirs, fs.at[9 + i], fr.at[9 + i], par)
        for i, (mine, theirs) in enumerate(((bu, bur), (bq, bqr), (bv, bvr)))
    ]
    hid_sib.start()

    acc[...] = jnp.zeros_like(acc)

    WST = TOT // A
    WCH = A // 4
    zb = z % 2
    zp = ((z + 1 - 2 * zb) * 2 + x, t)

    def wrows(i, qx, qz):
        return pl.ds(pl.multiple_of(i * A + (2 * qx + qz) * WCH, WCH), WCH)

    def wy(i):
        rows = wrows(i, x, zb)
        return remote(w.at[0, rows], w.at[1, rows], wys.at[i], wyr.at[i], par)

    def wx(i):
        rows = wrows(i, x, zb)
        return remote(w.at[1, rows], w.at[1, rows], wxs.at[i], wxr.at[i], xp)

    def wz(i):
        rows = wrows(i, x, zb)
        return remote(w.at[1, rows], w.at[1, rows], wzs.at[i], wzr.at[i], zp)

    def wf(i):
        rows = wrows(i, 1 - x, zb) if i % 2 == 0 else wrows(i, x, 1 - zb)
        return remote(w.at[1, rows], w.at[1, rows], wfs.at[i], wfr.at[i], zp if i % 2 == 0 else xp)

    LATE = WST - D // A

    def wd(i):
        rows = wrows(i, 1 - x, 1 - zb)
        return remote(w.at[0, rows], w.at[1, rows], wds.at[i], wdr.at[i], par)

    LOOK = 4

    def send_quarters(i):
        if i < WST:
            wy(i).start()
            if i >= LATE:
                wd(i).start()

    def pump(i):
        wy(i).wait_recv()
        wx(i).start()
        wz(i).start()
        send_quarters(i + LOOK)

    def pass_on(i):
        (wx if i % 2 == 0 else wz)(i).wait_recv()
        wf(i).start()

    def have(lo, hi):
        for i in range(lo, hi):
            if i >= LATE:
                wx(i).wait_recv()
                wz(i).wait_recv()
                wd(i).wait_recv()
                continue
            (wz if i % 2 == 0 else wx)(i).wait_recv()
            wf(i).wait_recv()

    for copy in local[6:]:
        copy.wait()
    for i in range(3):
        wy(i).start()
    hid_par.start()
    for copy in bias_par:
        copy.start()
    for copy in local[:6]:
        copy.wait()
    wy(3).start()
    G[0 : 2 * B] = Y[0 : 2 * B].astype(b16)

    pump(0)
    pump(1)
    pass_on(0)
    pump(2)
    pass_on(1)
    hid_par.wait_recv()
    rows_t2 = pl.ds(t2 * B, B)
    hid_fwd = remote(hb.at[0, rows_t2], hb.at[0, rows_t2], fs.at[3], fr.at[3], sib)
    hid_fwd.start()
    for copy in bias_par:
        copy.wait_recv()
    for half, sources in enumerate(((bq, bv), (bqr, bvr))):
        for i, source in enumerate(sources):
            bcol[half, i * A : (i + 1) * A] = jnp.transpose(jnp.broadcast_to(source[...], (128, A)))
    hid_sib.wait_recv()
    hid_fwd.wait_recv()

    b_out, gain1, shift1, b_down, gain2, shift2 = (
        ref[...].reshape(1, D) for ref in (b_out, gain1, shift1, b_down, gain2, shift2)
    )
    length = len_ref[y]

    def loop(lo, hi, f):
        if isinstance(lo, int) and isinstance(hi, int) and hi - lo <= 4:
            for i in range(lo, hi):
                f(i)
            return

        def step(i, carry):
            f(i)
            return carry

        lax.fori_loop(lo, hi, step, 0)

    def chunk(m):
        return pl.ds(m * C if isinstance(m, int) else pl.multiple_of(m * C, C), C)

    def wide_chunk(m):
        return pl.ds(m * W if isinstance(m, int) else pl.multiple_of(m * W, W), W)

    def xcopy(k, m):
        return remote(xs.at[k % 2, chunk(m)], xr.at[k % 2, chunk(m)], es.at[k % 2, m], er.at[k % 2, m], sib)

    def xsend(k, m, value):
        xs[k % 2, chunk(m)] = value.astype(b16)
        xcopy(k, m).start()

    def xget(k, m):
        xcopy(k, m).wait()
        return xs[k % 2, chunk(m)].astype(f32) + xr[k % 2, chunk(m)].astype(f32)

    def xsend_wide(k, m, value):
        xsend(k, 2 * m, value[0:C])
        xsend(k, 2 * m + 1, value[C:W])

    def project(l, m):
        tok = wide_chunk(m)
        for half in range(2):
            got = dot(w[half, 0 : 3 * A], hb[l, tok], NT)
            base = half * 3 * A
            bq = jnp.concatenate([bcol[half, 0:A]] * (W // 128), axis=1)
            bv = jnp.concatenate([bcol[half, A : 2 * A]] * (W // 128), axis=1)
            qkv[l, base : base + A, tok] = ((got[0:A] + bq).astype(b16) * b16(HEAD**-0.5)).astype(b16)
            qkv[l, base + A : base + 2 * A, tok] = got[A : 2 * A].astype(b16)
            qkv[l, base + 2 * A : base + 3 * A, tok] = (got[2 * A : 3 * A] + bv).astype(b16)

    def head_rows(h, part):
        base = (h // NHH) * (3 * A) + part * A + (h % NHH) * HEAD
        return pl.ds(base, HEAD)

    def attend(l, h):
        counted = lax.broadcasted_iota(jnp.int32, (T, T), 0) < length
        scores = dot(qkv[l, head_rows(h, 1)], qkv[l, head_rows(h, 0)], TN)
        scores = jnp.where(counted, scores, NEG)
        top = jnp.max(scores, axis=0, keepdims=True)
        e = jnp.exp(scores - top)
        one = 1.0 / jnp.sum(e, axis=0, keepdims=True)
        eb = e.astype(b16)
        ex[l, h] = eb
        inv[l, h] = one
        got = dot(qkv[l, head_rows(h, 2)], eb, NN) * one
        ctx[l, pl.ds(h * HEAD, HEAD)] = got.astype(b16)

    def attend_range(l, lo, hi):
        for h in range(lo, hi):
            attend(l, h)

    def attn_out(l, k):
        def step(m):
            tok = wide_chunk(m)
            part = dot(ctx[l, 0:A, tok], w[0, 3 * A : 4 * A], TN)
            part += dot(ctx[l, A : 2 * A, tok], w[1, 3 * A : 4 * A], TN)
            xsend_wide(k, m, part)

        loop(0, NW, step)

    def zrows(z_at, m):
        return pl.ds(z_at * T + m * C if isinstance(m, int) else pl.multiple_of(z_at * T + m * C, C), C)

    def norm(resid, gain, shift, z_at, m):
        rows = chunk(m)
        centre = resid - jnp.mean(resid, axis=-1, keepdims=True)
        rstd = lax.rsqrt(jnp.mean(centre * centre, axis=-1, keepdims=True) + NORM_EPS)
        scaled = centre * rstd
        zs[zrows(z_at, m)] = scaled.astype(b16)
        rs[rows, z_at : z_at + 1] = rstd
        return scaled * gain + shift

    def norm_one(l, k, m):
        rows = chunk(m)
        before = hb[0, rows].astype(f32) if l == 0 else X[rows]
        first = norm(xget(k, m) + b_out + before, gain1, shift1, 2 * l, m)
        Y[rows] = first
        yb[l, rows] = first.astype(b16)

    def up_chunk(l, m):
        rows = wide_chunk(m)
        for half, source in enumerate((bu, bur)):
            cols = pl.ds(half * D, D)
            pre = dot(yb[l, rows], w[half, UP : UP + D], NN) + source[...].reshape(1, D)
            square = pre * pre
            more = 0.5 + 0.5 * jnp.tanh(pre * (GELU_C + (GELU_C * GELU_A) * square))
            value = pre * more
            act[l, rows, cols] = value.astype(b16)
            slope = more + value * (1.0 - more) * (2.0 * GELU_C + (6.0 * GELU_C * GELU_A) * square)
            gp[l, rows, cols] = slope.astype(b16)

    def down_chunk(l, k, m):
        rows = wide_chunk(m)
        part = dot(act[l, rows, 0:D], w[0, DN : DN + D], NN)
        part += dot(act[l, rows, D : 2 * D], w[1, DN : DN + D], NN)
        xsend_wide(k, m, part)

    def norm_two(l, k, m):
        rows = chunk(m)
        result = norm(xget(k, m) + b_down + Y[rows], gain2, shift2, 2 * l + 1, m)
        X[rows] = result
        if l == 0:
            hb[1, rows] = result.astype(b16)

    pass_on(2)
    pump(3)
    have(0, 3)
    pump(4)
    pass_on(3)
    loop(0, NW, lambda m: project(0, m))
    done = 5
    for h in range(HEADS):
        if h % 2 == 0 and done < LATE:
            pump(done)
            pass_on(done - 1)
            done += 1
        attend(0, h)
    while done < LATE:
        pump(done)
        pass_on(done - 1)
        done += 1
    have(3, 4)
    attn_out(0, 0)
    pass_on(LATE - 1)
    pump(LATE)
    loop(0, NCH, lambda m: norm_one(0, 0, m))
    pump(LATE + 1)
    have(4, LATE)
    for m in range(NW):
        up_chunk(0, m)
        pump(LATE + 2 + m)
    og_rows = pl.ds(t * B, B)
    og_mine, og_other = G.at[pl.ds(y * B, B)], G.at[pl.ds((1 - y) * B, B)]
    og_keep = pltpu.make_async_copy(og_mine, dattn.at[0, og_rows], lsem.at[0])
    og_sib = remote(og_mine, dattn.at[0, og_rows], fs.at[4], fr.at[4], sib)
    og_par = remote(og_other, dattn.at[0, og_rows], fs.at[5], fr.at[5], par)
    og_keep.start()
    og_par.start()
    og_sib.start()
    have(LATE, WST)
    loop(0, NW, lambda m: down_chunk(0, 1, m))

    def next_layer(m):
        norm_two(0, 1, 2 * m)
        norm_two(0, 1, 2 * m + 1)
        project(1, m)

    loop(0, NW, next_layer)

    attend_range(1, 0, HEADS)
    og_par.wait_recv()
    og_fwd = remote(dattn.at[0, rows_t2], dattn.at[0, rows_t2], fs.at[6], fr.at[6], sib)
    og_fwd.start()
    attn_out(1, 2)

    def feed_forward(m):
        norm_one(1, 2, 2 * m)
        norm_one(1, 2, 2 * m + 1)
        up_chunk(1, m)
        down_chunk(1, 3, m)

    loop(0, NW, feed_forward)
    loop(0, NCH, lambda m: norm_two(1, 3, m))
    out_keep = pltpu.make_async_copy(X.at[pl.ds(t * B, B)], out.at[y], lsem.at[1])
    out_par = remote(X.at[pl.ds(t2 * B, B)], out.at[y], fs.at[7], fr.at[7], par)
    out_keep.start()
    out_par.start()
    og_keep.wait()
    for i in range(WST):
        wy(i).wait_send()
        wx(i).wait_send()
        wz(i).wait_send()
        if i >= LATE:
            wd(i).wait_send()
        else:
            wf(i).wait_send()
    og_sib.wait_recv()
    og_fwd.wait_recv()

    def norm_two_back(l, m):
        rows = chunk(m)
        dout = dattn[0, rows].astype(f32) if l == 1 else X[rows]
        scaled = zs[zrows(2 * l + 1, m)].astype(f32)
        dr = rms_back(dout, scaled, rs[rows, 2 * l + 1 : 2 * l + 2], gain2)
        acc[3:4] += col_sum(dr)
        acc[4:5] += col_sum(dout * scaled)
        acc[5:6] += col_sum(dout)
        Y[rows] = dr
        dffn[l, rows] = dr.astype(b16)

    def ffn_back(l, k, m):
        rows = wide_chunk(m)
        drb = dffn[l, rows]
        part = None
        for half in range(2):
            cols = pl.ds(half * D, D)
            dact = dot(drb, w[half, DN : DN + D], NT)
            dp = (dact * gp[l, rows, cols].astype(f32)).astype(b16)
            dpre[l, rows, cols] = dp
            row = 6 + 8 * half
            acc[row : row + 1] += col_sum(dp.astype(f32))
            got = dot(dp, w[half, UP : UP + D], NT)
            part = got if part is None else part + got
        xsend_wide(k, m, part)

    def attn_out_back(l, k, m):
        rows = chunk(m)
        dfirst = Y[rows] + xget(k, m)
        scaled = zs[zrows(2 * l, m)].astype(f32)
        dr = rms_back(dfirst, scaled, rs[rows, 2 * l : 2 * l + 1], gain1)
        acc[0:1] += col_sum(dr)
        acc[1:2] += col_sum(dfirst * scaled)
        acc[2:3] += col_sum(dfirst)
        Y[rows] = dr
        drb = dr.astype(b16)
        dattn[l, rows] = drb

    def context_back(l):
        for half in range(2):
            got = dot(w[half, 3 * A : 4 * A], dattn[l], NT)
            for j in range(NHH):
                h = half * NHH + j
                scaled_rows = got[j * HEAD : (j + 1) * HEAD] * inv[l, h]
                dct[h * HEAD : (h + 1) * HEAD] = scaled_rows.astype(b16)

    def attend_back(l, h):
        mine = pl.ds(h * HEAD, HEAD)
        dc = dct[mine]
        dprobs = dot(qkv[l, head_rows(h, 2)], dc, TN)
        eb = ex[l, h]
        ef = eb.astype(f32)
        inner = col_sum(ef * dprobs) * inv[l, h]
        ds = (ef * (dprobs - inner)).astype(b16)
        dqkv[l, head_rows(h, 2)] = dot(dc, eb, NT).astype(b16)
        dqkv[l, head_rows(h, 0)] = (dot(qkv[l, head_rows(h, 1)], ds, NN) * (HEAD**-0.5)).astype(b16)
        dqkv[l, head_rows(h, 1)] = dot(qkv[l, head_rows(h, 0)], ds, NT).astype(b16)

    def attend_back_range(l, lo, hi):
        for h in range(lo, hi):
            attend_back(l, h)

    def project_back(l, k):
        def step(m):
            tok = wide_chunk(m)
            part = dot(dqkv[l, 0 : 3 * A, tok], w[0, 0 : 3 * A], TN)
            part += dot(dqkv[l, 3 * A : 6 * A, tok], w[1, 0 : 3 * A], TN)
            xsend_wide(k, m, part)

        loop(0, NW, step)
        ones = jnp.ones((8, T), b16)
        for half in range(2):
            sums = dot(ones, dqkv[l, half * 3 * A : (half + 1) * 3 * A], NT)
            row = 7 + 8 * half
            acc[row : row + 1, 0 : 3 * A] += sums[0:1]


    def second_layer_back(m):
        norm_two_back(1, 2 * m)
        norm_two_back(1, 2 * m + 1)
        ffn_back(1, 4, m)

    loop(0, NW, second_layer_back)
    loop(0, NCH, lambda m: attn_out_back(1, 4, m))
    context_back(1)
    attend_back_range(1, 0, HEADS)
    for copy in (og_sib, og_par, og_fwd):
        copy.wait_send()
    out_keep.wait()
    out_par.wait_send()
    project_back(1, 5)

    def first_layer_back(m):
        for i in (2 * m, 2 * m + 1):
            rows = chunk(i)
            X[rows] = Y[rows] + xget(5, i)
            norm_two_back(0, i)
        ffn_back(0, 6, m)

    loop(0, NW, first_layer_back)

    def both(ref, cols=slice(None)):
        value = ref[:, :, cols]
        return value.reshape(2 * value.shape[1], value.shape[2])

    FREE = T - 4 * A

    def grad_down(half, dst, off=0, ready=None):
        dy = both(dffn)
        for i in reversed(range(D // 256)):
            left = both(act, slice(half * D + i * 256, half * D + (i + 1) * 256))
            dst[off + DN + i * 256 : off + DN + (i + 1) * 256] = dot(left, dy, TN).astype(b16)
            if ready is not None:
                ready(CS * (D // 256 - i) * 256 // R)

    def grad_up(half, dst, off=0):
        dy = both(dpre, slice(half * D, (half + 1) * D))
        for i in reversed(range(D // 256)):
            left = both(yb, slice(i * 256, (i + 1) * 256))
            dst[off + UP + i * 256 : off + UP + (i + 1) * 256] = dot(left, dy, TN).astype(b16)

    def grad_attn(half, dst):
        rows = slice(half * A, (half + 1) * A)
        got = dot(ctx[0, rows], dattn[0], NN) + dot(ctx[1, rows], dattn[1], NN)
        dst[3 * A : 4 * A] = got.astype(b16)
        rows = slice(half * 3 * A, (half + 1) * 3 * A)
        got = dot(dqkv[0, rows], hb[0], NN) + dot(dqkv[1, rows], hb[1], NN)
        dst[0 : 3 * A] = got.astype(b16)

    FFN = CS * 2 * D // R

    def top_of(s):
        return TOT - (s // CS + 1) * R

    def cols_of(s):
        return pl.ds(pl.multiple_of((s % CS) * CW, 128), CW)

    def piece(s):
        return pl.ds(pl.multiple_of(top_of(s), R), R), cols_of(s)

    def half_of(s, which):
        return pl.ds(pl.multiple_of(top_of(s) + which * HR, HR), HR), cols_of(s)

    def part_of(s, which, p):
        return pl.ds(pl.multiple_of(top_of(s) + which * HR + p * Q, Q), Q), cols_of(s)

    def ycopy_ffn(s):
        src = zs.at[pl.ds(pl.multiple_of(top_of(s) + FREE, R), R), cols_of(s)]
        return remote(src, yr.at[piece(s)], ys.at[s], yrs.at[s], par)

    def ycopy_attn(s):
        return remote(gs.at[piece(s)], yr.at[piece(s)], ys.at[s], yrs.at[s], par)

    def ycopy(s):
        return remote(yr.at[piece(s)], yr.at[piece(s)], ys.at[s], yrs.at[s], par)

    def gxcopy(s):
        return remote(G.at[half_of(s, 1 - x)], xh.at[s], gxs.at[s], gxr.at[s], xp)

    def zcopy(s, k):
        src = G.at[part_of(s, x, (zlo + k) % NP)]
        return remote(src, zr.at[s, k - 1], zss.at[s, k - 1], zrs.at[s, k - 1], zdev(k))

    def hcopy(s, k):
        src = G.at[part_of(s, x, zlo)]
        return remote(src, hr.at[s % 2, k - 1], hss.at[s, k - 1], hrs.at[s, k - 1], hdev(k))

    def azcopy(s, k):
        rows = part_of(s, x, zlo)
        return remote(F.at[rows], F.at[rows], azs.at[s, k - 1], azr.at[s, k - 1], zdev(k))

    def axcopy(s, k):
        rows = part_of(s, x, (zlo + NP - k) % NP)
        return remote(F.at[rows], F.at[rows], axs.at[s, k], axr.at[s, k], xp)

    ocopies = [
        pltpu.make_async_copy(F.at[pl.ds(lo, rows)], ref, os.at[i])
        for i, (ref, lo, rows) in enumerate(
            (
                (gd_out, DN, D),
                (gu_out, UP, D),
                (go_out, 3 * A, A),
                (gv_out, 2 * A, A),
                (gk_out, A, A),
                (gq_out, 0, A),
            )
        )
    ]

    YLOOK = 3 * CS

    def ystart(s):
        if isinstance(s, int):
            if s < NS:
                (ycopy_ffn if s < FFN else ycopy_attn)(s).start()
            return

        @pl.when(s < FFN)
        def _():
            ycopy_ffn(s).start()

        @pl.when((s >= FFN) & (s < NS))
        def _():
            ycopy_attn(s).start()

    def stage_x(s):
        ycopy(s).wait_recv()
        ystart(s + YLOOK)
        for which in (1 - x, x):
            rows = half_of(s, which)
            G[rows] = (G[rows].astype(f32) + yr[rows].astype(f32)).astype(b16)
            if which is not x:
                gxcopy(s).start()

    def stage_z(s):
        gxcopy(s).wait_recv()
        rows = half_of(s, x)
        G[rows] = (G[rows].astype(f32) + xh[s].astype(f32)).astype(b16)
        for k in range(1, NP):
            zcopy(s, k).start()

    def stage_sum(s):
        rows = part_of(s, x, zlo)
        total = G[rows].astype(f32)
        for k in range(1, NP):
            zcopy(s, k).wait_recv()
            total += zr[s, k - 1].astype(f32)
        if NH > 1:
            G[rows] = total.astype(b16)
            for k in range(1, NH):
                hcopy(s, k).start()
            for k in range(1, NH):
                hcopy(s, k).wait()
                total += hr[s % 2, k - 1].astype(f32)
        F[rows] = total.astype(b16)
        for k in range(1, NP):
            azcopy(s, k).start()
        axcopy(s, 0).start()

    def stage_swap(s):
        for k in range(1, NP):
            azcopy(s, k).wait_recv()
            axcopy(s, k).start()

    def stage_out(s):
        for k in range(NP):
            axcopy(s, k).wait_recv()

    def drain(s):
        ycopy(s).wait_send()
        gxcopy(s).wait_send()
        for k in range(1, NP):
            zcopy(s, k).wait_send()
            azcopy(s, k).wait_send()
        for k in range(NP):
            axcopy(s, k).wait_send()

    stages = (stage_x, stage_z, stage_sum, stage_swap, stage_out, drain)

    LAGS = tuple(CS * i for i in range(5)) + (4 * CS + 1,)
    LAST = LAGS[-1]

    def run(i):
        for lag, stage in zip(LAGS, stages):
            s = i - lag
            if isinstance(s, int) and not 0 <= s < NS:
                continue
            stage(s)

    def run_some(n):
        for i in range(n * CS, (n + 1) * CS):
            run(i)

    begun = []

    def begin(ready):
        while len(begun) < min(ready, YLOOK):
            ystart(len(begun))
            begun.append(0)

    grad_down(1, zs, FREE, begin)
    grad_up(1, zs, FREE)
    grad_down(0, G)
    loop(0, NCH, lambda m: attn_out_back(0, 6, m))
    context_back(0)
    run_some(0)
    grad_up(0, G)
    attend_back_range(0, 0, HEADS // 2)
    run_some(1)
    attend_back_range(0, HEADS // 2, HEADS)
    run_some(2)
    project_back(0, 7)
    grad_attn(1, gs)
    run_some(3)
    acc[8:14] = acc[0:6]
    sm_y = remote(acc.at[pl.ds(8, 8)], smr.at[0], sms.at[0], smrs.at[0], par)
    sm_y.start()

    def last(m):
        rows = chunk(m)
        X[rows] = Y[rows] + xget(7, m)

    loop(0, NCH, last)
    xs[0, 0:B] = X[pl.ds(t * B, B)].astype(b16)
    xs[0, B : 2 * B] = X[pl.ds(t2 * B, B)].astype(b16)
    gi_keep = pltpu.make_async_copy(xs.at[0, pl.ds(0, B)], gib_out.at[y], lsem.at[2])
    gi_par = remote(xs.at[0, pl.ds(B, B)], gib_out.at[y], fs.at[8], fr.at[8], par)
    gi_keep.start()
    grad_attn(0, G)

    for i in range(4 * CS, LAST):
        run(i)
    loop(LAST, CS * D // R + LAGS[4], run)
    ocopies[0].start()
    loop(CS * D // R + LAGS[4], NS, run)
    gi_par.start()
    for i in range(NS, NS + LAGS[2]):
        run(i)
    sm_y.wait_recv()
    sm[0] = acc[0:8] + smr[0]
    sm_x = remote(sm.at[0], smr.at[1], sms.at[1], smrs.at[1], xp)
    sm_x.start()
    for i in range(NS + LAGS[2], NS + LAGS[3]):
        run(i)
    sm_x.wait_recv()
    sm[1] = sm[0] + smr[1]
    sm_z = [
        remote(sm.at[1], smr.at[1 + k], sms.at[1 + k], smrs.at[1 + k], zdev(k)) for k in range(1, NP)
    ]
    for copy in sm_z:
        copy.start()
    for i in range(NS + LAGS[3], NS + LAST):
        run(i)
    for copy in ocopies[1:]:
        copy.start()
    total = sm[1]
    for k, copy in enumerate(sm_z):
        copy.wait_recv()
        total += smr[2 + k]
    sm[2] = total
    if NH > 1:
        sm_h = [
            remote(sm.at[2], smr.at[NP + k], sms.at[NP + k], smrs.at[NP + k], hdev(k))
            for k in range(1, NH)
        ]
        for copy in sm_h:
            copy.start()
        for k, copy in enumerate(sm_h):
            copy.wait()
            total += smr[NP + 1 + k]
    sm_out[...] = total

    for copy in (hid_sib, hid_par, *bias_par, hid_fwd, gi_par, sm_y, sm_x):
        copy.wait_send()
    for copy in sm_z:
        copy.wait_send()
    out_par.wait_recv()
    gi_par.wait_recv()
    gi_keep.wait()
    for copy in ocopies:
        copy.wait()


def widen(*refs):
    names = 7
    big, result, small = refs[:names], refs[names], refs[names + 1]
    refs = refs[names + 2 :]
    wide, result_out, vectors = refs[:names], refs[names], refs[names + 1 : names + 10]
    refs = refs[names + 10 :]
    narrow, broad = refs[:names], refs[names : 2 * names]
    through, isem, osem = refs[2 * names :]
    loads = [pltpu.make_async_copy(big[i], narrow[i], isem.at[i]) for i in range(names)]
    stores = [pltpu.make_async_copy(broad[i], wide[i], osem.at[i]) for i in range(names)]
    keep_in = pltpu.make_async_copy(result, through, isem.at[names])
    keep = pltpu.make_async_copy(through, result_out, osem.at[names])
    for copy in loads:
        copy.start()
    keep_in.start()
    for i, ref in enumerate(vectors):
        if i < 7:
            ref[...] = small[i, :]
        else:
            rows = ref.shape[0]
            at = (i - 7) * 2 * rows
            ref[...] = small[7, at : at + rows]
    for load, store, i in zip(loads, stores, range(names)):
        load.wait()
        broad[i][...] = narrow[i][...].astype(f32)
        store.start()
    keep_in.wait()
    keep.start()
    for copy in stores:
        copy.wait()
    keep.wait()


def shards(
    dp,
    hidden_in,
    lengths,
    w_query,
    b_query,
    w_key,
    w_value,
    b_value,
    w_out,
    b_out,
    norm1_gain,
    norm1_shift,
    w_up,
    b_up,
    w_down,
    b_down,
    norm2_gain,
    norm2_shift,
    out_grad,
):
    _, B, D = hidden_in.shape
    A = w_query.shape[1]
    T = 4 * B
    TOT = 4 * A + 2 * D
    R = 128
    HR = R // 2
    nz = dp // 2
    NP = 1
    while nz % (2 * NP) == 0 and HR % (32 * NP) == 0:
        NP *= 2
    NH = nz // NP
    C = T // 4
    NCH = T // C
    CS = 1
    CW = D // CS
    NS = CS * TOT // R
    Q = HR // NP
    heads = 2 * A // HEAD
    cfg = dict(T=T, D=D, A=A, B=B, C=C, R=R, NP=NP, NH=NH, CS=CS)
    rows = [
        value if value.shape[0] == D else value.reshape(1, -1)
        for value in (
            b_up,
            b_query,
            b_value,
            b_out,
            norm1_gain,
            norm1_shift,
            b_down,
            norm2_gain,
            norm2_shift,
        )
    ]
    V = functools.partial(pltpu.VMEM)
    DMA = pltpu.SemaphoreType.DMA
    NPx = max(NP - 1, 1)
    NHx = max(NH - 1, 1)
    scratch = [
        V((2, TOT, D), b16),
        V((2, T, D), b16),
        V((2, 6 * A, T), b16),
        V((2, heads, T, T), b16),
        V((2, heads, 1, T), f32),
        V((2, 2 * A, T), b16),
        V((max(4 * T, T + 2 * D), D), b16),
        V((T, 128), f32),
        V((2, T, D), b16),
        V((2, T, 2 * D), b16),
        V((2, T, 2 * D), b16),
        V((T, D), f32),
        V((T, D), f32),
        V((2, T, D), b16),
        V((2, T, 2 * D), b16),
        V((2, T, D), b16),
        V((2, 6 * A, T), b16),
        V((2 * A, T), b16),
        V((2, T, D), b16),
        V((2, T, D), b16),
        V((D,), f32),
        V((1, A), f32),
        V((1, A), f32),
        V((2, 2 * A, 128), f32),
        V((16, D), f32),
        V((3, 8, D), f32),
        V((NP + NH, 8, D), f32),
        V((TOT, D), b16),
        V((4 * A, D), b16),
        V((TOT, D), b16),
        V((NS, HR, CW), b16),
        V((NS, NPx, Q, CW), b16),
        V((2, NHx, Q, CW), b16),
        V((TOT, D), b16),
        DMA((9,)),
        DMA((12,)),
        DMA((12,)),
        DMA((TOT // A,)),
        DMA((TOT // A,)),
        DMA((TOT // A,)),
        DMA((TOT // A,)),
        DMA((TOT // A,)),
        DMA((TOT // A,)),
        DMA((TOT // A,)),
        DMA((TOT // A,)),
        DMA((TOT // A,)),
        DMA((TOT // A,)),
        DMA((2, NCH)),
        DMA((2, NCH)),
        DMA((NS,)),
        DMA((NS,)),
        DMA((NS,)),
        DMA((NS,)),
        DMA((NS, NPx)),
        DMA((NS, NPx)),
        DMA((NS, NHx)),
        DMA((NS, NHx)),
        DMA((NS, NPx)),
        DMA((NS, NPx)),
        DMA((NS, NP)),
        DMA((NS, NP)),
        DMA((6,)),
        DMA((NP + NH,)),
        DMA((NP + NH,)),
    ]
    anywhere = pl.BlockSpec(memory_space=pl.ANY)
    vmem = pl.BlockSpec(memory_space=pltpu.VMEM)
    smem = pl.BlockSpec(memory_space=pltpu.SMEM)
    result, gib, gq, gk, gv, go, gu, gd, small = pl.pallas_call(
        functools.partial(whole_step, cfg),
        out_shape=(
            jax.ShapeDtypeStruct((2, B, D), f32),
            jax.ShapeDtypeStruct((2, B, D), b16),
            jax.ShapeDtypeStruct((A, D), b16),
            jax.ShapeDtypeStruct((A, D), b16),
            jax.ShapeDtypeStruct((A, D), b16),
            jax.ShapeDtypeStruct((A, D), b16),
            jax.ShapeDtypeStruct((D, D), b16),
            jax.ShapeDtypeStruct((D, D), b16),
            jax.ShapeDtypeStruct((8, D), f32),
        ),
        in_specs=[smem] + [anywhere] * 8 + [vmem] * 9,
        out_specs=(anywhere,) * 8 + (vmem,),
        scratch_shapes=scratch,
        compiler_params=pltpu.CompilerParams(
            collective_id=0, has_side_effects=True, vmem_limit_bytes=64 * 2**20
        ),
    )(
        lengths,
        hidden_in,
        out_grad,
        w_query.T,
        w_key.T,
        w_value.T,
        w_out,
        w_up,
        w_down,
        *rows,
    )
    bigs = (gd, gu, go, gq, gk, gv, gib)
    gd, gu, go, gq, gk, gv, gi, result, *vectors = pl.pallas_call(
        widen,
        out_shape=tuple(jax.ShapeDtypeStruct(v.shape, f32) for v in bigs + (result,))
        + (jax.ShapeDtypeStruct((D,), f32),) * 7
        + (jax.ShapeDtypeStruct((A,), f32),) * 2,
        in_specs=[anywhere] * 8 + [vmem],
        out_specs=(anywhere,) * 8 + (vmem,) * 9,
        scratch_shapes=[V(v.shape, b16) for v in bigs]
        + [V(v.shape, f32) for v in bigs]
        + [V(result.shape, f32), DMA((8,)), DMA((8,))],
        compiler_params=pltpu.CompilerParams(vmem_limit_bytes=64 * 2**20),
    )(*bigs, result, small)
    db_out, dgain1, dshift1, db_down, dgain2, dshift2, db_up, db_query, db_value = vectors
    return (
        result,
        gi,
        gq.T,
        db_query,
        gk.T,
        gv.T,
        db_value,
        go,
        db_out,
        dgain1,
        dshift1,
        gu,
        db_up,
        gd,
        db_down,
        dgain2,
        dshift2,
    )


def solution(mesh):
    placed = (
        P("dp", "tensor", None),
        P("dp"),
        P(None, "tensor"),
        P("tensor"),
        P(None, "tensor"),
        P(None, "tensor"),
        P("tensor"),
        P("tensor", None),
        P(),
        P(),
        P(),
        P(None, "tensor"),
        P("tensor"),
        P("tensor", None),
        P(),
        P(),
        P(),
        P("dp", "tensor", None),
    )
    return jax.shard_map(
        functools.partial(shards, mesh.shape["dp"]),
        mesh=mesh,
        in_specs=placed,
        out_specs=(
            P("dp", "tensor", None),
            P("dp", "tensor", None),
            P(None, "tensor"),
            P("tensor"),
            P(None, "tensor"),
            P(None, "tensor"),
            P("tensor"),
            P("tensor", None),
            P(),
            P(),
            P(),
            P(None, "tensor"),
            P("tensor"),
            P("tensor", None),
            P(),
            P(),
            P(),
        ),
        check_vma=False,
    )
```

```python
import functools

import jax
import jax.numpy as jnp
from jax import lax
from jax.experimental import pallas as pl
from jax.experimental.pallas import tpu as pltpu
from jax.sharding import PartitionSpec as P

HEAD = 64
NORM_EPS = 1e-12
NEG = -1000000000.0
GELU_C = 0.7978845608
GELU_A = 0.044715

NN = (((1,), (0,)), ((), ()))
NT = (((1,), (1,)), ((), ()))
TN = (((0,), (0,)), ((), ()))

b16 = jnp.bfloat16
f32 = jnp.float32


def dot(left, right, dims):
    return lax.dot_general(left, right, dims, preferred_element_type=f32)


def rms_back(dout, scaled, rstd, gain):
    dscaled = dout * gain
    return rstd * (
        dscaled
        - jnp.mean(dscaled, axis=-1, keepdims=True)
        - scaled * jnp.mean(dscaled * scaled, axis=-1, keepdims=True)
    )


def col_sum(value):
    return jnp.sum(value, axis=0, keepdims=True)


def whole_step(
    cfg,
    len_ref,
    hid,
    og,
    wq,
    wk,
    wv,
    wo,
    wu,
    wd,
    bu,
    bq,
    bv,
    b_out,
    gain1,
    shift1,
    b_down,
    gain2,
    shift2,
    out,
    gib_out,
    gq_out,
    gk_out,
    gv_out,
    go_out,
    gu_out,
    gd_out,
    sm_out,
    w,
    hb,
    qkv,
    ex,
    inv,
    ctx,
    zs,
    rs,
    yb,
    act,
    gp,
    X,
    Y,
    dffn,
    dpre,
    dattn,
    dqkv,
    dct,
    xs,
    xr,
    bur,
    bqr,
    bvr,
    bcol,
    acc,
    sm,
    smr,
    G,
    gs,
    yr,
    xh,
    zr,
    hr,
    F,
    lsem,
    fs,
    fr,
    wys,
    wyr,
    wxs,
    wxr,
    wzs,
    wzr,
    wfs,
    wfr,
    wds,
    wdr,
    es,
    er,
    ys,
    yrs,
    gxs,
    gxr,
    zss,
    zrs,
    hss,
    hrs,
    azs,
    azr,
    axs,
    axr,
    os,
    sms,
    smrs,
):
    T, D, A, B, C, R, NP, NH = (
        cfg["T"],
        cfg["D"],
        cfg["A"],
        cfg["B"],
        cfg["C"],
        cfg["R"],
        cfg["NP"],
        cfg["NH"],
    )
    NCH = T // C
    W = 2 * C
    NW = T // W
    TOT = 4 * A + 2 * D
    NS = TOT // R
    HR = R // 2
    Q = HR // NP
    NHH = A // HEAD
    HEADS = 2 * NHH
    MESH = pl.DeviceIdType.MESH
    UP, DN = 4 * A, 4 * A + D

    d = lax.axis_index("dp")
    t = lax.axis_index("tensor")
    y = t // 2
    c = t % 2
    x = d % 2
    z = d // 2
    zlo = z % NP
    zhi = z // NP
    t2 = (t + 2) % 4
    sib = (d, t + 1 - 2 * c)
    par = (d, t2)
    xp = (d + 1 - 2 * x, t)

    def zdev(k):
        return ((zhi * NP + (zlo + k) % NP) * 2 + x, t)

    def hdev(k):
        return ((((zhi + k) % NH) * NP + zlo) * 2 + x, t)

    def remote(src, dst, send, recv, dev):
        return pltpu.make_async_remote_copy(
            src_ref=src,
            dst_ref=dst,
            send_sem=send,
            recv_sem=recv,
            device_id=dev,
            device_id_type=MESH,
        )

    local = [
        pltpu.make_async_copy(hid.at[y], hb.at[0, pl.ds(t * B, B)], lsem.at[0]),
        pltpu.make_async_copy(wo, w.at[0, pl.ds(3 * A, A)], lsem.at[1]),
        pltpu.make_async_copy(wu, w.at[0, pl.ds(UP, D)], lsem.at[2]),
        pltpu.make_async_copy(wd, w.at[0, pl.ds(DN, D)], lsem.at[3]),
        pltpu.make_async_copy(og.at[0], Y.at[pl.ds(0, B)], lsem.at[4]),
        pltpu.make_async_copy(og.at[1], Y.at[pl.ds(B, B)], lsem.at[5]),
        pltpu.make_async_copy(wq, w.at[0, pl.ds(0, A)], lsem.at[6]),
        pltpu.make_async_copy(wk, w.at[0, pl.ds(A, A)], lsem.at[7]),
        pltpu.make_async_copy(wv, w.at[0, pl.ds(2 * A, A)], lsem.at[8]),
    ]
    for copy in local:
        copy.start()

    barrier = pltpu.get_barrier_semaphore()
    friends = [sib, par, xp] + [zdev(k) for k in range(1, NP)] + [hdev(k) for k in range(1, NH)]
    for dev in friends:
        pl.semaphore_signal(barrier, inc=1, device_id=dev, device_id_type=MESH)
    pl.semaphore_wait(barrier, len(friends))

    hid_sib = remote(hid.at[y], hb.at[0, pl.ds(t * B, B)], fs.at[0], fr.at[0], sib)
    hid_par = remote(hid.at[1 - y], hb.at[0, pl.ds(t * B, B)], fs.at[1], fr.at[1], par)
    bias_par = [
        remote(mine, theirs, fs.at[9 + i], fr.at[9 + i], par)
        for i, (mine, theirs) in enumerate(((bu, bur), (bq, bqr), (bv, bvr)))
    ]
    hid_sib.start()

    acc[...] = jnp.zeros_like(acc)

    WST = TOT // A
    WCH = A // 4
    zb = z % 2
    zp = ((z + 1 - 2 * zb) * 2 + x, t)

    def wrows(i, qx, qz):
        return pl.ds(pl.multiple_of(i * A + (2 * qx + qz) * WCH, WCH), WCH)

    def wy(i):
        rows = wrows(i, x, zb)
        return remote(w.at[0, rows], w.at[1, rows], wys.at[i], wyr.at[i], par)

    def wx(i):
        rows = wrows(i, x, zb)
        return remote(w.at[1, rows], w.at[1, rows], wxs.at[i], wxr.at[i], xp)

    def wz(i):
        rows = wrows(i, x, zb)
        return remote(w.at[1, rows], w.at[1, rows], wzs.at[i], wzr.at[i], zp)

    def wf(i):
        rows = wrows(i, 1 - x, zb) if i % 2 == 0 else wrows(i, x, 1 - zb)
        return remote(w.at[1, rows], w.at[1, rows], wfs.at[i], wfr.at[i], zp if i % 2 == 0 else xp)

    LATE = WST - D // A

    def wd(i):
        rows = wrows(i, 1 - x, 1 - zb)
        return remote(w.at[0, rows], w.at[1, rows], wds.at[i], wdr.at[i], par)

    LOOK = 4

    def send_quarters(i):
        if i < WST:
            wy(i).start()
            if i >= LATE:
                wd(i).start()

    def pump(i):
        wy(i).wait_recv()
        wx(i).start()
        wz(i).start()
        send_quarters(i + LOOK)

    def pass_on(i):
        (wx if i % 2 == 0 else wz)(i).wait_recv()
        wf(i).start()

    def have(lo, hi):
        for i in range(lo, hi):
            if i >= LATE:
                wx(i).wait_recv()
                wz(i).wait_recv()
                wd(i).wait_recv()
                continue
            (wz if i % 2 == 0 else wx)(i).wait_recv()
            wf(i).wait_recv()

    for copy in local[6:]:
        copy.wait()
    for i in range(3):
        wy(i).start()
    hid_par.start()
    for copy in bias_par:
        copy.start()
    for copy in local[:6]:
        copy.wait()
    wy(3).start()
    G[0 : 2 * B] = Y[0 : 2 * B].astype(b16)

    pump(0)
    pump(1)
    pass_on(0)
    pump(2)
    pass_on(1)
    hid_par.wait_recv()
    rows_t2 = pl.ds(t2 * B, B)
    hid_fwd = remote(hb.at[0, rows_t2], hb.at[0, rows_t2], fs.at[3], fr.at[3], sib)
    hid_fwd.start()
    for copy in bias_par:
        copy.wait_recv()
    for half, sources in enumerate(((bq, bv), (bqr, bvr))):
        for i, source in enumerate(sources):
            bcol[half, i * A : (i + 1) * A] = jnp.transpose(jnp.broadcast_to(source[...], (128, A)))
    hid_sib.wait_recv()
    hid_fwd.wait_recv()

    b_out, gain1, shift1, b_down, gain2, shift2 = (
        ref[...].reshape(1, D) for ref in (b_out, gain1, shift1, b_down, gain2, shift2)
    )
    length = len_ref[y]

    def loop(lo, hi, f):
        def step(i, carry):
            f(i)
            return carry

        lax.fori_loop(lo, hi, step, 0)

    def chunk(m):
        return pl.ds(pl.multiple_of(m * C, C), C)

    def wide_chunk(m):
        return pl.ds(pl.multiple_of(m * W, W), W)

    def xcopy(k, m):
        return remote(xs.at[k % 2, chunk(m)], xr.at[k % 2, chunk(m)], es.at[k % 2, m], er.at[k % 2, m], sib)

    def xsend(k, m, value):
        xs[k % 2, chunk(m)] = value.astype(b16)
        xcopy(k, m).start()

    def xget(k, m):
        xcopy(k, m).wait()
        return xs[k % 2, chunk(m)].astype(f32) + xr[k % 2, chunk(m)].astype(f32)

    def xsend_wide(k, m, value):
        xsend(k, 2 * m, value[0:C])
        xsend(k, 2 * m + 1, value[C:W])

    def project(l, m):
        tok = wide_chunk(m)
        for half in range(2):
            got = dot(w[half, 0 : 3 * A], hb[l, tok], NT)
            base = half * 3 * A
            bq = jnp.concatenate([bcol[half, 0:A]] * (W // 128), axis=1)
            bv = jnp.concatenate([bcol[half, A : 2 * A]] * (W // 128), axis=1)
            qkv[l, base : base + A, tok] = ((got[0:A] + bq).astype(b16) * b16(HEAD**-0.5)).astype(b16)
            qkv[l, base + A : base + 2 * A, tok] = got[A : 2 * A].astype(b16)
            qkv[l, base + 2 * A : base + 3 * A, tok] = (got[2 * A : 3 * A] + bv).astype(b16)

    def head_rows(h, part):
        base = (h // NHH) * (3 * A) + part * A + (h % NHH) * HEAD
        return pl.ds(base if isinstance(h, int) else pl.multiple_of(base, HEAD), HEAD)

    def ctx_rows(h):
        return pl.ds(h * HEAD if isinstance(h, int) else pl.multiple_of(h * HEAD, HEAD), HEAD)

    def attend(l, h):
        counted = lax.broadcasted_iota(jnp.int32, (T, T), 0) < length
        scores = dot(qkv[l, head_rows(h, 1)], qkv[l, head_rows(h, 0)], TN)
        scores = jnp.where(counted, scores, NEG)
        top = jnp.max(scores, axis=0, keepdims=True)
        e = jnp.exp(scores - top)
        one = 1.0 / jnp.sum(e, axis=0, keepdims=True)
        eb = e.astype(b16)
        ex[l, h] = eb
        inv[l, h] = one
        got = dot(qkv[l, head_rows(h, 2)], eb, NN) * one
        ctx[l, ctx_rows(h)] = got.astype(b16)

    def attend_range(l, lo, hi):
        if l == 0:
            loop(lo, hi, lambda h: attend(l, h))
        else:
            for h in range(lo, hi):
                attend(l, h)

    def attn_out(l, k):
        def step(m):
            tok = wide_chunk(m)
            part = dot(ctx[l, 0:A, tok], w[0, 3 * A : 4 * A], TN)
            part += dot(ctx[l, A : 2 * A, tok], w[1, 3 * A : 4 * A], TN)
            xsend_wide(k, m, part)

        loop(0, NW, step)

    def zrows(z_at, m):
        return pl.ds(pl.multiple_of(z_at * T + m * C, C), C)

    def norm(resid, gain, shift, z_at, m):
        rows = chunk(m)
        centre = resid - jnp.mean(resid, axis=-1, keepdims=True)
        rstd = lax.rsqrt(jnp.mean(centre * centre, axis=-1, keepdims=True) + NORM_EPS)
        scaled = centre * rstd
        zs[zrows(z_at, m)] = scaled.astype(b16)
        rs[rows, z_at : z_at + 1] = rstd
        return scaled * gain + shift

    def norm_one(l, k, m):
        rows = chunk(m)
        before = hb[0, rows].astype(f32) if l == 0 else X[rows]
        first = norm(xget(k, m) + b_out + before, gain1, shift1, 2 * l, m)
        Y[rows] = first
        yb[l, rows] = first.astype(b16)

    def up_chunk(l, m):
        rows = wide_chunk(m)
        for half, source in enumerate((bu, bur)):
            cols = pl.ds(half * D, D)
            pre = dot(yb[l, rows], w[half, UP : UP + D], NN) + source[...].reshape(1, D)
            square = pre * pre
            more = 0.5 + 0.5 * jnp.tanh(pre * (GELU_C + (GELU_C * GELU_A) * square))
            value = pre * more
            act[l, rows, cols] = value.astype(b16)
            slope = more + value * (1.0 - more) * (2.0 * GELU_C + (6.0 * GELU_C * GELU_A) * square)
            gp[l, rows, cols] = slope.astype(b16)

    def down_chunk(l, k, m):
        rows = wide_chunk(m)
        part = dot(act[l, rows, 0:D], w[0, DN : DN + D], NN)
        part += dot(act[l, rows, D : 2 * D], w[1, DN : DN + D], NN)
        xsend_wide(k, m, part)

    def norm_two(l, k, m):
        rows = chunk(m)
        result = norm(xget(k, m) + b_down + Y[rows], gain2, shift2, 2 * l + 1, m)
        X[rows] = result
        if l == 0:
            hb[1, rows] = result.astype(b16)

    pass_on(2)
    pump(3)
    have(0, 3)
    pump(4)
    pass_on(3)
    loop(0, NW, lambda m: project(0, m))
    done = 5
    for h in range(0, HEADS, 2):
        if done < LATE:
            pump(done)
            pass_on(done - 1)
            done += 1
        attend_range(0, h, min(h + 2, HEADS))
    while done < LATE:
        pump(done)
        pass_on(done - 1)
        done += 1
    have(3, 4)
    attn_out(0, 0)
    pass_on(LATE - 1)
    pump(LATE)
    loop(0, NCH, lambda m: norm_one(0, 0, m))
    pump(LATE + 1)
    have(4, LATE)
    for m in range(NW):
        up_chunk(0, m)
        pump(LATE + 2 + m)
    og_rows = pl.ds(t * B, B)
    og_mine, og_other = G.at[pl.ds(y * B, B)], G.at[pl.ds((1 - y) * B, B)]
    og_keep = pltpu.make_async_copy(og_mine, dattn.at[0, og_rows], lsem.at[0])
    og_sib = remote(og_mine, dattn.at[0, og_rows], fs.at[4], fr.at[4], sib)
    og_par = remote(og_other, dattn.at[0, og_rows], fs.at[5], fr.at[5], par)
    og_keep.start()
    og_par.start()
    og_sib.start()
    have(LATE, WST)
    loop(0, NW, lambda m: down_chunk(0, 1, m))

    def next_layer(m):
        norm_two(0, 1, 2 * m)
        norm_two(0, 1, 2 * m + 1)
        project(1, m)

    loop(0, NW, next_layer)

    attend_range(1, 0, HEADS)
    og_par.wait_recv()
    og_fwd = remote(dattn.at[0, rows_t2], dattn.at[0, rows_t2], fs.at[6], fr.at[6], sib)
    og_fwd.start()
    attn_out(1, 2)

    def feed_forward(m):
        norm_one(1, 2, 2 * m)
        norm_one(1, 2, 2 * m + 1)
        up_chunk(1, m)
        down_chunk(1, 3, m)

    loop(0, NW, feed_forward)
    loop(0, NCH, lambda m: norm_two(1, 3, m))
    out_keep = pltpu.make_async_copy(X.at[pl.ds(t * B, B)], out.at[y], lsem.at[1])
    out_par = remote(X.at[pl.ds(t2 * B, B)], out.at[y], fs.at[7], fr.at[7], par)
    out_keep.start()
    out_par.start()
    og_keep.wait()
    for i in range(WST):
        wy(i).wait_send()
        wx(i).wait_send()
        wz(i).wait_send()
        if i >= LATE:
            wd(i).wait_send()
        else:
            wf(i).wait_send()
    og_sib.wait_recv()
    og_fwd.wait_recv()

    def norm_two_back(l, m):
        rows = chunk(m)
        dout = dattn[0, rows].astype(f32) if l == 1 else X[rows]
        scaled = zs[zrows(2 * l + 1, m)].astype(f32)
        dr = rms_back(dout, scaled, rs[rows, 2 * l + 1 : 2 * l + 2], gain2)
        acc[3:4] += col_sum(dr)
        acc[4:5] += col_sum(dout * scaled)
        acc[5:6] += col_sum(dout)
        Y[rows] = dr
        dffn[l, rows] = dr.astype(b16)

    def ffn_back(l, k, m):
        rows = wide_chunk(m)
        drb = dffn[l, rows]
        part = None
        for half in range(2):
            cols = pl.ds(half * D, D)
            dact = dot(drb, w[half, DN : DN + D], NT)
            dp = (dact * gp[l, rows, cols].astype(f32)).astype(b16)
            dpre[l, rows, cols] = dp
            row = 6 + 8 * half
            acc[row : row + 1] += col_sum(dp.astype(f32))
            got = dot(dp, w[half, UP : UP + D], NT)
            part = got if part is None else part + got
        xsend_wide(k, m, part)

    def attn_out_back(l, k, m):
        rows = chunk(m)
        dfirst = Y[rows] + xget(k, m)
        scaled = zs[zrows(2 * l, m)].astype(f32)
        dr = rms_back(dfirst, scaled, rs[rows, 2 * l : 2 * l + 1], gain1)
        acc[0:1] += col_sum(dr)
        acc[1:2] += col_sum(dfirst * scaled)
        acc[2:3] += col_sum(dfirst)
        Y[rows] = dr
        drb = dr.astype(b16)
        dattn[l, rows] = drb

    def context_back(l):
        for half in range(2):
            got = dot(w[half, 3 * A : 4 * A], dattn[l], NT)
            for j in range(NHH):
                h = half * NHH + j
                scaled_rows = got[j * HEAD : (j + 1) * HEAD] * inv[l, h]
                dct[h * HEAD : (h + 1) * HEAD] = scaled_rows.astype(b16)

    def attend_back(l, h):
        mine = ctx_rows(h)
        dc = dct[mine]
        dprobs = dot(qkv[l, head_rows(h, 2)], dc, TN)
        eb = ex[l, h]
        ef = eb.astype(f32)
        inner = col_sum(ef * dprobs) * inv[l, h]
        ds = (ef * (dprobs - inner)).astype(b16)
        dqkv[l, head_rows(h, 2)] = dot(dc, eb, NT).astype(b16)
        dqkv[l, head_rows(h, 0)] = (dot(qkv[l, head_rows(h, 1)], ds, NN) * (HEAD**-0.5)).astype(b16)
        dqkv[l, head_rows(h, 1)] = dot(qkv[l, head_rows(h, 0)], ds, NT).astype(b16)

    def attend_back_range(l, lo, hi):
        if l == 0:
            loop(lo, hi, lambda h: attend_back(l, h))
        else:
            for h in range(lo, hi):
                attend_back(l, h)

    def project_back(l, k):
        def step(m):
            tok = wide_chunk(m)
            part = dot(dqkv[l, 0 : 3 * A, tok], w[0, 0 : 3 * A], TN)
            part += dot(dqkv[l, 3 * A : 6 * A, tok], w[1, 0 : 3 * A], TN)
            xsend_wide(k, m, part)

        loop(0, NW, step)
        ones = jnp.ones((8, T), b16)
        for half in range(2):
            sums = dot(ones, dqkv[l, half * 3 * A : (half + 1) * 3 * A], NT)
            row = 7 + 8 * half
            acc[row : row + 1, 0 : 3 * A] += sums[0:1]


    def second_layer_back(m):
        norm_two_back(1, 2 * m)
        norm_two_back(1, 2 * m + 1)
        ffn_back(1, 4, m)

    loop(0, NW, second_layer_back)
    loop(0, NCH, lambda m: attn_out_back(1, 4, m))
    context_back(1)
    attend_back_range(1, 0, HEADS)
    for copy in (og_sib, og_par, og_fwd):
        copy.wait_send()
    out_keep.wait()
    out_par.wait_send()
    project_back(1, 5)

    def first_layer_back(m):
        for i in (2 * m, 2 * m + 1):
            rows = chunk(i)
            X[rows] = Y[rows] + xget(5, i)
            norm_two_back(0, i)
        ffn_back(0, 6, m)

    loop(0, NW, first_layer_back)

    FREE = T - 4 * A

    GB = D // 256

    def grad_down(half, dst, off=0, lo=0, hi=GB):
        def step(j):
            at = pl.multiple_of((GB - 1 - j) * 256, 256)
            got = None
            for l in range(2):
                one = dot(act[l, :, pl.ds(half * D + at, 256)], dffn[l], TN)
                got = one if got is None else got + one
            dst[pl.ds(pl.multiple_of(off + DN + at, 256), 256)] = got.astype(b16)

        loop(lo, hi, step)

    def grad_up(half, dst, off=0):
        def step(j):
            at = pl.multiple_of((GB - 1 - j) * 256, 256)
            got = None
            for l in range(2):
                one = dot(yb[l, :, pl.ds(at, 256)], dpre[l, :, half * D : (half + 1) * D], TN)
                got = one if got is None else got + one
            dst[pl.ds(pl.multiple_of(off + UP + at, 256), 256)] = got.astype(b16)

        loop(0, GB, step)

    def grad_attn(half, dst):
        rows = slice(half * A, (half + 1) * A)
        got = dot(ctx[0, rows], dattn[0], NN) + dot(ctx[1, rows], dattn[1], NN)
        dst[3 * A : 4 * A] = got.astype(b16)

        def step(i):
            rows = pl.ds(pl.multiple_of(half * 3 * A + i * A, A), A)
            got = dot(dqkv[0, rows], hb[0], NN) + dot(dqkv[1, rows], hb[1], NN)
            dst[pl.ds(pl.multiple_of(i * A, A), A)] = got.astype(b16)

        loop(0, 3, step)

    def top_of(s):
        return pl.multiple_of(TOT - (s + 1) * R, R)

    def piece(s):
        return pl.ds(top_of(s), R)

    def half_of(s, which):
        return pl.ds(pl.multiple_of(top_of(s) + which * HR, HR), HR)

    def part_of(s, which, p):
        return pl.ds(pl.multiple_of(top_of(s) + which * HR + p * Q, Q), Q)

    def ycopy_ffn(s):
        src = zs.at[pl.ds(pl.multiple_of(top_of(s) + FREE, R), R)]
        return remote(src, yr.at[piece(s)], ys.at[s], yrs.at[s], par)

    def ycopy_attn(s):
        return remote(gs.at[piece(s)], yr.at[piece(s)], ys.at[s], yrs.at[s], par)

    def ycopy(s):
        return remote(yr.at[piece(s)], yr.at[piece(s)], ys.at[s], yrs.at[s], par)

    def gxcopy(s):
        return remote(G.at[half_of(s, 1 - x)], xh.at[s], gxs.at[s], gxr.at[s], xp)

    def zcopy(s, k):
        src = G.at[part_of(s, x, (zlo + k) % NP)]
        return remote(src, zr.at[s, k - 1], zss.at[s, k - 1], zrs.at[s, k - 1], zdev(k))

    def hcopy(s, k):
        src = G.at[part_of(s, x, zlo)]
        return remote(src, hr.at[s % 2, k - 1], hss.at[s, k - 1], hrs.at[s, k - 1], hdev(k))

    def azcopy(s, k):
        rows = part_of(s, x, zlo)
        return remote(F.at[rows], F.at[rows], azs.at[s, k - 1], azr.at[s, k - 1], zdev(k))

    def axcopy(s, k):
        rows = part_of(s, x, (zlo + NP - k) % NP)
        return remote(F.at[rows], F.at[rows], axs.at[s, k], axr.at[s, k], xp)

    ocopies = [
        pltpu.make_async_copy(F.at[pl.ds(lo, rows)], ref, os.at[i])
        for i, (ref, lo, rows) in enumerate(
            (
                (gd_out, DN, D),
                (gu_out, UP, D),
                (go_out, 3 * A, A),
                (gv_out, 2 * A, A),
                (gk_out, A, A),
                (gq_out, 0, A),
            )
        )
    ]

    YLOOK = 3

    def ystart(s):
        if isinstance(s, int):
            if s < NS:
                (ycopy_ffn if s < 2 * D // R else ycopy_attn)(s).start()
            return

        @pl.when(s < 2 * D // R)
        def _():
            ycopy_ffn(s).start()

        @pl.when((s >= 2 * D // R) & (s < NS))
        def _():
            ycopy_attn(s).start()

    def stage_x(s):
        ycopy(s).wait_recv()
        ystart(s + YLOOK)
        for which in (1 - x, x):
            rows = half_of(s, which)
            G[rows] = (G[rows].astype(f32) + yr[rows].astype(f32)).astype(b16)
            if which is not x:
                gxcopy(s).start()

    def stage_z(s):
        gxcopy(s).wait_recv()
        rows = half_of(s, x)
        G[rows] = (G[rows].astype(f32) + xh[s].astype(f32)).astype(b16)
        for k in range(1, NP):
            zcopy(s, k).start()

    def stage_sum(s):
        rows = part_of(s, x, zlo)
        total = G[rows].astype(f32)
        for k in range(1, NP):
            zcopy(s, k).wait_recv()
            total += zr[s, k - 1].astype(f32)
        if NH > 1:
            G[rows] = total.astype(b16)
            for k in range(1, NH):
                hcopy(s, k).start()
            for k in range(1, NH):
                hcopy(s, k).wait()
                total += hr[s % 2, k - 1].astype(f32)
        F[rows] = total.astype(b16)
        for k in range(1, NP):
            azcopy(s, k).start()
        axcopy(s, 0).start()

    def stage_swap(s):
        for k in range(1, NP):
            azcopy(s, k).wait_recv()
            axcopy(s, k).start()

    def stage_out(s):
        for k in range(NP):
            axcopy(s, k).wait_recv()

    def drain(s):
        ycopy(s).wait_send()
        gxcopy(s).wait_send()
        for k in range(1, NP):
            zcopy(s, k).wait_send()
            azcopy(s, k).wait_send()
        for k in range(NP):
            axcopy(s, k).wait_send()

    stages = (stage_x, stage_z, stage_sum, stage_swap, stage_out, drain)

    def run(i):
        for lag, stage in enumerate(stages):
            s = i - lag
            if isinstance(s, int) and not 0 <= s < NS:
                continue
            stage(s)

    first_ready = min(256 // R, YLOOK)
    grad_down(1, zs, FREE, 0, 1)
    for s in range(first_ready):
        ystart(s)
    grad_down(1, zs, FREE, 1, GB)
    for s in range(first_ready, YLOOK):
        ystart(s)
    grad_up(1, zs, FREE)
    grad_down(0, G)
    loop(0, NCH, lambda m: attn_out_back(0, 6, m))
    context_back(0)
    run(0)
    grad_up(0, G)
    attend_back_range(0, 0, HEADS // 2)
    run(1)
    attend_back_range(0, HEADS // 2, HEADS)
    run(2)
    project_back(0, 7)
    grad_attn(1, gs)
    run(3)
    acc[8:14] = acc[0:6]
    sm_y = remote(acc.at[pl.ds(8, 8)], smr.at[0], sms.at[0], smrs.at[0], par)
    sm_y.start()

    def last(m):
        rows = chunk(m)
        X[rows] = Y[rows] + xget(7, m)

    loop(0, NCH, last)
    xs[0, 0:B] = X[pl.ds(t * B, B)].astype(b16)
    xs[0, B : 2 * B] = X[pl.ds(t2 * B, B)].astype(b16)
    gi_keep = pltpu.make_async_copy(xs.at[0, pl.ds(0, B)], gib_out.at[y], lsem.at[2])
    gi_par = remote(xs.at[0, pl.ds(B, B)], gib_out.at[y], fs.at[8], fr.at[8], par)
    gi_keep.start()
    grad_attn(0, G)

    run(4)
    loop(5, D // R + 4, run)
    ocopies[0].start()
    loop(D // R + 4, NS, run)
    gi_par.start()
    for i in range(NS, NS + 2):
        run(i)
    sm_y.wait_recv()
    sm[0] = acc[0:8] + smr[0]
    sm_x = remote(sm.at[0], smr.at[1], sms.at[1], smrs.at[1], xp)
    sm_x.start()
    run(NS + 2)
    sm_x.wait_recv()
    sm[1] = sm[0] + smr[1]
    sm_z = [
        remote(sm.at[1], smr.at[1 + k], sms.at[1 + k], smrs.at[1 + k], zdev(k)) for k in range(1, NP)
    ]
    for copy in sm_z:
        copy.start()
    run(NS + 3)
    for copy in ocopies[1:]:
        copy.start()
    total = sm[1]
    for k, copy in enumerate(sm_z):
        copy.wait_recv()
        total += smr[2 + k]
    sm[2] = total
    if NH > 1:
        sm_h = [
            remote(sm.at[2], smr.at[NP + k], sms.at[NP + k], smrs.at[NP + k], hdev(k))
            for k in range(1, NH)
        ]
        for copy in sm_h:
            copy.start()
        for k, copy in enumerate(sm_h):
            copy.wait()
            total += smr[NP + 1 + k]
    sm_out[...] = total

    for copy in (hid_sib, hid_par, *bias_par, hid_fwd, gi_par, sm_y, sm_x):
        copy.wait_send()
    for copy in sm_z:
        copy.wait_send()
    out_par.wait_recv()
    gi_par.wait_recv()
    gi_keep.wait()
    drain(NS - 1)
    for copy in ocopies:
        copy.wait()


def widen(*refs):
    names = 7
    big, result, small = refs[:names], refs[names], refs[names + 1]
    refs = refs[names + 2 :]
    wide, result_out, vectors = refs[:names], refs[names], refs[names + 1 : names + 10]
    refs = refs[names + 10 :]
    narrow, broad = refs[:names], refs[names : 2 * names]
    through, isem, osem = refs[2 * names :]
    loads = [pltpu.make_async_copy(big[i], narrow[i], isem.at[i]) for i in range(names)]
    stores = [pltpu.make_async_copy(broad[i], wide[i], osem.at[i]) for i in range(names)]
    keep_in = pltpu.make_async_copy(result, through, isem.at[names])
    keep = pltpu.make_async_copy(through, result_out, osem.at[names])
    for copy in loads:
        copy.start()
    keep_in.start()
    for i, ref in enumerate(vectors):
        if i < 7:
            ref[...] = small[i, :]
        else:
            rows = ref.shape[0]
            at = (i - 7) * 2 * rows
            ref[...] = small[7, at : at + rows]
    for load, store, i in zip(loads, stores, range(names)):
        load.wait()
        broad[i][...] = narrow[i][...].astype(f32)
        store.start()
    keep_in.wait()
    keep.start()
    for copy in stores:
        copy.wait()
    keep.wait()


def shards(
    dp,
    hidden_in,
    lengths,
    w_query,
    b_query,
    w_key,
    w_value,
    b_value,
    w_out,
    b_out,
    norm1_gain,
    norm1_shift,
    w_up,
    b_up,
    w_down,
    b_down,
    norm2_gain,
    norm2_shift,
    out_grad,
):
    _, B, D = hidden_in.shape
    A = w_query.shape[1]
    T = 4 * B
    TOT = 4 * A + 2 * D
    R = 128
    HR = R // 2
    nz = dp // 2
    NP = 1
    while nz % (2 * NP) == 0 and HR % (32 * NP) == 0:
        NP *= 2
    NH = nz // NP
    C = T // 4
    NCH = T // C
    NS = TOT // R
    Q = HR // NP
    heads = 2 * A // HEAD
    cfg = dict(T=T, D=D, A=A, B=B, C=C, R=R, NP=NP, NH=NH)
    rows = [
        value if value.shape[0] == D else value.reshape(1, -1)
        for value in (
            b_up,
            b_query,
            b_value,
            b_out,
            norm1_gain,
            norm1_shift,
            b_down,
            norm2_gain,
            norm2_shift,
        )
    ]
    V = functools.partial(pltpu.VMEM)
    DMA = pltpu.SemaphoreType.DMA
    NPx = max(NP - 1, 1)
    NHx = max(NH - 1, 1)
    scratch = [
        V((2, TOT, D), b16),
        V((2, T, D), b16),
        V((2, 6 * A, T), b16),
        V((2, heads, T, T), b16),
        V((2, heads, 1, T), f32),
        V((2, 2 * A, T), b16),
        V((max(4 * T, T + 2 * D), D), b16),
        V((T, 128), f32),
        V((2, T, D), b16),
        V((2, T, 2 * D), b16),
        V((2, T, 2 * D), b16),
        V((T, D), f32),
        V((T, D), f32),
        V((2, T, D), b16),
        V((2, T, 2 * D), b16),
        V((2, T, D), b16),
        V((2, 6 * A, T), b16),
        V((2 * A, T), b16),
        V((2, T, D), b16),
        V((2, T, D), b16),
        V((D,), f32),
        V((1, A), f32),
        V((1, A), f32),
        V((2, 2 * A, 128), f32),
        V((16, D), f32),
        V((3, 8, D), f32),
        V((NP + NH, 8, D), f32),
        V((TOT, D), b16),
        V((4 * A, D), b16),
        V((TOT, D), b16),
        V((NS, HR, D), b16),
        V((NS, NPx, Q, D), b16),
        V((2, NHx, Q, D), b16),
        V((TOT, D), b16),
        DMA((9,)),
        DMA((12,)),
        DMA((12,)),
        DMA((TOT // A,)),
        DMA((TOT // A,)),
        DMA((TOT // A,)),
        DMA((TOT // A,)),
        DMA((TOT // A,)),
        DMA((TOT // A,)),
        DMA((TOT // A,)),
        DMA((TOT // A,)),
        DMA((TOT // A,)),
        DMA((TOT // A,)),
        DMA((2, NCH)),
        DMA((2, NCH)),
        DMA((NS,)),
        DMA((NS,)),
        DMA((NS,)),
        DMA((NS,)),
        DMA((NS, NPx)),
        DMA((NS, NPx)),
        DMA((NS, NHx)),
        DMA((NS, NHx)),
        DMA((NS, NPx)),
        DMA((NS, NPx)),
        DMA((NS, NP)),
        DMA((NS, NP)),
        DMA((6,)),
        DMA((NP + NH,)),
        DMA((NP + NH,)),
    ]
    anywhere = pl.BlockSpec(memory_space=pl.ANY)
    vmem = pl.BlockSpec(memory_space=pltpu.VMEM)
    smem = pl.BlockSpec(memory_space=pltpu.SMEM)
    result, gib, gq, gk, gv, go, gu, gd, small = pl.pallas_call(
        functools.partial(whole_step, cfg),
        out_shape=(
            jax.ShapeDtypeStruct((2, B, D), f32),
            jax.ShapeDtypeStruct((2, B, D), b16),
            jax.ShapeDtypeStruct((A, D), b16),
            jax.ShapeDtypeStruct((A, D), b16),
            jax.ShapeDtypeStruct((A, D), b16),
            jax.ShapeDtypeStruct((A, D), b16),
            jax.ShapeDtypeStruct((D, D), b16),
            jax.ShapeDtypeStruct((D, D), b16),
            jax.ShapeDtypeStruct((8, D), f32),
        ),
        in_specs=[smem] + [anywhere] * 8 + [vmem] * 9,
        out_specs=(anywhere,) * 8 + (vmem,),
        scratch_shapes=scratch,
        compiler_params=pltpu.CompilerParams(
            collective_id=0, has_side_effects=True, vmem_limit_bytes=64 * 2**20
        ),
    )(
        lengths,
        hidden_in,
        out_grad,
        w_query.T,
        w_key.T,
        w_value.T,
        w_out,
        w_up,
        w_down,
        *rows,
    )
    bigs = (gd, gu, go, gq, gk, gv, gib)
    gd, gu, go, gq, gk, gv, gi, result, *vectors = pl.pallas_call(
        widen,
        out_shape=tuple(jax.ShapeDtypeStruct(v.shape, f32) for v in bigs + (result,))
        + (jax.ShapeDtypeStruct((D,), f32),) * 7
        + (jax.ShapeDtypeStruct((A,), f32),) * 2,
        in_specs=[anywhere] * 8 + [vmem],
        out_specs=(anywhere,) * 8 + (vmem,) * 9,
        scratch_shapes=[V(v.shape, b16) for v in bigs]
        + [V(v.shape, f32) for v in bigs]
        + [V(result.shape, f32), DMA((8,)), DMA((8,))],
        compiler_params=pltpu.CompilerParams(vmem_limit_bytes=64 * 2**20),
    )(*bigs, result, small)
    db_out, dgain1, dshift1, db_down, dgain2, dshift2, db_up, db_query, db_value = vectors
    return (
        result,
        gi,
        gq.T,
        db_query,
        gk.T,
        gv.T,
        db_value,
        go,
        db_out,
        dgain1,
        dshift1,
        gu,
        db_up,
        gd,
        db_down,
        dgain2,
        dshift2,
    )


def solution(mesh):
    placed = (
        P("dp", "tensor", None),
        P("dp"),
        P(None, "tensor"),
        P("tensor"),
        P(None, "tensor"),
        P(None, "tensor"),
        P("tensor"),
        P("tensor", None),
        P(),
        P(),
        P(),
        P(None, "tensor"),
        P("tensor"),
        P("tensor", None),
        P(),
        P(),
        P(),
        P("dp", "tensor", None),
    )
    return jax.shard_map(
        functools.partial(shards, mesh.shape["dp"]),
        mesh=mesh,
        in_specs=placed,
        out_specs=(
            P("dp", "tensor", None),
            P("dp", "tensor", None),
            P(None, "tensor"),
            P("tensor"),
            P(None, "tensor"),
            P(None, "tensor"),
            P("tensor"),
            P("tensor", None),
            P(),
            P(),
            P(),
            P(None, "tensor"),
            P("tensor"),
            P("tensor", None),
            P(),
            P(),
            P(),
        ),
        check_vma=False,
    )
```

```python
import functools

import jax
import jax.numpy as jnp
from jax import lax
from jax.experimental import pallas as pl
from jax.experimental.pallas import tpu as pltpu
from jax.sharding import PartitionSpec as P

HEAD = 64
NORM_EPS = 1e-12
NEG = -1000000000.0
GELU_C = 0.7978845608
GELU_A = 0.044715

NN = (((1,), (0,)), ((), ()))
NT = (((1,), (1,)), ((), ()))
TN = (((0,), (0,)), ((), ()))

b16 = jnp.bfloat16
f32 = jnp.float32


def dot(left, right, dims):
    return lax.dot_general(left, right, dims, preferred_element_type=f32)


def rms_back(dout, scaled, rstd, gain):
    dscaled = dout * gain
    return rstd * (
        dscaled
        - jnp.mean(dscaled, axis=-1, keepdims=True)
        - scaled * jnp.mean(dscaled * scaled, axis=-1, keepdims=True)
    )


def col_sum(value):
    return jnp.sum(value, axis=0, keepdims=True)


def whole_step(
    cfg,
    len_ref,
    hid,
    og,
    wq,
    wk,
    wv,
    wo,
    wu,
    wd,
    bu_in,
    bq_in,
    bv_in,
    b_out_in,
    gain1_in,
    shift1_in,
    b_down_in,
    gain2_in,
    shift2_in,
    out,
    gib_out,
    gq_out,
    gk_out,
    gv_out,
    go_out,
    gu_out,
    gd_out,
    sm_out,
    w,
    hb,
    qkv,
    ex,
    inv,
    ctx,
    zs,
    rs,
    yb,
    act,
    gp,
    X,
    Y,
    dffn,
    dpre,
    dattn,
    dqkv,
    dct,
    xs,
    xr,
    bur,
    bqr,
    bvr,
    bcol,
    acc,
    sm,
    smr,
    G,
    gs,
    yr,
    xh,
    zr,
    hr,
    F,
    bu,
    bq,
    bv,
    b_out,
    gain1,
    shift1,
    b_down,
    gain2,
    shift2,
    vsem,
    lsem,
    fs,
    fr,
    wys,
    wyr,
    wxs,
    wxr,
    wzs,
    wzr,
    wfs,
    wfr,
    wds,
    wdr,
    es,
    er,
    ys,
    yrs,
    gxs,
    gxr,
    zss,
    zrs,
    hss,
    hrs,
    azs,
    azr,
    axs,
    axr,
    os,
    sms,
    smrs,
):
    T, D, A, B, C, R, NP, NH = (
        cfg["T"],
        cfg["D"],
        cfg["A"],
        cfg["B"],
        cfg["C"],
        cfg["R"],
        cfg["NP"],
        cfg["NH"],
    )
    NCH = T // C
    W = 2 * C
    NW = T // W
    TOT = 4 * A + 2 * D
    NS = TOT // R
    HR = R // 2
    Q = HR // NP
    NHH = A // HEAD
    HEADS = 2 * NHH
    MESH = pl.DeviceIdType.MESH
    UP, DN = 4 * A, 4 * A + D

    d = lax.axis_index("dp")
    t = lax.axis_index("tensor")
    y = t // 2
    c = t % 2
    x = d % 2
    z = d // 2
    zlo = z % NP
    zhi = z // NP
    t2 = (t + 2) % 4
    sib = (d, t + 1 - 2 * c)
    par = (d, t2)
    xp = (d + 1 - 2 * x, t)

    def zdev(k):
        return ((zhi * NP + (zlo + k) % NP) * 2 + x, t)

    def hdev(k):
        return ((((zhi + k) % NH) * NP + zlo) * 2 + x, t)

    def remote(src, dst, send, recv, dev):
        return pltpu.make_async_remote_copy(
            src_ref=src,
            dst_ref=dst,
            send_sem=send,
            recv_sem=recv,
            device_id=dev,
            device_id_type=MESH,
        )

    vectors = [
        pltpu.make_async_copy(src, dst, vsem.at[i])
        for i, (src, dst) in enumerate(
            (
                (bu_in, bu),
                (bq_in, bq),
                (bv_in, bv),
                (b_out_in, b_out),
                (gain1_in, gain1),
                (shift1_in, shift1),
                (b_down_in, b_down),
                (gain2_in, gain2),
                (shift2_in, shift2),
            )
        )
    ]
    for copy in vectors:
        copy.start()
    local = [
        pltpu.make_async_copy(hid.at[y], hb.at[0, pl.ds(t * B, B)], lsem.at[0]),
        pltpu.make_async_copy(wo, w.at[0, pl.ds(3 * A, A)], lsem.at[1]),
        pltpu.make_async_copy(wu, w.at[0, pl.ds(UP, D)], lsem.at[2]),
        pltpu.make_async_copy(wd, w.at[0, pl.ds(DN, D)], lsem.at[3]),
        pltpu.make_async_copy(og.at[0], Y.at[pl.ds(0, B)], lsem.at[4]),
        pltpu.make_async_copy(og.at[1], Y.at[pl.ds(B, B)], lsem.at[5]),
        pltpu.make_async_copy(wq, w.at[0, pl.ds(0, A)], lsem.at[6]),
        pltpu.make_async_copy(wk, w.at[0, pl.ds(A, A)], lsem.at[7]),
        pltpu.make_async_copy(wv, w.at[0, pl.ds(2 * A, A)], lsem.at[8]),
    ]
    for copy in local:
        copy.start()

    barrier = pltpu.get_barrier_semaphore()
    friends = [sib, par, xp] + [zdev(k) for k in range(1, NP)] + [hdev(k) for k in range(1, NH)]
    for dev in friends:
        pl.semaphore_signal(barrier, inc=1, device_id=dev, device_id_type=MESH)
    pl.semaphore_wait(barrier, len(friends))

    hid_sib = remote(hid.at[y], hb.at[0, pl.ds(t * B, B)], fs.at[0], fr.at[0], sib)
    hid_par = remote(hid.at[1 - y], hb.at[0, pl.ds(t * B, B)], fs.at[1], fr.at[1], par)
    for copy in vectors:
        copy.wait()
    bias_par = [
        remote(mine, theirs, fs.at[9 + i], fr.at[9 + i], par)
        for i, (mine, theirs) in enumerate(((bu, bur), (bq, bqr), (bv, bvr)))
    ]
    hid_sib.start()

    acc[...] = jnp.zeros_like(acc)

    WST = TOT // A
    WCH = A // 4
    zb = z % 2
    zp = ((z + 1 - 2 * zb) * 2 + x, t)

    def wrows(i, qx, qz):
        return pl.ds(pl.multiple_of(i * A + (2 * qx + qz) * WCH, WCH), WCH)

    def wy(i):
        rows = wrows(i, x, zb)
        return remote(w.at[0, rows], w.at[1, rows], wys.at[i], wyr.at[i], par)

    def wx(i):
        rows = wrows(i, x, zb)
        return remote(w.at[1, rows], w.at[1, rows], wxs.at[i], wxr.at[i], xp)

    def wz(i):
        rows = wrows(i, x, zb)
        return remote(w.at[1, rows], w.at[1, rows], wzs.at[i], wzr.at[i], zp)

    def wf(i):
        rows = wrows(i, 1 - x, zb) if i % 2 == 0 else wrows(i, x, 1 - zb)
        return remote(w.at[1, rows], w.at[1, rows], wfs.at[i], wfr.at[i], zp if i % 2 == 0 else xp)

    LATE = WST - D // A

    def wd(i):
        rows = wrows(i, 1 - x, 1 - zb)
        return remote(w.at[0, rows], w.at[1, rows], wds.at[i], wdr.at[i], par)

    LOOK = 4

    def send_quarters(i):
        if i < WST:
            wy(i).start()
            if i >= LATE:
                wd(i).start()

    def pump(i):
        wy(i).wait_recv()
        wx(i).start()
        wz(i).start()
        send_quarters(i + LOOK)

    def pass_on(i):
        (wx if i % 2 == 0 else wz)(i).wait_recv()
        wf(i).start()

    def have(lo, hi):
        for i in range(lo, hi):
            if i >= LATE:
                wx(i).wait_recv()
                wz(i).wait_recv()
                wd(i).wait_recv()
                continue
            (wz if i % 2 == 0 else wx)(i).wait_recv()
            wf(i).wait_recv()

    for copy in local[6:]:
        copy.wait()
    for i in range(3):
        wy(i).start()
    hid_par.start()
    for copy in bias_par:
        copy.start()
    for copy in local[:6]:
        copy.wait()
    wy(3).start()
    G[0 : 2 * B] = Y[0 : 2 * B].astype(b16)

    pump(0)
    pump(1)
    pass_on(0)
    pump(2)
    pass_on(1)
    hid_par.wait_recv()
    rows_t2 = pl.ds(t2 * B, B)
    hid_fwd = remote(hb.at[0, rows_t2], hb.at[0, rows_t2], fs.at[3], fr.at[3], sib)
    hid_fwd.start()
    for copy in bias_par:
        copy.wait_recv()
    for half, sources in enumerate(((bq, bv), (bqr, bvr))):
        for i, source in enumerate(sources):
            bcol[half, i * A : (i + 1) * A] = jnp.transpose(jnp.broadcast_to(source[...], (128, A)))
    hid_sib.wait_recv()
    hid_fwd.wait_recv()

    b_out, gain1, shift1, b_down, gain2, shift2 = (
        ref[...].reshape(1, D) for ref in (b_out, gain1, shift1, b_down, gain2, shift2)
    )
    length = len_ref[y]

    def loop(lo, hi, f):
        def step(i, carry):
            f(i)
            return carry

        lax.fori_loop(lo, hi, step, 0)

    def chunk(m):
        return pl.ds(pl.multiple_of(m * C, C), C)

    def wide_chunk(m):
        return pl.ds(pl.multiple_of(m * W, W), W)

    def xcopy(k, m):
        return remote(xs.at[k % 2, chunk(m)], xr.at[k % 2, chunk(m)], es.at[k % 2, m], er.at[k % 2, m], sib)

    def xsend(k, m, value):
        xs[k % 2, chunk(m)] = value.astype(b16)
        xcopy(k, m).start()

    def xget(k, m):
        xcopy(k, m).wait()
        return xs[k % 2, chunk(m)].astype(f32) + xr[k % 2, chunk(m)].astype(f32)

    def xsend_wide(k, m, value):
        xsend(k, 2 * m, value[0:C])
        xsend(k, 2 * m + 1, value[C:W])

    def project(l, m):
        tok = wide_chunk(m)
        for half in range(2):
            got = dot(w[half, 0 : 3 * A], hb[l, tok], NT)
            base = half * 3 * A
            bq = jnp.concatenate([bcol[half, 0:A]] * (W // 128), axis=1)
            bv = jnp.concatenate([bcol[half, A : 2 * A]] * (W // 128), axis=1)
            qkv[l, base : base + A, tok] = ((got[0:A] + bq).astype(b16) * b16(HEAD**-0.5)).astype(b16)
            qkv[l, base + A : base + 2 * A, tok] = got[A : 2 * A].astype(b16)
            qkv[l, base + 2 * A : base + 3 * A, tok] = (got[2 * A : 3 * A] + bv).astype(b16)

    def head_rows(h, part):
        base = (h // NHH) * (3 * A) + part * A + (h % NHH) * HEAD
        return pl.ds(base if isinstance(h, int) else pl.multiple_of(base, HEAD), HEAD)

    def ctx_rows(h):
        return pl.ds(h * HEAD if isinstance(h, int) else pl.multiple_of(h * HEAD, HEAD), HEAD)

    def attend(l, h):
        counted = lax.broadcasted_iota(jnp.int32, (T, T), 0) < length
        scores = dot(qkv[l, head_rows(h, 1)], qkv[l, head_rows(h, 0)], TN)
        scores = jnp.where(counted, scores, NEG)
        top = jnp.max(scores, axis=0, keepdims=True)
        e = jnp.exp(scores - top)
        one = 1.0 / jnp.sum(e, axis=0, keepdims=True)
        eb = e.astype(b16)
        ex[l, h] = eb
        inv[l, h] = one
        got = dot(qkv[l, head_rows(h, 2)], eb, NN) * one
        ctx[l, ctx_rows(h)] = got.astype(b16)

    def attend_range(l, lo, hi):
        if l == 0:
            loop(lo, hi, lambda h: attend(l, h))
        else:
            for h in range(lo, hi):
                attend(l, h)

    def attn_out(l, k):
        def step(m):
            tok = wide_chunk(m)
            part = dot(ctx[l, 0:A, tok], w[0, 3 * A : 4 * A], TN)
            part += dot(ctx[l, A : 2 * A, tok], w[1, 3 * A : 4 * A], TN)
            xsend_wide(k, m, part)

        loop(0, NW, step)

    def zrows(z_at, m):
        return pl.ds(pl.multiple_of(z_at * T + m * C, C), C)

    def norm(resid, gain, shift, z_at, m):
        rows = chunk(m)
        centre = resid - jnp.mean(resid, axis=-1, keepdims=True)
        rstd = lax.rsqrt(jnp.mean(centre * centre, axis=-1, keepdims=True) + NORM_EPS)
        scaled = centre * rstd
        zs[zrows(z_at, m)] = scaled.astype(b16)
        rs[rows, z_at : z_at + 1] = rstd
        return scaled * gain + shift

    def norm_one(l, k, m):
        rows = chunk(m)
        before = hb[0, rows].astype(f32) if l == 0 else X[rows]
        first = norm(xget(k, m) + b_out + before, gain1, shift1, 2 * l, m)
        Y[rows] = first
        yb[l, rows] = first.astype(b16)

    def up_chunk(l, m):
        rows = wide_chunk(m)
        for half, source in enumerate((bu, bur)):
            cols = pl.ds(half * D, D)
            pre = dot(yb[l, rows], w[half, UP : UP + D], NN) + source[...].reshape(1, D)
            square = pre * pre
            more = 0.5 + 0.5 * jnp.tanh(pre * (GELU_C + (GELU_C * GELU_A) * square))
            value = pre * more
            act[l, rows, cols] = value.astype(b16)
            slope = more + value * (1.0 - more) * (2.0 * GELU_C + (6.0 * GELU_C * GELU_A) * square)
            gp[l, rows, cols] = slope.astype(b16)

    def down_chunk(l, k, m):
        rows = wide_chunk(m)
        part = dot(act[l, rows, 0:D], w[0, DN : DN + D], NN)
        part += dot(act[l, rows, D : 2 * D], w[1, DN : DN + D], NN)
        xsend_wide(k, m, part)

    def norm_two(l, k, m):
        rows = chunk(m)
        result = norm(xget(k, m) + b_down + Y[rows], gain2, shift2, 2 * l + 1, m)
        X[rows] = result
        if l == 0:
            hb[1, rows] = result.astype(b16)

    pass_on(2)
    pump(3)
    have(0, 3)
    pump(4)
    pass_on(3)
    loop(0, NW, lambda m: project(0, m))
    done = 5
    for h in range(0, HEADS, 2):
        if done < LATE:
            pump(done)
            pass_on(done - 1)
            done += 1
        attend_range(0, h, min(h + 2, HEADS))
    while done < LATE:
        pump(done)
        pass_on(done - 1)
        done += 1
    have(3, 4)
    attn_out(0, 0)
    pass_on(LATE - 1)
    pump(LATE)
    loop(0, NCH, lambda m: norm_one(0, 0, m))
    pump(LATE + 1)
    have(4, LATE)
    for m in range(NW):
        up_chunk(0, m)
        pump(LATE + 2 + m)
    og_rows = pl.ds(t * B, B)
    og_mine, og_other = G.at[pl.ds(y * B, B)], G.at[pl.ds((1 - y) * B, B)]
    og_keep = pltpu.make_async_copy(og_mine, dattn.at[0, og_rows], lsem.at[0])
    og_sib = remote(og_mine, dattn.at[0, og_rows], fs.at[4], fr.at[4], sib)
    og_par = remote(og_other, dattn.at[0, og_rows], fs.at[5], fr.at[5], par)
    og_keep.start()
    og_par.start()
    og_sib.start()
    have(LATE, WST)
    loop(0, NW, lambda m: down_chunk(0, 1, m))

    def next_layer(m):
        norm_two(0, 1, 2 * m)
        norm_two(0, 1, 2 * m + 1)
        project(1, m)

    loop(0, NW, next_layer)

    attend_range(1, 0, HEADS)
    og_par.wait_recv()
    og_fwd = remote(dattn.at[0, rows_t2], dattn.at[0, rows_t2], fs.at[6], fr.at[6], sib)
    og_fwd.start()
    attn_out(1, 2)

    def feed_forward(m):
        norm_one(1, 2, 2 * m)
        norm_one(1, 2, 2 * m + 1)
        up_chunk(1, m)
        down_chunk(1, 3, m)

    loop(0, NW, feed_forward)
    loop(0, NCH, lambda m: norm_two(1, 3, m))
    out_keep = pltpu.make_async_copy(X.at[pl.ds(t * B, B)], out.at[y], lsem.at[1])
    out_par = remote(X.at[pl.ds(t2 * B, B)], out.at[y], fs.at[7], fr.at[7], par)
    out_keep.start()
    out_par.start()
    og_keep.wait()
    for i in range(WST):
        wy(i).wait_send()
        wx(i).wait_send()
        wz(i).wait_send()
        if i >= LATE:
            wd(i).wait_send()
        else:
            wf(i).wait_send()
    og_sib.wait_recv()
    og_fwd.wait_recv()

    def norm_two_back(l, m):
        rows = chunk(m)
        dout = dattn[0, rows].astype(f32) if l == 1 else X[rows]
        scaled = zs[zrows(2 * l + 1, m)].astype(f32)
        dr = rms_back(dout, scaled, rs[rows, 2 * l + 1 : 2 * l + 2], gain2)
        acc[3:4] += col_sum(dr)
        acc[4:5] += col_sum(dout * scaled)
        acc[5:6] += col_sum(dout)
        Y[rows] = dr
        dffn[l, rows] = dr.astype(b16)

    def ffn_back(l, k, m):
        rows = wide_chunk(m)
        drb = dffn[l, rows]
        part = None
        for half in range(2):
            cols = pl.ds(half * D, D)
            dact = dot(drb, w[half, DN : DN + D], NT)
            dp = (dact * gp[l, rows, cols].astype(f32)).astype(b16)
            dpre[l, rows, cols] = dp
            row = 6 + 8 * half
            acc[row : row + 1] += col_sum(dp.astype(f32))
            got = dot(dp, w[half, UP : UP + D], NT)
            part = got if part is None else part + got
        xsend_wide(k, m, part)

    def attn_out_back(l, k, m):
        rows = chunk(m)
        dfirst = Y[rows] + xget(k, m)
        scaled = zs[zrows(2 * l, m)].astype(f32)
        dr = rms_back(dfirst, scaled, rs[rows, 2 * l : 2 * l + 1], gain1)
        acc[0:1] += col_sum(dr)
        acc[1:2] += col_sum(dfirst * scaled)
        acc[2:3] += col_sum(dfirst)
        Y[rows] = dr
        drb = dr.astype(b16)
        dattn[l, rows] = drb

    def context_back(l):
        for half in range(2):
            got = dot(w[half, 3 * A : 4 * A], dattn[l], NT)
            for j in range(NHH):
                h = half * NHH + j
                scaled_rows = got[j * HEAD : (j + 1) * HEAD] * inv[l, h]
                dct[h * HEAD : (h + 1) * HEAD] = scaled_rows.astype(b16)

    def attend_back(l, h):
        mine = ctx_rows(h)
        dc = dct[mine]
        dprobs = dot(qkv[l, head_rows(h, 2)], dc, TN)
        eb = ex[l, h]
        ef = eb.astype(f32)
        inner = col_sum(ef * dprobs) * inv[l, h]
        ds = (ef * (dprobs - inner)).astype(b16)
        dqkv[l, head_rows(h, 2)] = dot(dc, eb, NT).astype(b16)
        dqkv[l, head_rows(h, 0)] = (dot(qkv[l, head_rows(h, 1)], ds, NN) * (HEAD**-0.5)).astype(b16)
        dqkv[l, head_rows(h, 1)] = dot(qkv[l, head_rows(h, 0)], ds, NT).astype(b16)

    def attend_back_range(l, lo, hi):
        if l == 0:
            loop(lo, hi, lambda h: attend_back(l, h))
        else:
            for h in range(lo, hi):
                attend_back(l, h)

    def project_back(l, k):
        def step(m):
            tok = wide_chunk(m)
            part = dot(dqkv[l, 0 : 3 * A, tok], w[0, 0 : 3 * A], TN)
            part += dot(dqkv[l, 3 * A : 6 * A, tok], w[1, 0 : 3 * A], TN)
            xsend_wide(k, m, part)

        loop(0, NW, step)
        ones = jnp.ones((8, T), b16)
        for half in range(2):
            sums = dot(ones, dqkv[l, half * 3 * A : (half + 1) * 3 * A], NT)
            row = 7 + 8 * half
            acc[row : row + 1, 0 : 3 * A] += sums[0:1]


    def second_layer_back(m):
        norm_two_back(1, 2 * m)
        norm_two_back(1, 2 * m + 1)
        ffn_back(1, 4, m)

    loop(0, NW, second_layer_back)
    loop(0, NCH, lambda m: attn_out_back(1, 4, m))
    context_back(1)
    attend_back_range(1, 0, HEADS)
    for copy in (og_sib, og_par, og_fwd):
        copy.wait_send()
    out_keep.wait()
    out_par.wait_send()
    project_back(1, 5)

    def first_layer_back(m):
        for i in (2 * m, 2 * m + 1):
            rows = chunk(i)
            X[rows] = Y[rows] + xget(5, i)
            norm_two_back(0, i)
        ffn_back(0, 6, m)

    loop(0, NW, first_layer_back)

    FREE = T - 4 * A

    GB = D // 256

    def grad_down(half, dst, off=0, lo=0, hi=GB):
        def step(j):
            at = pl.multiple_of((GB - 1 - j) * 256, 256)
            got = None
            for l in range(2):
                one = dot(act[l, :, pl.ds(half * D + at, 256)], dffn[l], TN)
                got = one if got is None else got + one
            dst[pl.ds(pl.multiple_of(off + DN + at, 256), 256)] = got.astype(b16)

        loop(lo, hi, step)

    def grad_up(half, dst, off=0):
        def step(j):
            at = pl.multiple_of((GB - 1 - j) * 256, 256)
            got = None
            for l in range(2):
                one = dot(yb[l, :, pl.ds(at, 256)], dpre[l, :, half * D : (half + 1) * D], TN)
                got = one if got is None else got + one
            dst[pl.ds(pl.multiple_of(off + UP + at, 256), 256)] = got.astype(b16)

        loop(0, GB, step)

    def grad_attn(half, dst):
        rows = slice(half * A, (half + 1) * A)
        got = dot(ctx[0, rows], dattn[0], NN) + dot(ctx[1, rows], dattn[1], NN)
        dst[3 * A : 4 * A] = got.astype(b16)

        def step(i):
            rows = pl.ds(pl.multiple_of(half * 3 * A + i * A, A), A)
            got = dot(dqkv[0, rows], hb[0], NN) + dot(dqkv[1, rows], hb[1], NN)
            dst[pl.ds(pl.multiple_of(i * A, A), A)] = got.astype(b16)

        loop(0, 3, step)

    def top_of(s):
        return pl.multiple_of(TOT - (s + 1) * R, R)

    def piece(s):
        return pl.ds(top_of(s), R)

    def half_of(s, which):
        return pl.ds(pl.multiple_of(top_of(s) + which * HR, HR), HR)

    def part_of(s, which, p):
        return pl.ds(pl.multiple_of(top_of(s) + which * HR + p * Q, Q), Q)

    def ycopy_ffn(s):
        src = zs.at[pl.ds(pl.multiple_of(top_of(s) + FREE, R), R)]
        return remote(src, yr.at[piece(s)], ys.at[s], yrs.at[s], par)

    def ycopy_attn(s):
        return remote(gs.at[piece(s)], yr.at[piece(s)], ys.at[s], yrs.at[s], par)

    def ycopy(s):
        return remote(yr.at[piece(s)], yr.at[piece(s)], ys.at[s], yrs.at[s], par)

    def gxcopy(s):
        return remote(G.at[half_of(s, 1 - x)], xh.at[s], gxs.at[s], gxr.at[s], xp)

    def zcopy(s, k):
        src = G.at[part_of(s, x, (zlo + k) % NP)]
        return remote(src, zr.at[s, k - 1], zss.at[s, k - 1], zrs.at[s, k - 1], zdev(k))

    def hcopy(s, k):
        src = G.at[part_of(s, x, zlo)]
        return remote(src, hr.at[s % 2, k - 1], hss.at[s, k - 1], hrs.at[s, k - 1], hdev(k))

    def azcopy(s, k):
        rows = part_of(s, x, zlo)
        return remote(F.at[rows], F.at[rows], azs.at[s, k - 1], azr.at[s, k - 1], zdev(k))

    def axcopy(s, k):
        rows = part_of(s, x, (zlo + NP - k) % NP)
        return remote(F.at[rows], F.at[rows], axs.at[s, k], axr.at[s, k], xp)

    ocopies = [
        pltpu.make_async_copy(F.at[pl.ds(lo, rows)], ref, os.at[i])
        for i, (ref, lo, rows) in enumerate(
            (
                (gd_out, DN, D),
                (gu_out, UP, D),
                (go_out, 3 * A, A),
                (gv_out, 2 * A, A),
                (gk_out, A, A),
                (gq_out, 0, A),
            )
        )
    ]

    YLOOK = 3

    def ystart(s):
        if isinstance(s, int):
            if s < NS:
                (ycopy_ffn if s < 2 * D // R else ycopy_attn)(s).start()
            return

        @pl.when(s < 2 * D // R)
        def _():
            ycopy_ffn(s).start()

        @pl.when((s >= 2 * D // R) & (s < NS))
        def _():
            ycopy_attn(s).start()

    def stage_x(s):
        ycopy(s).wait_recv()
        ystart(s + YLOOK)
        for which in (1 - x, x):
            rows = half_of(s, which)
            G[rows] = (G[rows].astype(f32) + yr[rows].astype(f32)).astype(b16)
            if which is not x:
                gxcopy(s).start()

    def stage_z(s):
        gxcopy(s).wait_recv()
        rows = half_of(s, x)
        G[rows] = (G[rows].astype(f32) + xh[s].astype(f32)).astype(b16)
        for k in range(1, NP):
            zcopy(s, k).start()

    def stage_sum(s):
        rows = part_of(s, x, zlo)
        total = G[rows].astype(f32)
        for k in range(1, NP):
            zcopy(s, k).wait_recv()
            total += zr[s, k - 1].astype(f32)
        if NH > 1:
            G[rows] = total.astype(b16)
            for k in range(1, NH):
                hcopy(s, k).start()
            for k in range(1, NH):
                hcopy(s, k).wait()
                total += hr[s % 2, k - 1].astype(f32)
        F[rows] = total.astype(b16)
        for k in range(1, NP):
            azcopy(s, k).start()
        axcopy(s, 0).start()

    def stage_swap(s):
        for k in range(1, NP):
            azcopy(s, k).wait_recv()
            axcopy(s, k).start()

    def stage_out(s):
        for k in range(NP):
            axcopy(s, k).wait_recv()

    def drain(s):
        ycopy(s).wait_send()
        gxcopy(s).wait_send()
        for k in range(1, NP):
            zcopy(s, k).wait_send()
            azcopy(s, k).wait_send()
        for k in range(NP):
            axcopy(s, k).wait_send()

    stages = (stage_x, stage_z, stage_sum, stage_swap, stage_out, drain)

    def run(i):
        for lag, stage in enumerate(stages):
            s = i - lag
            if isinstance(s, int) and not 0 <= s < NS:
                continue
            stage(s)

    first_ready = min(256 // R, YLOOK)
    grad_down(1, zs, FREE, 0, 1)
    for s in range(first_ready):
        ystart(s)
    grad_down(1, zs, FREE, 1, GB)
    for s in range(first_ready, YLOOK):
        ystart(s)
    grad_up(1, zs, FREE)
    grad_down(0, G)
    loop(0, NCH, lambda m: attn_out_back(0, 6, m))
    context_back(0)
    run(0)
    grad_up(0, G)
    attend_back_range(0, 0, HEADS // 2)
    run(1)
    attend_back_range(0, HEADS // 2, HEADS)
    run(2)
    project_back(0, 7)
    grad_attn(1, gs)
    run(3)
    acc[8:14] = acc[0:6]
    sm_y = remote(acc.at[pl.ds(8, 8)], smr.at[0], sms.at[0], smrs.at[0], par)
    sm_y.start()

    def last(m):
        rows = chunk(m)
        X[rows] = Y[rows] + xget(7, m)

    loop(0, NCH, last)
    xs[0, 0:B] = X[pl.ds(t * B, B)].astype(b16)
    xs[0, B : 2 * B] = X[pl.ds(t2 * B, B)].astype(b16)
    gi_keep = pltpu.make_async_copy(xs.at[0, pl.ds(0, B)], gib_out.at[y], lsem.at[2])
    gi_par = remote(xs.at[0, pl.ds(B, B)], gib_out.at[y], fs.at[8], fr.at[8], par)
    gi_keep.start()
    grad_attn(0, G)

    run(4)
    loop(5, D // R + 4, run)
    ocopies[0].start()
    loop(D // R + 4, NS, run)
    gi_par.start()
    for i in range(NS, NS + 2):
        run(i)
    sm_y.wait_recv()
    sm[0] = acc[0:8] + smr[0]
    sm_x = remote(sm.at[0], smr.at[1], sms.at[1], smrs.at[1], xp)
    sm_x.start()
    run(NS + 2)
    sm_x.wait_recv()
    sm[1] = sm[0] + smr[1]
    sm_z = [
        remote(sm.at[1], smr.at[1 + k], sms.at[1 + k], smrs.at[1 + k], zdev(k)) for k in range(1, NP)
    ]
    for copy in sm_z:
        copy.start()
    run(NS + 3)
    for copy in ocopies[1:]:
        copy.start()
    total = sm[1]
    for k, copy in enumerate(sm_z):
        copy.wait_recv()
        total += smr[2 + k]
    sm[2] = total
    if NH > 1:
        sm_h = [
            remote(sm.at[2], smr.at[NP + k], sms.at[NP + k], smrs.at[NP + k], hdev(k))
            for k in range(1, NH)
        ]
        for copy in sm_h:
            copy.start()
        for k, copy in enumerate(sm_h):
            copy.wait()
            total += smr[NP + 1 + k]
    sm_x.wait_send()
    sm[0] = total
    small_keep = pltpu.make_async_copy(sm.at[0], sm_out, vsem.at[0])
    small_keep.start()

    for copy in (hid_sib, hid_par, *bias_par, hid_fwd, gi_par, sm_y):
        copy.wait_send()
    for copy in sm_z:
        copy.wait_send()
    out_par.wait_recv()
    gi_par.wait_recv()
    gi_keep.wait()
    small_keep.wait()
    drain(NS - 1)
    for copy in ocopies:
        copy.wait()


def widen(*refs):
    names = 7
    big, result, small = refs[:names], refs[names], refs[names + 1]
    refs = refs[names + 2 :]
    wide, result_out, vectors = refs[:names], refs[names], refs[names + 1 : names + 10]
    refs = refs[names + 10 :]
    narrow, broad = refs[:names], refs[names : 2 * names]
    through, sums, *held, isem, osem = refs[2 * names :]
    get_sums = pltpu.make_async_copy(small, sums, isem.at[names + 1])
    get_sums.start()
    loads = [pltpu.make_async_copy(big[i], narrow[i], isem.at[i]) for i in range(names)]
    stores = [pltpu.make_async_copy(broad[i], wide[i], osem.at[i]) for i in range(names)]
    keep_in = pltpu.make_async_copy(result, through, isem.at[names])
    keep = pltpu.make_async_copy(through, result_out, osem.at[names])
    for copy in loads:
        copy.start()
    keep_in.start()
    get_sums.wait()
    small_out = []
    for i, (ref, dst) in enumerate(zip(held, vectors)):
        if i < 7:
            ref[...] = sums[i, :]
        else:
            rows = ref.shape[0]
            at = (i - 7) * 2 * rows
            ref[...] = sums[7, at : at + rows]
        small_out.append(pltpu.make_async_copy(ref, dst, osem.at[names + 1 + i]))
        small_out[-1].start()
    for load, store, i in zip(loads, stores, range(names)):
        load.wait()
        broad[i][...] = narrow[i][...].astype(f32)
        store.start()
    keep_in.wait()
    keep.start()
    for copy in stores + small_out:
        copy.wait()
    keep.wait()


def shards(
    dp,
    hidden_in,
    lengths,
    w_query,
    b_query,
    w_key,
    w_value,
    b_value,
    w_out,
    b_out,
    norm1_gain,
    norm1_shift,
    w_up,
    b_up,
    w_down,
    b_down,
    norm2_gain,
    norm2_shift,
    out_grad,
):
    _, B, D = hidden_in.shape
    A = w_query.shape[1]
    T = 4 * B
    TOT = 4 * A + 2 * D
    R = 128
    HR = R // 2
    nz = dp // 2
    NP = 1
    while nz % (2 * NP) == 0 and HR % (32 * NP) == 0:
        NP *= 2
    NH = nz // NP
    C = T // 4
    NCH = T // C
    NS = TOT // R
    Q = HR // NP
    heads = 2 * A // HEAD
    cfg = dict(T=T, D=D, A=A, B=B, C=C, R=R, NP=NP, NH=NH)
    rows = [
        value if value.shape[0] == D else value.reshape(1, -1)
        for value in (
            b_up,
            b_query,
            b_value,
            b_out,
            norm1_gain,
            norm1_shift,
            b_down,
            norm2_gain,
            norm2_shift,
        )
    ]
    V = functools.partial(pltpu.VMEM)
    DMA = pltpu.SemaphoreType.DMA
    NPx = max(NP - 1, 1)
    NHx = max(NH - 1, 1)
    scratch = [
        V((2, TOT, D), b16),
        V((2, T, D), b16),
        V((2, 6 * A, T), b16),
        V((2, heads, T, T), b16),
        V((2, heads, 1, T), f32),
        V((2, 2 * A, T), b16),
        V((max(4 * T, T + 2 * D), D), b16),
        V((T, 128), f32),
        V((2, T, D), b16),
        V((2, T, 2 * D), b16),
        V((2, T, 2 * D), b16),
        V((T, D), f32),
        V((T, D), f32),
        V((2, T, D), b16),
        V((2, T, 2 * D), b16),
        V((2, T, D), b16),
        V((2, 6 * A, T), b16),
        V((2 * A, T), b16),
        V((2, T, D), b16),
        V((2, T, D), b16),
        V((D,), f32),
        V((1, A), f32),
        V((1, A), f32),
        V((2, 2 * A, 128), f32),
        V((16, D), f32),
        V((3, 8, D), f32),
        V((NP + NH, 8, D), f32),
        V((TOT, D), b16),
        V((4 * A, D), b16),
        V((TOT, D), b16),
        V((NS, HR, D), b16),
        V((NS, NPx, Q, D), b16),
        V((2, NHx, Q, D), b16),
        V((TOT, D), b16),
        *[V(value.shape, f32) for value in rows],
        DMA((9,)),
        DMA((9,)),
        DMA((12,)),
        DMA((12,)),
        DMA((TOT // A,)),
        DMA((TOT // A,)),
        DMA((TOT // A,)),
        DMA((TOT // A,)),
        DMA((TOT // A,)),
        DMA((TOT // A,)),
        DMA((TOT // A,)),
        DMA((TOT // A,)),
        DMA((TOT // A,)),
        DMA((TOT // A,)),
        DMA((2, NCH)),
        DMA((2, NCH)),
        DMA((NS,)),
        DMA((NS,)),
        DMA((NS,)),
        DMA((NS,)),
        DMA((NS, NPx)),
        DMA((NS, NPx)),
        DMA((NS, NHx)),
        DMA((NS, NHx)),
        DMA((NS, NPx)),
        DMA((NS, NPx)),
        DMA((NS, NP)),
        DMA((NS, NP)),
        DMA((6,)),
        DMA((NP + NH,)),
        DMA((NP + NH,)),
    ]
    anywhere = pl.BlockSpec(memory_space=pl.ANY)
    smem = pl.BlockSpec(memory_space=pltpu.SMEM)
    result, gib, gq, gk, gv, go, gu, gd, small = pl.pallas_call(
        functools.partial(whole_step, cfg),
        out_shape=(
            jax.ShapeDtypeStruct((2, B, D), f32),
            jax.ShapeDtypeStruct((2, B, D), b16),
            jax.ShapeDtypeStruct((A, D), b16),
            jax.ShapeDtypeStruct((A, D), b16),
            jax.ShapeDtypeStruct((A, D), b16),
            jax.ShapeDtypeStruct((A, D), b16),
            jax.ShapeDtypeStruct((D, D), b16),
            jax.ShapeDtypeStruct((D, D), b16),
            jax.ShapeDtypeStruct((8, D), f32),
        ),
        in_specs=[smem] + [anywhere] * 17,
        out_specs=(anywhere,) * 9,
        scratch_shapes=scratch,
        compiler_params=pltpu.CompilerParams(
            collective_id=0, has_side_effects=True, vmem_limit_bytes=64 * 2**20
        ),
    )(
        lengths,
        hidden_in,
        out_grad,
        w_query.T,
        w_key.T,
        w_value.T,
        w_out,
        w_up,
        w_down,
        *rows,
    )
    bigs = (gd, gu, go, gq, gk, gv, gib)
    gd, gu, go, gq, gk, gv, gi, result, *vectors = pl.pallas_call(
        widen,
        out_shape=tuple(jax.ShapeDtypeStruct(v.shape, f32) for v in bigs + (result,))
        + (jax.ShapeDtypeStruct((D,), f32),) * 7
        + (jax.ShapeDtypeStruct((A,), f32),) * 2,
        in_specs=[anywhere] * 9,
        out_specs=(anywhere,) * 17,
        scratch_shapes=[V(v.shape, b16) for v in bigs]
        + [V(v.shape, f32) for v in bigs]
        + [V(result.shape, f32), V((8, D), f32)]
        + [V((D,), f32)] * 7
        + [V((A,), f32)] * 2
        + [DMA((9,)), DMA((17,))],
        compiler_params=pltpu.CompilerParams(vmem_limit_bytes=64 * 2**20),
    )(*bigs, result, small)
    db_out, dgain1, dshift1, db_down, dgain2, dshift2, db_up, db_query, db_value = vectors
    return (
        result,
        gi,
        gq.T,
        db_query,
        gk.T,
        gv.T,
        db_value,
        go,
        db_out,
        dgain1,
        dshift1,
        gu,
        db_up,
        gd,
        db_down,
        dgain2,
        dshift2,
    )


def solution(mesh):
    placed = (
        P("dp", "tensor", None),
        P("dp"),
        P(None, "tensor"),
        P("tensor"),
        P(None, "tensor"),
        P(None, "tensor"),
        P("tensor"),
        P("tensor", None),
        P(),
        P(),
        P(),
        P(None, "tensor"),
        P("tensor"),
        P("tensor", None),
        P(),
        P(),
        P(),
        P("dp", "tensor", None),
    )
    return jax.shard_map(
        functools.partial(shards, mesh.shape["dp"]),
        mesh=mesh,
        in_specs=placed,
        out_specs=(
            P("dp", "tensor", None),
            P("dp", "tensor", None),
            P(None, "tensor"),
            P("tensor"),
            P(None, "tensor"),
            P(None, "tensor"),
            P("tensor"),
            P("tensor", None),
            P(),
            P(),
            P(),
            P(None, "tensor"),
            P("tensor"),
            P("tensor", None),
            P(),
            P(),
            P(),
        ),
        check_vma=False,
    )
```
